128 devices in a mesh: pre: 8 (over x, core), row: 16 (over z, y).
Axes of the slice: x: 4, y: 4, z: 4, core: 2. Of those that a mesh axis runs over, the one named last changes fastest.
Arguments:
- queries: bfloat16 [1024, 12288], P(('pre', 'row')), may hold values from -9 to 9
- prompt_ids: int32 [1024, 1], P(('pre', 'row')), may hold values from 0 to 7; in each aligned block of 8 rows (0 to 7, 8 to 15, ...) at most 2 rows name the same one
- suffix_len: int32 [1024], P(('pre', 'row')), may hold values from 1 to 256, as said below
- page_table: int32 [1024, 16], P(('pre', 'row')), may hold values from 0 to 127, as said below
- suffix_pool: bfloat16 [16384, 16, 2048], P(('pre', 'row')), may hold values from -24 to 24
- prefix_kv: bfloat16 [8, 16384, 2048], P('pre', 'row'), may hold values from -18 to 18
Outputs:
- attention: bfloat16 [1024, 12288], P(('pre', 'row'))
The draws below stay inside these ranges and needn't reach their ends.
Inputs may be any that keep to these rules, and one draw needn't show every extreme that they name: `suffix_len`: each device's 8 rows include one of length 256. `page_table`: the rows of one device name each of that device's 128 pages exactly once. `prompt_ids`: in the rows of one device no prompt is named by more than 2 rows.
All inputs are finite; a program needn't handle non-finite values.
Results may differ from the reference program's by a relative error of at most 0.014.
Values may be sent and summed in bfloat16 or wider, within the bound.
No kernel may reach another device: no remote copies, remote signals or barrier semaphores. Data moves between devices by JAX's collectives and lax.ppermute only.
A program may use at most 512 MiB of HBM per device.

```python
import math
import jax
import jax.numpy as jnp
import numpy as np
from jax import lax

QH = 96
KVH = 8
HD = 128
ROW_DEV = 8
CAP = 2
PLEN_DEV = 1024
PAGE = 16
MAXP = 16
PROMPTS = 8
ROWS = 1024
PLEN = 16384
SUFMAX = 256
PAGES_DEV = 128
PAGES = 16384
N_PRE = 8
N_ROW = 16


def draw_queries(key, part):
    key = jax.random.fold_in(key, 11)
    values = jnp.clip(jax.random.normal(key, (ROWS, QH * HD), jnp.float32), -6.0, 6.0)
    return values.astype(jnp.bfloat16)


def draw_prefix_kv(key, part):
    key = jax.random.fold_in(key, 23)
    kv_width = KVH * HD
    full_shape = (PROMPTS, PLEN, kv_width)
    key_part = jnp.clip(2.7 * jax.random.normal(jax.random.fold_in(key, 1), full_shape, jnp.float32), -16.0, 16.0)
    values = jnp.clip(3.0 * jax.random.normal(jax.random.fold_in(key, 3), full_shape, jnp.float32), -18.0, 18.0)
    return jnp.concatenate((key_part, values), axis=2).astype(jnp.bfloat16)


def draw_suffix_pool(key, part):
    key = jax.random.fold_in(key, 31)
    kv_width = KVH * HD
    full_shape = (PAGES, PAGE, kv_width)
    key_part = jnp.clip(4.0 * jax.random.normal(jax.random.fold_in(key, 1), full_shape, jnp.float32), -24.0, 24.0)
    values = jnp.clip(3.0 * jax.random.normal(jax.random.fold_in(key, 2), full_shape, jnp.float32), -18.0, 18.0)
    return jnp.concatenate((key_part, values), axis=2).astype(jnp.bfloat16)


def draw_suffix_len(key, part):
    key = jax.random.fold_in(key, 37)
    blocks = ROWS // ROW_DEV
    lengths = jax.random.randint(jax.random.fold_in(key, 1), (blocks, ROW_DEV), 1, SUFMAX + 1)
    longest = jax.random.randint(jax.random.fold_in(key, 2), (blocks, 1), 0, ROW_DEV)
    lengths = jnp.where(jnp.arange(ROW_DEV)[None, :] == longest, SUFMAX, lengths)
    return lengths.reshape(ROWS).astype(jnp.int32)


def draw_page_table(key, part):
    key = jax.random.fold_in(key, 53)
    blocks = ROWS // ROW_DEV
    block_keys = jax.random.split(key, blocks)
    orders = jax.vmap(lambda single: jax.random.permutation(single, PAGES_DEV))(block_keys)
    return orders.reshape(ROWS, MAXP).astype(jnp.int32)


def shared_out(rng, own, number, rows, amount, top, most, slope):
    order = jax.random.permutation(rng, amount)
    crowded, ordinary = shares(amount, rows * top, most, slope, True), shares(amount, rows * top, most, slope, False)
    places = jnp.arange(amount)

    def named(sizes, offset_by):
        used = int((sizes > 0).sum())
        fixed = max(1, used // 4)
        moved = fixed + (places - fixed + offset_by * (used - fixed)) % max(1, amount - fixed)
        return jnp.zeros((amount,), jnp.int32).at[order[jnp.where(places < fixed, places, moved)]].set(jnp.asarray(sizes, jnp.int32))

    sizes = jnp.where(number % 4 == 0, named(crowded, number // 4), named(ordinary, number - number // 4 - 1))
    mixed = jax.random.permutation(jax.random.fold_in(own, 3), amount)
    giver, receiver = mixed[0:amount // 2 * 2:2], mixed[1:amount // 2 * 2:2]
    room = jnp.minimum(sizes[giver] - 1, most - sizes[receiver]) // 2
    room = jnp.where((giver == order[0]) | (receiver == order[0]) | (sizes[receiver] == 0), 0, jnp.maximum(room, 0))
    moved = jax.random.randint(jax.random.fold_in(own, 4), (amount // 2,), 0, 1 << 20) % (room + 1)
    sizes = sizes.at[giver].add(-moved).at[receiver].add(moved)
    labels = jnp.searchsorted(jnp.cumsum(sizes), jnp.arange(rows * top), side="right").astype(jnp.int32)
    table = labels.reshape(top, rows).T
    table = table[jax.random.permutation(jax.random.fold_in(own, 1), rows)]
    offset_by = jax.random.randint(jax.random.fold_in(own, 2), (rows, 1), 0, top)
    return jnp.take_along_axis(table, (jnp.arange(top)[None, :] + offset_by) % top, axis=1)


def shares(count, total, limit, skew, full):
    loads = [(1 << 20) // math.isqrt(rank ** skew) + 1 for rank in range(1, count + 1)]
    largest = limit if full else min(limit, max(-(-total // count), total * loads[0] // sum(loads)))
    least = 1 if total - largest >= count - 1 else 0
    holding, surplus = [largest] + [least] * (count - 1), total - largest - least * (count - 1)
    while surplus > 0:
        movable = [i for i in range(1, count) if holding[i] < largest] or [i for i in range(1, count) if holding[i] < limit]
        pool, budget = sum([loads[i] for i in movable]), surplus
        for i in movable:
            addition = min(limit - holding[i], max(1, budget * loads[i] // pool), surplus)
            holding[i] = holding[i] + addition
            surplus = surplus - addition
    return np.array(holding)


def setup_inputs(seed: int = 0) -> dict:
    streams_of = jax.random.split(jax.random.key(seed), 7)
    queries = draw_queries(jax.random.fold_in(streams_of[6], 71), 0)
    prompt_ids_keys = jax.random.split(jax.random.fold_in(streams_of[1], 1), ROWS // ROW_DEV)
    prompt_ids_turns = jax.random.permutation(jax.random.fold_in(streams_of[1], 3), ROWS // ROW_DEV)
    prompt_ids = jax.vmap(lambda own, number: shared_out(jax.random.fold_in(streams_of[1], 2), own, number, ROW_DEV, PROMPTS, 1, CAP, 2))(prompt_ids_keys, prompt_ids_turns).reshape((ROWS, 1))
    suffix_len = draw_suffix_len(jax.random.fold_in(streams_of[6], 71), 0)
    page_table = draw_page_table(jax.random.fold_in(streams_of[6], 71), 0)
    suffix_pool = draw_suffix_pool(jax.random.fold_in(streams_of[6], 71), 0)
    prefix_kv = draw_prefix_kv(jax.random.fold_in(streams_of[6], 71), 0)
    return {"queries": queries, "prompt_ids": prompt_ids, "suffix_len": suffix_len, "page_table": page_table, "suffix_pool": suffix_pool, "prefix_kv": prefix_kv}


def combine_parts(former, latter):
    highest = jnp.maximum(former[0], latter[0])
    left_scale = jnp.exp(former[0] - highest)
    right_scale = jnp.exp(latter[0] - highest)
    return (highest, former[1] * left_scale + latter[1] * right_scale, former[2] * left_scale[..., None] + latter[2] * right_scale[..., None])

def prefix_part(query_rows, block_rows):
    kv_width = KVH * HD
    key_rows = block_rows[:, :kv_width].astype(jnp.float32).reshape(-1, KVH, HD)
    value_rows = block_rows[:, kv_width:].astype(jnp.float32).reshape(-1, KVH, HD)
    scores = jnp.einsum('bkgd,tkd->bkgt', query_rows, key_rows) * (1.0 / math.sqrt(HD))
    maxima = lax.optimization_barrier(jnp.max(scores, axis=3))
    expo_terms = jnp.exp(scores - maxima[..., None])
    totals = lax.optimization_barrier(jnp.sum(expo_terms, axis=3))
    weights = lax.optimization_barrier(expo_terms.astype(jnp.bfloat16)).astype(jnp.float32)
    output = jnp.einsum('bkgt,tkd->bkgd', weights, value_rows)
    return (maxima, totals, output)

def suffix_part(query_rows, page_rows, lengths):
    kv_width = KVH * HD
    count = page_rows.shape[0]
    flattened = page_rows.reshape(count, SUFMAX, 2 * kv_width)
    key_rows = flattened[:, :, :kv_width].astype(jnp.float32).reshape(count, SUFMAX, KVH, HD)
    value_rows = flattened[:, :, kv_width:].astype(jnp.float32).reshape(count, SUFMAX, KVH, HD)
    scores = jnp.einsum('bkgd,btkd->bkgt', query_rows, key_rows) * (1.0 / math.sqrt(HD))
    in_range = (jnp.arange(SUFMAX, dtype=jnp.int32)[None, :] < lengths[:, None])[:, None, None, :]
    scores = jnp.where(in_range, scores, -1e+30)
    maxima = lax.optimization_barrier(jnp.max(scores, axis=3))
    expo_terms = jnp.where(in_range, jnp.exp(scores - maxima[..., None]), 0.0)
    totals = lax.optimization_barrier(jnp.sum(expo_terms, axis=3))
    weights = lax.optimization_barrier(expo_terms.astype(jnp.bfloat16)).astype(jnp.float32)
    output = jnp.einsum('bkgt,btkd->bkgd', weights, value_rows)
    return (maxima, totals, output)

def reference(queries, prompt_ids, suffix_len, page_table, suffix_pool, prefix_kv):
    group_size = QH // KVH
    bucket = CAP * N_PRE * N_ROW
    block_count = PLEN // PLEN_DEV
    prompt_of = prompt_ids[:, 0]
    query_all = queries.astype(jnp.float32).reshape(ROWS, KVH, group_size, HD)

    def per_prompt(prompt):
        chosen = jnp.nonzero(prompt_of == prompt, size=bucket, fill_value=ROWS)[0].astype(jnp.int32)
        query_rows = query_all[jnp.minimum(chosen, ROWS - 1)]
        sequence = lax.dynamic_index_in_dim(prefix_kv, prompt, 0, keepdims=False)
        sequence = sequence.reshape(block_count, PLEN_DEV, 2 * KVH * HD)

        def advance(carry, block_rows):
            return (combine_parts(carry, prefix_part(query_rows, block_rows)), None)
        opening = prefix_part(query_rows, sequence[0])
        result, unused = lax.scan(advance, opening, sequence[1:])
        return (chosen, result)
    chosen, parts = lax.map(per_prompt, jnp.arange(PROMPTS, dtype=jnp.int32))
    flat_rows = chosen.reshape(-1)
    pre_max = jnp.zeros((ROWS, KVH, group_size), jnp.float32).at[flat_rows].set(parts[0].reshape(-1, KVH, group_size), mode='drop')
    pre_total = jnp.zeros((ROWS, KVH, group_size), jnp.float32).at[flat_rows].set(parts[1].reshape(-1, KVH, group_size), mode='drop')
    pre_output = jnp.zeros((ROWS, KVH, group_size, HD), jnp.float32).at[flat_rows].set(parts[2].reshape(-1, KVH, group_size, HD), mode='drop')

    def per_device(device):
        row_start = device * ROW_DEV
        query_rows = lax.dynamic_slice_in_dim(query_all, row_start, ROW_DEV, 0)
        page_rows = lax.dynamic_slice_in_dim(page_table, row_start, ROW_DEV, 0)
        lengths = lax.dynamic_slice_in_dim(suffix_len, row_start, ROW_DEV, 0)
        pool_rows = lax.dynamic_slice_in_dim(suffix_pool, device * PAGES_DEV, PAGES_DEV, 0)
        return suffix_part(query_rows, pool_rows[page_rows], lengths)
    suffix_parts = lax.map(per_device, jnp.arange(ROWS // ROW_DEV, dtype=jnp.int32))
    suffix_parts = (suffix_parts[0].reshape(ROWS, KVH, group_size), suffix_parts[1].reshape(ROWS, KVH, group_size), suffix_parts[2].reshape(ROWS, KVH, group_size, HD))
    merged = combine_parts((pre_max, pre_total, pre_output), suffix_parts)
    result = merged[2] / merged[1][..., None]
    return result.reshape(ROWS, QH * HD).astype(jnp.bfloat16)
```

```python
import functools
import math

import jax
import jax.numpy as jnp
from jax import lax
from jax.experimental import pallas as pl
from jax.experimental.pallas import tpu as pltpu
from jax.sharding import PartitionSpec as P

KVH = 8
HD = 128
CAP = 2
GROUP = 12
ROWS = 8
WIDE = GROUP * HD
KVW = KVH * HD
NX, NC, NZ, NY = 4, 2, 4, 4
DEVS = NX * NC * NZ * NY
BLOCK = 1024
PAGE = 16
MAXP = 16
SPAN = PAGE * MAXP
SLOTS = 2 * CAP
ARR = DEVS * SLOTS
HALF = ARR // 2
TILE = 32
EMPTY = 256.0
SCALE = 1.0 / math.sqrt(HD)
AXES = ("pre", "row")
MB = 1 << 20
F32 = jnp.float32
BF16 = jnp.bfloat16


def dot(a, b):
    return jnp.dot(a, b, preferred_element_type=F32)


def dot_t(a, b):
    return lax.dot_general(a, b, (((1,), (1,)), ((), ())), preferred_element_type=F32)


def iota(shape, dim):
    return lax.broadcasted_iota(jnp.int32, shape, dim)


def device_number(x, c, z, y):
    return ((x * NC + c) * NZ + z) * NY + y


def routes(k, cross):
    pairs = []
    for x in range(NX):
        for c in range(NC):
            for z in range(NZ):
                for y in range(NY):
                    if (c ^ cross) == 0:
                        to = device_number(x, 0, (z + k) % NZ, y)
                    else:
                        to = device_number(x, 1, z, (y + k) % NY)
                    pairs.append((device_number(x, c, z, y), to))
    return pairs


def split_heads_kernel(head_ref, kv_ref, *refs):
    outs, sems = refs[:-1], refs[-1]
    copies = []
    for i, out in enumerate(outs):
        for part in range(2):
            start = pl.multiple_of(part * KVW + head_ref[i] * HD, HD)
            copies.append(
                pltpu.make_async_copy(
                    kv_ref.at[0, :, pl.ds(start, HD)], out.at[part], sems.at[i, part]
                )
            )
    for copy in copies:
        copy.start()
    for copy in copies:
        copy.wait()


def split_heads(heads, prefix_kv):
    n = heads.shape[0]
    return pl.pallas_call(
        split_heads_kernel,
        out_shape=[jax.ShapeDtypeStruct((2, BLOCK, HD), BF16)] * n,
        in_specs=[pl.BlockSpec(memory_space=pltpu.SMEM), pl.BlockSpec(memory_space=pl.ANY)],
        out_specs=[pl.BlockSpec(memory_space=pl.ANY)] * n,
        scratch_shapes=[pltpu.SemaphoreType.DMA((n, 2))],
        name="split_heads",
    )(heads, prefix_kv)


def send_kernel(col_ref, row_ref, q_ref, out_ref):
    wide = NY * ROWS
    mates = (col_ref[...] == row_ref[...]) & (
        iota((ROWS, wide), 0) < iota((ROWS, wide), 1) % ROWS
    )
    rank = jnp.sum(mates.astype(jnp.int32), axis=0, keepdims=True)
    slot = row_ref[...] * CAP + rank
    rows = NX * NY * SLOTS
    r = iota((rows, wide), 0)
    base = r // (NY * SLOTS) * SLOTS
    lane = iota((rows, wide), 1)
    first = (base + r % SLOTS == slot) & (lane < ROWS)
    second = (base + (r + CAP) % SLOTS == slot) & (r // SLOTS % NY == lane // ROWS)
    first = first.astype(F32)
    second = second.astype(F32)
    empty_first = (1.0 - jnp.sum(first, axis=1, keepdims=True)) * EMPTY
    empty_second = (1.0 - jnp.sum(second, axis=1, keepdims=True)) * EMPTY
    first = first[:, :ROWS].astype(BF16)
    second = second.astype(BF16)
    unit = NY * SLOTS
    for z in range(NZ):
        piece = dot(first, q_ref[:, z * WIDE : (z + 1) * WIDE]) + empty_first
        piece = piece.astype(BF16)
        for x in range(NX):
            at = device_number(x, 0, z, 0) * SLOTS
            out_ref[at : at + unit, :] = piece[x * unit : (x + 1) * unit]
    stacked = jnp.concatenate(
        [
            q_ref[:, (NZ + y) * WIDE : (NZ + y + 1) * WIDE].astype(F32)
            for y in range(NY)
        ],
        axis=0,
    ).astype(BF16)
    piece = (dot(second, stacked) + empty_second).astype(BF16)
    for x in range(NX):
        for z in range(NZ):
            at = device_number(x, 1, z, 0) * SLOTS
            out_ref[at : at + unit, :] = piece[x * unit : (x + 1) * unit]


def fill_sends(prompt_ids, queries):
    return pl.pallas_call(
        send_kernel,
        out_shape=jax.ShapeDtypeStruct((ARR, WIDE), BF16),
        compiler_params=pltpu.CompilerParams(vmem_limit_bytes=32 * MB),
        name="fill_sends",
    )(prompt_ids, jnp.tile(prompt_ids.reshape(1, ROWS), (1, NY)), queries)


def suffix_kernel(table_ref, len_ref, q_ref, pool_ref, out_ref, lse_ref, kv, sems):
    i = pl.program_id(0)

    def fetch(row, slot):
        for p in range(MAXP):
            pltpu.make_async_copy(
                pool_ref.at[table_ref[row, p]],
                kv.at[slot, pl.ds(p * PAGE, PAGE), :],
                sems.at[slot],
            ).start()

    @pl.when(i == 0)
    def _():
        fetch(0, 0)

    @pl.when(i + 1 < ROWS)
    def _():
        fetch(i + 1, (i + 1) % 2)

    slot = i % 2
    pltpu.make_async_copy(kv.at[slot], kv.at[slot], sems.at[slot]).wait()
    in_range = iota((16, SPAN), 1) < len_ref[i]
    for h in range(KVH):
        keys = kv[slot, :, h * HD : (h + 1) * HD]
        values = kv[slot, :, KVW + h * HD : KVW + (h + 1) * HD]
        scores = jnp.where(in_range, dot_t(q_ref[0, h], keys) * SCALE, -1e30)
        top = jnp.max(scores, axis=1, keepdims=True)
        weights = jnp.where(in_range, jnp.exp(scores - top), 0.0)
        total = jnp.sum(weights, axis=1, keepdims=True)
        out_ref[0, h] = dot(weights.astype(BF16), values) / total
        lse_ref[0, h] = jnp.broadcast_to(top + jnp.log(total), (16, HD))


def suffix(page_table, suffix_len, queries, suffix_pool):
    q = queries.reshape(ROWS, KVH, GROUP, HD)
    q = jnp.pad(q, ((0, 0), (0, 0), (0, 16 - GROUP), (0, 0)))
    spec = pl.BlockSpec((1, KVH, 16, HD), lambda i: (i, 0, 0, 0))
    smem = pl.BlockSpec(memory_space=pltpu.SMEM)
    shape = jax.ShapeDtypeStruct((ROWS, KVH, 16, HD), F32)
    out, lse = pl.pallas_call(
        suffix_kernel,
        grid=(ROWS,),
        out_shape=[shape, shape],
        in_specs=[smem, smem, spec, pl.BlockSpec(memory_space=pl.ANY)],
        out_specs=[spec, spec],
        scratch_shapes=[pltpu.VMEM((2, SPAN, 2 * KVW), BF16), pltpu.SemaphoreType.DMA((2,))],
        compiler_params=pltpu.CompilerParams(vmem_limit_bytes=32 * MB),
        cost_estimate=pl.CostEstimate(
            flops=4 * ROWS * KVH * 256 * SPAN * HD, bytes_accessed=9 * MB, transcendentals=0
        ),
        name="suffix",
    )(page_table, suffix_len, q, suffix_pool)
    return (
        out[:, :, :GROUP].reshape(ROWS, KVH * WIDE),
        lse[:, :, :GROUP].reshape(ROWS, KVH * WIDE),
    )


def prefix_kernel(x_ref, *refs):
    kv_refs = refs[:8]
    out_ref, qs, os, ls = refs[8:]
    log2e = 1.0 / math.log(2.0)
    pick = (iota((8, HD), 1) == 0).astype(BF16)
    mark_row = dot_t(pick, x_ref[:, :HD])
    held_row = mark_row < EMPTY / 2
    turn_row = iota((8, ARR), 1) % SLOTS // CAP
    before = (iota((ARR, ARR), 0) <= iota((ARR, ARR), 1)) & (
        iota((ARR, ARR), 0) % SLOTS // CAP == iota((ARR, ARR), 1) % SLOTS // CAP
    )
    place_row = dot(held_row.astype(BF16), before.astype(BF16)).astype(jnp.int32) - 1
    held_col = x_ref[:, :HD].astype(F32)[:, 0:1] < EMPTY / 2
    upto = (iota((ARR, ARR), 1) <= iota((ARR, ARR), 0)) & (
        iota((ARR, ARR), 0) % SLOTS // CAP == iota((ARR, ARR), 1) % SLOTS // CAP
    )
    held_wide = jnp.broadcast_to(held_col.astype(F32), (ARR, HD)).astype(BF16)
    place_col = dot(upto.astype(BF16), held_wide)[:, 0:1].astype(jnp.int32) - 1
    turn_col = iota((ARR, 1), 0) % SLOTS // CAP

    for turn in range(2):
        chosen_row = held_row & (turn_row == turn)
        gather = (
            (place_row[0:1] == iota((HALF, ARR), 0)) & chosen_row[0:1]
        ).astype(BF16)
        for g in range(GROUP):
            qs[turn, g] = dot(gather, x_ref[:, g * HD : (g + 1) * HD]).astype(BF16)
        os[turn] = jnp.zeros((GROUP, HALF, HD), BF16)
        ls[turn] = jnp.zeros((HALF, HD), BF16)
        count = jnp.sum(chosen_row[0:1].astype(jnp.int32))

        def tile(t, carry, turn=turn):
            at = pl.multiple_of(t * TILE, TILE)
            q = qs[turn, :, pl.ds(at, TILE), :].reshape(GROUP * TILE, HD)
            top = total = acc = None
            for k in range(4):
                kv = kv_refs[k * 2 + turn]
                s = dot_t(q, kv[0])
                high = jnp.max(s, axis=1, keepdims=True)
                if k > 0:
                    high = jnp.maximum(top, high)
                p = jnp.exp2(s * (SCALE * log2e) - high * (SCALE * log2e))
                part_total = jnp.sum(p, axis=1, keepdims=True)
                part = dot(p.astype(BF16), kv[1])
                if k > 0:
                    fade = jnp.exp2((top - high) * (SCALE * log2e))
                    total = total * fade + part_total
                    acc = acc * fade + part
                else:
                    total, acc = part_total, part
                top = high
            os[turn, :, pl.ds(at, TILE), :] = (
                (acc / total).astype(BF16).reshape(GROUP, TILE, HD)
            )
            lse = (top * SCALE + jnp.log(total)).reshape(GROUP, TILE, 1)
            lane = iota((TILE, HD), 1)
            wide = jnp.zeros((TILE, HD), F32)
            for g in range(GROUP):
                mine = (lane == g) | (lane == g + GROUP) | (lane == g + 2 * GROUP)
                wide = wide + jnp.where(mine, lse[g], 0.0)
            one = wide.astype(BF16).astype(F32)
            two = (wide - one).astype(BF16).astype(F32)
            three = wide - one - two
            split = jnp.where(lane < GROUP, one, jnp.where(lane < 2 * GROUP, two, three))
            ls[turn, pl.ds(at, TILE), :] = split.astype(BF16)
            return carry

        lax.fori_loop(0, (count + TILE - 1) // TILE, tile, 0)

    scatter = [
        ((place_col == iota((ARR, HALF), 1)) & held_col & (turn_col == turn)).astype(BF16)
        for turn in range(2)
    ]
    for g in range(GROUP):
        piece = dot(scatter[0], os[0, g]) + dot(scatter[1], os[1, g])
        out_ref[:, g * HD : (g + 1) * HD] = piece.astype(BF16)
    piece = dot(scatter[0], ls[0]) + dot(scatter[1], ls[1])
    out_ref[:, WIDE:] = piece.astype(BF16)


def prefix(arrived, kv):
    return pl.pallas_call(
        prefix_kernel,
        out_shape=jax.ShapeDtypeStruct((ARR, WIDE + HD), BF16),
        scratch_shapes=[
            pltpu.VMEM((2, GROUP, HALF, HD), BF16),
            pltpu.VMEM((2, GROUP, HALF, HD), BF16),
            pltpu.VMEM((2, HALF, HD), BF16),
        ],
        compiler_params=pltpu.CompilerParams(vmem_limit_bytes=56 * MB),
        cost_estimate=pl.CostEstimate(
            flops=20 * 10**9, bytes_accessed=8 * MB, transcendentals=0
        ),
        name="prefix",
    )(arrived, *kv)


def merge_kernel(at_ref, back_ref, so_ref, sl_ref, out_ref):
    sel = (at_ref[...] == iota((KVH * 4 * ROWS, ARR), 1)).astype(BF16)
    mine = dot(sel, back_ref[...])
    spread = (
        (iota((HD, WIDE), 0) % GROUP == iota((HD, WIDE), 1) // HD)
        & (iota((HD, WIDE), 0) < 3 * GROUP)
    ).astype(BF16)
    lse = dot(mine[:, WIDE:].astype(BF16), spread)
    for h in range(KVH):
        cut = slice(h * WIDE, (h + 1) * WIDE)
        rows = [slice((h * 4 + j) * ROWS, (h * 4 + j + 1) * ROWS) for j in range(4)]
        parts = [(lse[r], mine[r, :WIDE]) for r in rows]
        parts.append((sl_ref[:, cut], so_ref[:, cut]))
        top = functools.reduce(jnp.maximum, [p[0] for p in parts])
        weights = [jnp.exp(p[0] - top) for p in parts]
        total = functools.reduce(jnp.add, weights)
        acc = functools.reduce(jnp.add, [w * p[1] for w, p in zip(weights, parts)])
        out_ref[:, cut] = (acc / total).astype(BF16)


def merge(prompt_ids, back, so, sl):
    prompt = prompt_ids[:, 0]
    earlier = jnp.arange(ROWS)[None, :] < jnp.arange(ROWS)[:, None]
    rank = jnp.sum(((prompt[:, None] == prompt[None, :]) & earlier).astype(jnp.int32), axis=1)
    h = jnp.arange(KVH)[:, None, None]
    j = jnp.arange(4)[None, :, None]
    c = h // 4
    z = jnp.where(c == 0, h, j)
    y = jnp.where(c == 0, j, h - 4)
    place = (prompt % 2 != c).astype(jnp.int32) * CAP + rank
    at = device_number(prompt // 2, c, z, y) * SLOTS + place
    return pl.pallas_call(
        merge_kernel,
        out_shape=jax.ShapeDtypeStruct((ROWS, KVH * WIDE), BF16),
        compiler_params=pltpu.CompilerParams(vmem_limit_bytes=32 * MB),
        name="merge",
    )(at.reshape(-1, 1), back, so, sl)


def exchange(array):
    width = array.shape[1]
    moved = lax.all_to_all(
        array.reshape(DEVS, SLOTS, width), AXES, split_axis=0, concat_axis=0, tiled=True
    )
    return moved.reshape(ARR, width)


def body(queries, prompt_ids, suffix_len, page_table, suffix_pool, prefix_kv):
    c = lax.axis_index("pre") % NC
    z = lax.axis_index("row") // NY
    y = lax.axis_index("row") % NY
    heads = jnp.stack(
        [
            jnp.where(c ^ cross == 0, (z + k) % NZ, NZ + (y + k) % NY)
            for k in range(4)
            for cross in range(2)
        ]
    ).astype(jnp.int32)
    pieces = split_heads(heads, prefix_kv)
    kv = [
        piece if n == 0 else lax.ppermute(piece, AXES, routes(n // 2, n % 2))
        for n, piece in enumerate(pieces)
    ]
    arrived = exchange(fill_sends(prompt_ids, queries))
    so, sl = suffix(page_table, suffix_len, queries, suffix_pool)
    back = exchange(prefix(arrived, kv))
    return merge(prompt_ids, back, so, sl)


def solution(mesh):
    return jax.shard_map(
        body,
        mesh=mesh,
        in_specs=(
            P(("pre", "row"), None),
            P(("pre", "row"), None),
            P(("pre", "row")),
            P(("pre", "row"), None),
            P(("pre", "row"), None, None),
            P("pre", "row", None),
        ),
        out_specs=P(("pre", "row"), None),
        check_vma=False,
    )
```

```python
import functools
import math

import jax
import jax.numpy as jnp
from jax import lax
from jax.experimental import pallas as pl
from jax.experimental.pallas import tpu as pltpu
from jax.sharding import PartitionSpec as P

KVH = 8
HD = 128
CAP = 2
GROUP = 12
ROWS = 8
WIDE = GROUP * HD
KVW = KVH * HD
NX, NC, NZ, NY = 4, 2, 4, 4
DEVS = NX * NC * NZ * NY
BLOCK = 1024
PAGE = 16
MAXP = 16
SPAN = PAGE * MAXP
SLOTS = 2 * CAP
HALVES = 2
PER_HALF = GROUP // HALVES
PAIRS = PER_HALF // 2
PART = PER_HALF * HD
LINES = HALVES * SLOTS
ARR = DEVS * LINES
HALF = DEVS * CAP
TILE = 64
CHUNK = 512
STRIPS = 4
EMPTY = 256.0
SCALE = 1.0 / math.sqrt(HD)
FACTOR = SCALE / math.log(2.0)
LEAST = 1e-26
MOST = 1e30
AXES = ("pre", "row")
MB = 1 << 20
F32 = jnp.float32
BF16 = jnp.bfloat16


def dot(a, b):
    return jnp.dot(a, b, preferred_element_type=F32)


def dot_t(a, b):
    return lax.dot_general(a, b, (((1,), (1,)), ((), ())), preferred_element_type=F32)


def iota(shape, dim):
    return lax.broadcasted_iota(jnp.int32, shape, dim)


def device_number(x, c, z, y):
    return ((x * NC + c) * NZ + z) * NY + y


def routes(k, cross):
    pairs = []
    for x in range(NX):
        for c in range(NC):
            for z in range(NZ):
                for y in range(NY):
                    if (c ^ cross) == 0:
                        to = device_number(x, 0, (z + k) % NZ, y)
                    else:
                        to = device_number(x, 1, z, (y + k) % NY)
                    pairs.append((device_number(x, c, z, y), to))
    return pairs


def split_heads_kernel(head_ref, kv_ref, *refs):
    outs, (held, sems) = refs[:-2], refs[-2:]
    inward, outward = [], []
    for i, out in enumerate(outs):
        for part in range(2):
            start = pl.multiple_of(part * KVW + head_ref[i] * HD, HD)
            inward.append(
                pltpu.make_async_copy(
                    kv_ref.at[0, :, pl.ds(start, HD)], held.at[i, part], sems.at[0, i, part]
                )
            )
            outward.append(
                pltpu.make_async_copy(held.at[i, part], out.at[part], sems.at[1, i, part])
            )
    for copy in inward:
        copy.start()
    for copy, onward in zip(inward, outward):
        copy.wait()
        onward.start()
    for copy in outward:
        copy.wait()


def split_heads(heads, prefix_kv):
    n = heads.shape[0]
    return pl.pallas_call(
        split_heads_kernel,
        out_shape=[jax.ShapeDtypeStruct((2, BLOCK, HD), BF16)] * n,
        in_specs=[pl.BlockSpec(memory_space=pltpu.SMEM), pl.BlockSpec(memory_space=pl.ANY)],
        out_specs=[pl.BlockSpec(memory_space=pl.ANY)] * n,
        scratch_shapes=[
            pltpu.VMEM((n, 2, BLOCK, HD), BF16),
            pltpu.SemaphoreType.DMA((2, n, 2)),
        ],
        compiler_params=pltpu.CompilerParams(vmem_limit_bytes=16 * MB),
        name="split_heads",
    )(heads, prefix_kv)


def send_kernel(col_ref, row_ref, q_ref, out_ref):
    wide = HALVES * NY * ROWS
    mates = (col_ref[...] == row_ref[...]) & (
        iota((ROWS, wide), 0) < iota((ROWS, wide), 1) % ROWS
    )
    rank = jnp.sum(mates.astype(jnp.int32), axis=0, keepdims=True)
    slot = row_ref[...] * CAP + rank
    unit = NY * LINES
    rows = NX * unit
    r = iota((rows, wide), 0)
    lane = iota((rows, wide), 1)
    base = r // unit * SLOTS
    half_fits = r // SLOTS % HALVES == lane // ROWS % HALVES
    first = (base + r % SLOTS == slot) & half_fits & (lane < HALVES * ROWS)
    second = (
        (base + (r + CAP) % SLOTS == slot)
        & half_fits
        & (r // LINES % NY == lane // (HALVES * ROWS))
    )
    first = first.astype(F32)
    second = second.astype(F32)
    empty_first = (1.0 - jnp.sum(first, axis=1, keepdims=True)) * EMPTY
    empty_second = (1.0 - jnp.sum(second, axis=1, keepdims=True)) * EMPTY
    first = first[:, : HALVES * ROWS].astype(BF16)
    second = second.astype(BF16)

    def stacked(heads):
        return jnp.concatenate(
            [
                q_ref[:, h * WIDE + half * PART : h * WIDE + (half + 1) * PART].astype(F32)
                for h in heads
                for half in range(HALVES)
            ],
            axis=0,
        ).astype(BF16)

    for z in range(NZ):
        piece = (dot(first, stacked([z])) + empty_first).astype(BF16)
        for x in range(NX):
            at = device_number(x, 0, z, 0) * LINES
            out_ref[at : at + unit, :] = piece[x * unit : (x + 1) * unit]
    piece = dot(second, stacked([NZ + y for y in range(NY)])) + empty_second
    piece = piece.astype(BF16)
    for x in range(NX):
        for z in range(NZ):
            at = device_number(x, 1, z, 0) * LINES
            out_ref[at : at + unit, :] = piece[x * unit : (x + 1) * unit]


def fill_sends(prompt_ids, queries):
    return pl.pallas_call(
        send_kernel,
        out_shape=jax.ShapeDtypeStruct((ARR, PART), BF16),
        compiler_params=pltpu.CompilerParams(vmem_limit_bytes=32 * MB),
        name="fill_sends",
    )(prompt_ids, jnp.tile(prompt_ids.reshape(1, ROWS), (1, HALVES * NY)), queries)


def suffix_kernel(table_ref, len_ref, q_ref, pool_ref, out_ref, lse_ref, kv, sems):
    for row in range(ROWS):
        for p in range(MAXP):
            pltpu.make_async_copy(
                pool_ref.at[table_ref[row, p]],
                kv.at[row, pl.ds(p * PAGE, PAGE), :],
                sems.at[row],
            ).start()

    def one(row, carry):
        pltpu.make_async_copy(kv.at[row], kv.at[row], sems.at[row]).wait()
        scores = jnp.concatenate(
            [
                dot_t(q_ref[row, h], kv[row, :, h * HD : (h + 1) * HD])
                for h in range(KVH)
            ],
            axis=0,
        )
        in_range = iota((KVH * 16, SPAN), 1) < len_ref[row]
        scores = jnp.where(in_range, scores * SCALE, -1e30)
        top = jnp.max(scores, axis=1, keepdims=True)
        weights = jnp.where(in_range, jnp.exp(scores - top), 0.0)
        total = jnp.sum(weights, axis=1, keepdims=True)
        scale = 1.0 / total
        lse = top + jnp.log(total)
        weights = weights.astype(BF16)
        for h in range(KVH):
            cut = slice(h * 16, (h + 1) * 16)
            values = kv[row, :, KVW + h * HD : KVW + (h + 1) * HD]
            out_ref[row, h] = dot(weights[cut], values) * scale[cut]
            lse_ref[row, h] = jnp.broadcast_to(lse[cut], (16, HD))
        return carry

    lax.fori_loop(0, ROWS, one, 0)


def suffix(page_table, suffix_len, queries, suffix_pool):
    q = queries.reshape(ROWS, KVH, GROUP, HD)
    q = jnp.pad(q, ((0, 0), (0, 0), (0, 16 - GROUP), (0, 0)))
    smem = pl.BlockSpec(memory_space=pltpu.SMEM)
    vmem = pl.BlockSpec(memory_space=pltpu.VMEM)
    shape = jax.ShapeDtypeStruct((ROWS, KVH, 16, HD), F32)
    out, lse = pl.pallas_call(
        suffix_kernel,
        out_shape=[shape, shape],
        in_specs=[smem, smem, vmem, pl.BlockSpec(memory_space=pl.ANY)],
        out_specs=[vmem, vmem],
        scratch_shapes=[
            pltpu.VMEM((ROWS, SPAN, 2 * KVW), BF16),
            pltpu.SemaphoreType.DMA((ROWS,)),
        ],
        compiler_params=pltpu.CompilerParams(vmem_limit_bytes=48 * MB),
        cost_estimate=pl.CostEstimate(
            flops=10**9, bytes_accessed=9 * MB, transcendentals=0
        ),
        name="suffix",
    )(page_table, suffix_len, q, suffix_pool)
    return (
        out[:, :, :GROUP].reshape(ROWS, KVH * WIDE),
        lse[:, :, :GROUP].reshape(ROWS, KVH * WIDE),
    )


def line_turn(line):
    return line // CAP % 2


def line_half(line):
    return line // SLOTS % HALVES


def gather_kernel(x_ref, q_ref, place_ref):
    pick = (iota((8, HD), 1) == 0).astype(BF16)
    held = dot_t(pick, x_ref[:, :HD]) < EMPTY / 2
    a, b = iota((ARR, ARR), 0), iota((ARR, ARR), 1)
    before = (a <= b) & (((a ^ b) & (LINES - CAP)) == 0)
    place = dot(held.astype(BF16), before.astype(BF16)).astype(jnp.int32) - 1
    place = jnp.where(held, place, -1)
    place_ref[...] = place
    line = iota((1, ARR), 1)
    for turn in range(2):
        for half in range(HALVES):
            mine = (line_turn(line) == turn) & (line_half(line) == half)
            row = jnp.where(mine, place[0:1], -1)
            gather = (row == iota((HALF, ARR), 0)).astype(BF16)
            for p in range(PAIRS):
                two = dot(gather, x_ref[:, p * 2 * HD : (p + 1) * 2 * HD]).astype(BF16)
                q_ref[turn, half * PER_HALF + 2 * p] = two[:, :HD]
                q_ref[turn, half * PER_HALF + 2 * p + 1] = two[:, HD:]


def gather_rows(arrived):
    return pl.pallas_call(
        gather_kernel,
        out_shape=[
            jax.ShapeDtypeStruct((2, GROUP, HALF, HD), BF16),
            jax.ShapeDtypeStruct((8, ARR), jnp.int32),
        ],
        compiler_params=pltpu.CompilerParams(vmem_limit_bytes=24 * MB),
        name="gather_rows",
    )(arrived)


def prefix_kernel(q_ref, place_ref, *refs):
    kv_refs = refs[:8]
    out_ref, os, ls, ks, vs, sems = refs[8:]
    copies = []
    for n in range(8):
        rows = pl.ds(n // 2 * BLOCK, BLOCK)
        copies.append(
            pltpu.make_async_copy(kv_refs[n].at[0], ks.at[n % 2, rows], sems.at[n, 0])
        )
        copies.append(
            pltpu.make_async_copy(
                kv_refs[n].at[1], vs.at[n % 2, rows, pl.ds(0, HD)], sems.at[n, 1]
            )
        )
    for copy in copies:
        copy.start()
    vs[:, :, HD:] = jnp.ones((2, 4 * BLOCK, HD), BF16)
    for turn in range(2):
        os[turn] = jnp.zeros((GROUP // 2, HALF, 2 * HD), BF16)
        ls[turn] = jnp.zeros((HALF, HD), BF16)
    place = place_ref[...]
    line = iota((1, ARR), 1)
    counts = [
        jnp.max(jnp.where(line_turn(line) == turn, place[0:1], -1)) + 1 for turn in range(2)
    ]
    for copy in copies:
        copy.wait()
    high_rows = GROUP * TILE
    strip = high_rows // STRIPS

    def finish(turn, at, acc, shift):
        total = acc[:, HD : HD + 1]
        out = (acc[:, :HD] / total).astype(BF16).reshape(GROUP, TILE, HD)
        for g in range(GROUP):
            os[turn, g // 2, pl.ds(at, TILE), g % 2 * HD : (g % 2 + 1) * HD] = out[g]
        lse = (shift + jnp.log(total)).reshape(GROUP, TILE, 1)
        lane = iota((TILE, HD), 1)
        wide = jnp.zeros((TILE, HD), F32)
        for g in range(GROUP):
            mine = (lane == g) | (lane == g + GROUP) | (lane == g + 2 * GROUP)
            wide = wide + jnp.where(mine, lse[g], 0.0)
        one = wide.astype(BF16).astype(F32)
        two = (wide - one).astype(BF16).astype(F32)
        three = wide - one - two
        split = jnp.where(lane < GROUP, one, jnp.where(lane < 2 * GROUP, two, three))
        ls[turn, pl.ds(at, TILE), :] = split.astype(BF16)

    for turn in range(2):

        def tile(t, carry, turn=turn):
            at = pl.multiple_of(t * TILE, TILE)
            q = q_ref[turn, :, pl.ds(at, TILE), :].reshape(high_rows, HD)
            accs = []
            for i in range(STRIPS):
                part_q = q[i * strip : (i + 1) * strip]
                acc = None
                score = dot_t(part_q, ks[turn, :CHUNK, :])
                for j in range(4 * BLOCK // CHUNK):
                    after = None
                    if (j + 1) * CHUNK < 4 * BLOCK:
                        after = dot_t(part_q, ks[turn, (j + 1) * CHUNK : (j + 2) * CHUNK, :])
                    weights = jnp.exp2(score * FACTOR).astype(BF16)
                    part = dot(weights, vs[turn, j * CHUNK : (j + 1) * CHUNK, :])
                    acc = part if acc is None else acc + part
                    score = after
                accs.append(acc)
            acc = jnp.concatenate(accs, axis=0)
            finish(turn, at, acc, 0.0)
            total = acc[:, HD : HD + 1]
            plain = (jnp.min(total) > LEAST) & (jnp.max(total) < MOST)

            @pl.when(jnp.logical_not(plain))
            def _():
                top = acc = None
                for k in range(4):
                    rows = slice(k * BLOCK, (k + 1) * BLOCK)
                    score = dot_t(q, ks[turn, rows, :])
                    high = jnp.max(score, axis=1, keepdims=True)
                    if k > 0:
                        high = jnp.maximum(top, high)
                    weights = jnp.exp2(score * FACTOR - high * FACTOR).astype(BF16)
                    part = dot(weights, vs[turn, rows, :])
                    if k > 0:
                        part = acc * jnp.exp2((top - high) * FACTOR) + part
                    top, acc = high, part
                finish(turn, at, acc, top * SCALE)

            return carry

        lax.fori_loop(0, (counts[turn] + TILE - 1) // TILE, tile, 0)

    place_col = jnp.transpose(place.astype(F32))[:, 0:1].astype(jnp.int32)
    line = iota((ARR, 1), 0)
    scatter = jnp.concatenate(
        [
            (
                jnp.where((line_turn(line) == turn) & (line_half(line) == half), place_col, -1)
                == iota((ARR, HALF), 1)
            ).astype(BF16)
            for turn in range(2)
            for half in range(HALVES)
        ],
        axis=1,
    )
    for p in range(PAIRS):
        source = jnp.concatenate(
            [os[turn, half * PAIRS + p] for turn in range(2) for half in range(HALVES)], axis=0
        )
        out_ref[:, p * 2 * HD : (p + 1) * 2 * HD] = dot(scatter, source).astype(BF16)
    source = jnp.concatenate([ls[0], ls[0], ls[1], ls[1]], axis=0)
    out_ref[:, PART:] = dot(scatter, source).astype(BF16)


def prefix(arrived, kv):
    rows, place = gather_rows(arrived)
    return pl.pallas_call(
        prefix_kernel,
        out_shape=jax.ShapeDtypeStruct((ARR, PART + HD), BF16),
        in_specs=[pl.BlockSpec(memory_space=pltpu.VMEM)] * 2
        + [pl.BlockSpec(memory_space=pl.ANY)] * 8,
        scratch_shapes=[
            pltpu.VMEM((2, GROUP // 2, HALF, 2 * HD), BF16),
            pltpu.VMEM((2, HALF, HD), BF16),
            pltpu.VMEM((2, 4 * BLOCK, HD), BF16),
            pltpu.VMEM((2, 4 * BLOCK, 2 * HD), BF16),
            pltpu.SemaphoreType.DMA((8, 2)),
        ],
        compiler_params=pltpu.CompilerParams(vmem_limit_bytes=48 * MB),
        cost_estimate=pl.CostEstimate(
            flops=20 * 10**9, bytes_accessed=8 * MB, transcendentals=0
        ),
        name="prefix",
    )(rows, place, *kv)


def merge_kernel(at_ref, back_ref, so_ref, sl_ref, out_ref):
    picked = KVH * 4 * ROWS
    line = iota((picked, ARR), 1)
    first = dot((at_ref[...] == line).astype(BF16), back_ref[...])
    second = dot((at_ref[...] + SLOTS == line).astype(BF16), back_ref[:, :PART])
    spread = (
        (iota((HD, WIDE), 0) % GROUP == iota((HD, WIDE), 1) // HD)
        & (iota((HD, WIDE), 0) < 3 * GROUP)
    ).astype(BF16)
    lse = dot(first[:, PART:].astype(BF16), spread)
    for h in range(KVH):
        cut = slice(h * WIDE, (h + 1) * WIDE)
        rows = [slice((h * 4 + j) * ROWS, (h * 4 + j + 1) * ROWS) for j in range(4)]
        parts = [
            (lse[r], jnp.concatenate([first[r, :PART], second[r]], axis=1)) for r in rows
        ]
        parts.append((sl_ref[:, cut], so_ref[:, cut]))
        top = functools.reduce(jnp.maximum, [p[0] for p in parts])
        weights = [jnp.exp(p[0] - top) for p in parts]
        total = functools.reduce(jnp.add, weights)
        acc = functools.reduce(jnp.add, [w * p[1] for w, p in zip(weights, parts)])
        out_ref[:, cut] = (acc / total).astype(BF16)


def merge(prompt_ids, back, so, sl):
    prompt = prompt_ids[:, 0]
    earlier = jnp.arange(ROWS)[None, :] < jnp.arange(ROWS)[:, None]
    rank = jnp.sum(((prompt[:, None] == prompt[None, :]) & earlier).astype(jnp.int32), axis=1)
    h = jnp.arange(KVH)[:, None, None]
    j = jnp.arange(4)[None, :, None]
    c = h // 4
    z = jnp.where(c == 0, h, j)
    y = jnp.where(c == 0, j, h - 4)
    place = (prompt % 2 != c).astype(jnp.int32) * CAP + rank
    at = device_number(prompt // 2, c, z, y) * LINES + place
    return pl.pallas_call(
        merge_kernel,
        out_shape=jax.ShapeDtypeStruct((ROWS, KVH * WIDE), BF16),
        compiler_params=pltpu.CompilerParams(vmem_limit_bytes=32 * MB),
        name="merge",
    )(at.reshape(-1, 1), back, so, sl)


def exchange(array):
    width = array.shape[1]
    moved = lax.all_to_all(
        array.reshape(DEVS, LINES, width), AXES, split_axis=0, concat_axis=0, tiled=True
    )
    return moved.reshape(ARR, width)


def body(queries, prompt_ids, suffix_len, page_table, suffix_pool, prefix_kv):
    c = lax.axis_index("pre") % NC
    z = lax.axis_index("row") // NY
    y = lax.axis_index("row") % NY
    heads = jnp.stack(
        [
            jnp.where(c ^ cross == 0, (z + k) % NZ, NZ + (y + k) % NY)
            for k in range(4)
            for cross in range(2)
        ]
    ).astype(jnp.int32)
    pieces = split_heads(heads, prefix_kv)
    pieces, queries = lax.optimization_barrier((pieces, queries))

    def move(n, piece):
        return lax.ppermute(piece, AXES, routes(n // 2, n % 2))

    kv = list(pieces)
    for n in (2, 3, 6, 7, 4):
        kv[n] = move(n, pieces[n])
    arrived = exchange(fill_sends(prompt_ids, queries))
    kv[2], kv[3], late, last, queries = lax.optimization_barrier(
        (kv[2], kv[3], pieces[5], pieces[1], queries)
    )
    kv[5] = move(5, late)
    kv[1] = move(1, last)
    so, sl = suffix(page_table, suffix_len, queries, suffix_pool)
    arrived, so, sl = lax.optimization_barrier((arrived, so, sl))
    back = exchange(prefix(arrived, kv))
    return merge(prompt_ids, back, so, sl)


def solution(mesh):
    return jax.shard_map(
        body,
        mesh=mesh,
        in_specs=(
            P(("pre", "row"), None),
            P(("pre", "row"), None),
            P(("pre", "row")),
            P(("pre", "row"), None),
            P(("pre", "row"), None, None),
            P("pre", "row", None),
        ),
        out_specs=P(("pre", "row"), None),
        check_vma=False,
    )
```

```python
import functools
import math

import jax
import jax.numpy as jnp
from jax import lax
from jax.experimental import pallas as pl
from jax.experimental.pallas import tpu as pltpu
from jax.sharding import PartitionSpec as P

KVH = 8
HD = 128
CAP = 2
GROUP = 12
ROWS = 8
WIDE = GROUP * HD
KVW = KVH * HD
NX, NC, NZ, NY = 4, 2, 4, 4
DEVS = NX * NC * NZ * NY
BLOCK = 1024
PAGE = 16
MAXP = 16
SPAN = PAGE * MAXP
SLOTS = 2 * CAP
HALVES = 2
PER_HALF = GROUP // HALVES
PAIRS = PER_HALF // 2
PART = PER_HALF * HD
LINES = HALVES * SLOTS
ARR = DEVS * LINES
HALF = DEVS * CAP
TILE = 64
STRIPS = 4
EMPTY = 256.0
SCALE = 1.0 / math.sqrt(HD)
FACTOR = SCALE / math.log(2.0)
LEAST = 1e-26
MOST = 1e30
AXES = ("pre", "row")
MB = 1 << 20
F32 = jnp.float32
BF16 = jnp.bfloat16


def dot(a, b):
    return jnp.dot(a, b, preferred_element_type=F32)


def dot_t(a, b):
    return lax.dot_general(a, b, (((1,), (1,)), ((), ())), preferred_element_type=F32)


def iota(shape, dim):
    return lax.broadcasted_iota(jnp.int32, shape, dim)


def device_number(x, c, z, y):
    return ((x * NC + c) * NZ + z) * NY + y


def routes(k, cross):
    pairs = []
    for x in range(NX):
        for c in range(NC):
            for z in range(NZ):
                for y in range(NY):
                    if (c ^ cross) == 0:
                        to = device_number(x, 0, (z + k) % NZ, y)
                    else:
                        to = device_number(x, 1, z, (y + k) % NY)
                    pairs.append((device_number(x, c, z, y), to))
    return pairs


def split_heads_kernel(head_ref, kv_ref, *refs):
    outs, (held, sems) = refs[:-2], refs[-2:]
    inward, outward = [], []
    for i, out in enumerate(outs):
        for part in range(2):
            start = pl.multiple_of(part * KVW + head_ref[i] * HD, HD)
            inward.append(
                pltpu.make_async_copy(
                    kv_ref.at[0, :, pl.ds(start, HD)], held.at[i, part], sems.at[0, i, part]
                )
            )
            outward.append(
                pltpu.make_async_copy(held.at[i, part], out.at[part], sems.at[1, i, part])
            )
    for copy in inward:
        copy.start()
    for copy, onward in zip(inward, outward):
        copy.wait()
        onward.start()
    for copy in outward:
        copy.wait()


def split_heads(heads, prefix_kv):
    n = heads.shape[0]
    return pl.pallas_call(
        split_heads_kernel,
        out_shape=[jax.ShapeDtypeStruct((2, BLOCK, HD), BF16)] * n,
        in_specs=[pl.BlockSpec(memory_space=pltpu.SMEM), pl.BlockSpec(memory_space=pl.ANY)],
        out_specs=[pl.BlockSpec(memory_space=pl.ANY)] * n,
        scratch_shapes=[
            pltpu.VMEM((n, 2, BLOCK, HD), BF16),
            pltpu.SemaphoreType.DMA((2, n, 2)),
        ],
        compiler_params=pltpu.CompilerParams(vmem_limit_bytes=16 * MB),
        name="split_heads",
    )(heads, prefix_kv)


def send_kernel(col_ref, row_ref, q_ref, out_ref):
    wide = HALVES * NY * ROWS
    mates = (col_ref[...] == row_ref[...]) & (
        iota((ROWS, wide), 0) < iota((ROWS, wide), 1) % ROWS
    )
    rank = jnp.sum(mates.astype(jnp.int32), axis=0, keepdims=True)
    slot = row_ref[...] * CAP + rank
    unit = NY * LINES
    rows = NX * unit
    r = iota((rows, wide), 0)
    lane = iota((rows, wide), 1)
    base = r // unit * SLOTS
    half_fits = r // SLOTS % HALVES == lane // ROWS % HALVES
    first = (base + r % SLOTS == slot) & half_fits & (lane < HALVES * ROWS)
    second = (
        (base + (r + CAP) % SLOTS == slot)
        & half_fits
        & (r // LINES % NY == lane // (HALVES * ROWS))
    )
    first = first.astype(F32)
    second = second.astype(F32)
    empty_first = (1.0 - jnp.sum(first, axis=1, keepdims=True)) * EMPTY
    empty_second = (1.0 - jnp.sum(second, axis=1, keepdims=True)) * EMPTY
    first = first[:, : HALVES * ROWS].astype(BF16)
    second = second.astype(BF16)

    def stacked(heads):
        return jnp.concatenate(
            [
                q_ref[:, h * WIDE + half * PART : h * WIDE + (half + 1) * PART].astype(F32)
                for h in heads
                for half in range(HALVES)
            ],
            axis=0,
        ).astype(BF16)

    for z in range(NZ):
        piece = (dot(first, stacked([z])) + empty_first).astype(BF16)
        for x in range(NX):
            at = device_number(x, 0, z, 0) * LINES
            out_ref[at : at + unit, :] = piece[x * unit : (x + 1) * unit]
    piece = dot(second, stacked([NZ + y for y in range(NY)])) + empty_second
    piece = piece.astype(BF16)
    for x in range(NX):
        for z in range(NZ):
            at = device_number(x, 1, z, 0) * LINES
            out_ref[at : at + unit, :] = piece[x * unit : (x + 1) * unit]


def fill_sends(prompt_ids, queries):
    return pl.pallas_call(
        send_kernel,
        out_shape=jax.ShapeDtypeStruct((ARR, PART), BF16),
        compiler_params=pltpu.CompilerParams(vmem_limit_bytes=32 * MB),
        name="fill_sends",
    )(prompt_ids, jnp.tile(prompt_ids.reshape(1, ROWS), (1, HALVES * NY)), queries)


def suffix_kernel(table_ref, len_ref, q_ref, pool_ref, out_ref, lse_ref, kv, sems):
    for row in range(ROWS):
        for p in range(MAXP):
            pltpu.make_async_copy(
                pool_ref.at[table_ref[row, p]],
                kv.at[row, pl.ds(p * PAGE, PAGE), :],
                sems.at[row],
            ).start()

    def one(row, carry):
        pltpu.make_async_copy(kv.at[row], kv.at[row], sems.at[row]).wait()
        scores = jnp.concatenate(
            [
                dot_t(q_ref[row, h], kv[row, :, h * HD : (h + 1) * HD])
                for h in range(KVH)
            ],
            axis=0,
        )
        in_range = iota((KVH * 16, SPAN), 1) < len_ref[row]
        scores = jnp.where(in_range, scores * SCALE, -1e30)
        top = jnp.max(scores, axis=1, keepdims=True)
        weights = jnp.where(in_range, jnp.exp(scores - top), 0.0)
        total = jnp.sum(weights, axis=1, keepdims=True)
        scale = 1.0 / total
        lse = top + jnp.log(total)
        weights = weights.astype(BF16)
        for h in range(KVH):
            cut = slice(h * 16, (h + 1) * 16)
            values = kv[row, :, KVW + h * HD : KVW + (h + 1) * HD]
            out_ref[row, h] = dot(weights[cut], values) * scale[cut]
            lse_ref[row, h] = jnp.broadcast_to(lse[cut], (16, HD))
        return carry

    lax.fori_loop(0, ROWS, one, 0)


def suffix(page_table, suffix_len, queries, suffix_pool):
    q = queries.reshape(ROWS, KVH, GROUP, HD)
    q = jnp.pad(q, ((0, 0), (0, 0), (0, 16 - GROUP), (0, 0)))
    smem = pl.BlockSpec(memory_space=pltpu.SMEM)
    vmem = pl.BlockSpec(memory_space=pltpu.VMEM)
    shape = jax.ShapeDtypeStruct((ROWS, KVH, 16, HD), F32)
    out, lse = pl.pallas_call(
        suffix_kernel,
        out_shape=[shape, shape],
        in_specs=[smem, smem, vmem, pl.BlockSpec(memory_space=pl.ANY)],
        out_specs=[vmem, vmem],
        scratch_shapes=[
            pltpu.VMEM((ROWS, SPAN, 2 * KVW), BF16),
            pltpu.SemaphoreType.DMA((ROWS,)),
        ],
        compiler_params=pltpu.CompilerParams(vmem_limit_bytes=48 * MB),
        cost_estimate=pl.CostEstimate(
            flops=10**9, bytes_accessed=9 * MB, transcendentals=0
        ),
        name="suffix",
    )(page_table, suffix_len, q, suffix_pool)
    return (
        out[:, :, :GROUP].reshape(ROWS, KVH * WIDE),
        lse[:, :, :GROUP].reshape(ROWS, KVH * WIDE),
    )


def line_turn(line):
    return line // CAP % 2


def line_half(line):
    return line // SLOTS % HALVES


def gather_kernel(x_ref, q_ref, place_ref):
    pick = (iota((8, HD), 1) == 0).astype(BF16)
    held = dot_t(pick, x_ref[:, :HD]) < EMPTY / 2
    a, b = iota((ARR, ARR), 0), iota((ARR, ARR), 1)
    before = (a <= b) & (((a ^ b) & (LINES - CAP)) == 0)
    place = dot(held.astype(BF16), before.astype(BF16)).astype(jnp.int32) - 1
    place = jnp.where(held, place, -1)
    place_ref[...] = place
    line = iota((1, ARR), 1)
    for turn in range(2):
        for half in range(HALVES):
            mine = (line_turn(line) == turn) & (line_half(line) == half)
            row = jnp.where(mine, place[0:1], -1)
            gather = (row == iota((HALF, ARR), 0)).astype(BF16)
            for p in range(PAIRS):
                two = dot(gather, x_ref[:, p * 2 * HD : (p + 1) * 2 * HD]).astype(BF16)
                q_ref[turn, half * PER_HALF + 2 * p] = two[:, :HD]
                q_ref[turn, half * PER_HALF + 2 * p + 1] = two[:, HD:]


def gather_rows(arrived):
    return pl.pallas_call(
        gather_kernel,
        out_shape=[
            jax.ShapeDtypeStruct((2, GROUP, HALF, HD), BF16),
            jax.ShapeDtypeStruct((8, ARR), jnp.int32),
        ],
        compiler_params=pltpu.CompilerParams(vmem_limit_bytes=24 * MB),
        name="gather_rows",
    )(arrived)


def row_counts(place_ref):
    line = iota((1, ARR), 1)
    return [
        jnp.max(jnp.where(line_turn(line) == turn, place_ref[0:1], -1)) + 1
        for turn in range(2)
    ]


def widen(column):
    column = column.reshape(GROUP, TILE, 1)
    lane = iota((TILE, HD), 1)
    wide = jnp.zeros((TILE, HD), F32)
    for g in range(GROUP):
        mine = (lane == g) | (lane == g + GROUP) | (lane == g + 2 * GROUP)
        wide = wide + jnp.where(mine, column[g], 0.0)
    return wide


def plain_part(q, keys, values):
    strip = GROUP * TILE // STRIPS
    outs, totals = [], []
    for i in range(STRIPS):
        score = dot_t(q[i * strip : (i + 1) * strip], keys)
        weights = jnp.exp2(score * FACTOR)
        cuts = [weights[:, c : c + HD] for c in range(0, weights.shape[1], HD)]
        totals.append(jnp.sum(functools.reduce(jnp.add, cuts), axis=1, keepdims=True))
        outs.append(dot(weights.astype(BF16), values))
    out = jnp.concatenate(outs, axis=0).reshape(GROUP, TILE, HD)
    return out, widen(jnp.concatenate(totals, axis=0))


def tile_part(q_ref, kv_refs, turn, at):
    q = q_ref[turn, :, pl.ds(at, TILE), :].reshape(GROUP * TILE, HD)
    mine = kv_refs[turn::2]
    keys = jnp.concatenate([ref[0] for ref in mine], axis=0)
    values = jnp.concatenate([ref[1] for ref in mine], axis=0)
    return plain_part(q, keys, values)


def over_tiles(count, step):
    def tile(t, carry):
        step(pl.multiple_of(t * TILE, TILE))
        return carry

    lax.fori_loop(0, (count + TILE - 1) // TILE, tile, 0)


def sums_kernel(blocks, first, q_ref, place_ref, *refs):
    kv_refs, refs = refs[: 2 * blocks], refs[2 * blocks :]
    out_ref, total_ref = refs[-2:]
    for turn, count in enumerate(row_counts(place_ref)):

        def step(at, turn=turn):
            out, total = tile_part(q_ref, kv_refs, turn, at)
            if not first:
                out = out + refs[0][turn, :, pl.ds(at, TILE), :]
                total = total + refs[1][turn, pl.ds(at, TILE), :]
            out_ref[turn, :, pl.ds(at, TILE), :] = out
            total_ref[turn, pl.ds(at, TILE), :] = total

        over_tiles(count, step)


def add_sums(rows, place, kv, state):
    blocks = len(kv) // 2
    vmem = pl.BlockSpec(memory_space=pltpu.VMEM)
    return pl.pallas_call(
        functools.partial(sums_kernel, blocks, not state),
        out_shape=[
            jax.ShapeDtypeStruct((2, GROUP, HALF, HD), F32),
            jax.ShapeDtypeStruct((2, HALF, HD), F32),
        ],
        in_specs=[vmem] * (2 + len(kv) + len(state)),
        out_specs=[vmem, vmem],
        compiler_params=pltpu.CompilerParams(vmem_limit_bytes=32 * MB),
        cost_estimate=pl.CostEstimate(
            flops=blocks * 4 * 10**9, bytes_accessed=8 * MB, transcendentals=0
        ),
        name="sums_%d" % blocks,
    )(rows, place, *kv, *state)


def last_kernel(q_ref, place_ref, sum_ref, total_ref, *refs):
    kv_refs, all_refs, (out_ref, os, ls, held, sems) = refs[:2], refs[2:10], refs[10:]
    for turn in range(2):
        os[turn] = jnp.zeros((GROUP // 2, HALF, 2 * HD), BF16)
        ls[turn] = jnp.zeros((HALF, HD), BF16)
    lane = iota((TILE, HD), 1)

    def finish(turn, at, out, total, shift):
        for g in range(GROUP):
            os[turn, g // 2, pl.ds(at, TILE), g % 2 * HD : (g % 2 + 1) * HD] = (
                out[g] / total[:, g : g + 1]
            ).astype(BF16)
        lse = jnp.where(lane < 3 * GROUP, shift + jnp.log(total), 0.0)
        one = lse.astype(BF16).astype(F32)
        two = (lse - one).astype(BF16).astype(F32)
        three = lse - one - two
        split = jnp.where(lane < GROUP, one, jnp.where(lane < 2 * GROUP, two, three))
        ls[turn, pl.ds(at, TILE), :] = split.astype(BF16)

    for turn, count in enumerate(row_counts(place_ref)):

        def step(at, turn=turn):
            out, total = tile_part(q_ref, kv_refs, turn, at)
            out = out + sum_ref[turn, :, pl.ds(at, TILE), :]
            total = total + total_ref[turn, pl.ds(at, TILE), :]
            finish(turn, at, out, total, 0.0)
            known = jnp.where(lane < 3 * GROUP, total, 1.0)
            plain = (jnp.min(known) > LEAST) & (jnp.max(known) < MOST)

            @pl.when(jnp.logical_not(plain))
            def _():
                q = q_ref[turn, :, pl.ds(at, TILE), :].reshape(GROUP * TILE, HD)
                top = amount = acc = None
                for k in range(4):
                    copy = pltpu.make_async_copy(all_refs[k * 2 + turn], held, sems.at[0])
                    copy.start()
                    copy.wait()
                    score = dot_t(q, held[0])
                    high = jnp.max(score, axis=1, keepdims=True)
                    if k > 0:
                        high = jnp.maximum(top, high)
                    weights = jnp.exp2(score * FACTOR - high * FACTOR)
                    part_amount = jnp.sum(weights, axis=1, keepdims=True)
                    part = dot(weights.astype(BF16), held[1])
                    if k > 0:
                        fade = jnp.exp2((top - high) * FACTOR)
                        part = acc * fade + part
                        part_amount = amount * fade + part_amount
                    top, amount, acc = high, part_amount, part
                acc = acc.reshape(GROUP, TILE, HD)
                finish(turn, at, acc, widen(amount), widen(top * SCALE))

        over_tiles(count, step)

    place_col = jnp.transpose(place_ref[...].astype(F32))[:, 0:1].astype(jnp.int32)
    line = iota((ARR, 1), 0)
    scatter = jnp.concatenate(
        [
            (
                jnp.where((line_turn(line) == turn) & (line_half(line) == half), place_col, -1)
                == iota((ARR, HALF), 1)
            ).astype(BF16)
            for turn in range(2)
            for half in range(HALVES)
        ],
        axis=1,
    )
    for p in range(PAIRS):
        source = jnp.concatenate(
            [os[turn, half * PAIRS + p] for turn in range(2) for half in range(HALVES)], axis=0
        )
        out_ref[:, p * 2 * HD : (p + 1) * 2 * HD] = dot(scatter, source).astype(BF16)
    source = jnp.concatenate([ls[0], ls[0], ls[1], ls[1]], axis=0)
    out_ref[:, PART:] = dot(scatter, source).astype(BF16)


def finish_prefix(rows, place, state, last, everything):
    vmem = pl.BlockSpec(memory_space=pltpu.VMEM)
    return pl.pallas_call(
        last_kernel,
        out_shape=jax.ShapeDtypeStruct((ARR, PART + HD), BF16),
        in_specs=[vmem] * 6 + [pl.BlockSpec(memory_space=pl.ANY)] * 8,
        scratch_shapes=[
            pltpu.VMEM((2, GROUP // 2, HALF, 2 * HD), BF16),
            pltpu.VMEM((2, HALF, HD), BF16),
            pltpu.VMEM((2, BLOCK, HD), BF16),
            pltpu.SemaphoreType.DMA((1,)),
        ],
        compiler_params=pltpu.CompilerParams(vmem_limit_bytes=36 * MB),
        cost_estimate=pl.CostEstimate(
            flops=6 * 10**9, bytes_accessed=8 * MB, transcendentals=0
        ),
        name="finish_prefix",
    )(rows, place, *state, *last, *everything)


def merge_kernel(at_ref, back_ref, so_ref, sl_ref, out_ref):
    picked = KVH * 4 * ROWS
    line = iota((picked, ARR), 1)
    first = dot((at_ref[...] == line).astype(BF16), back_ref[...])
    second = dot((at_ref[...] + SLOTS == line).astype(BF16), back_ref[:, :PART])
    spread = (
        (iota((HD, WIDE), 0) % GROUP == iota((HD, WIDE), 1) // HD)
        & (iota((HD, WIDE), 0) < 3 * GROUP)
    ).astype(BF16)
    lse = dot(first[:, PART:].astype(BF16), spread)
    for h in range(KVH):
        cut = slice(h * WIDE, (h + 1) * WIDE)
        rows = [slice((h * 4 + j) * ROWS, (h * 4 + j + 1) * ROWS) for j in range(4)]
        parts = [
            (lse[r], jnp.concatenate([first[r, :PART], second[r]], axis=1)) for r in rows
        ]
        parts.append((sl_ref[:, cut], so_ref[:, cut]))
        top = functools.reduce(jnp.maximum, [p[0] for p in parts])
        weights = [jnp.exp(p[0] - top) for p in parts]
        total = functools.reduce(jnp.add, weights)
        acc = functools.reduce(jnp.add, [w * p[1] for w, p in zip(weights, parts)])
        out_ref[:, cut] = (acc / total).astype(BF16)


def merge(prompt_ids, back, so, sl):
    prompt = prompt_ids[:, 0]
    earlier = jnp.arange(ROWS)[None, :] < jnp.arange(ROWS)[:, None]
    rank = jnp.sum(((prompt[:, None] == prompt[None, :]) & earlier).astype(jnp.int32), axis=1)
    h = jnp.arange(KVH)[:, None, None]
    j = jnp.arange(4)[None, :, None]
    c = h // 4
    z = jnp.where(c == 0, h, j)
    y = jnp.where(c == 0, j, h - 4)
    place = (prompt % 2 != c).astype(jnp.int32) * CAP + rank
    at = device_number(prompt // 2, c, z, y) * LINES + place
    return pl.pallas_call(
        merge_kernel,
        out_shape=jax.ShapeDtypeStruct((ROWS, KVH * WIDE), BF16),
        compiler_params=pltpu.CompilerParams(vmem_limit_bytes=32 * MB),
        name="merge",
    )(at.reshape(-1, 1), back, so, sl)


def exchange(array):
    width = array.shape[1]
    moved = lax.all_to_all(
        array.reshape(DEVS, LINES, width), AXES, split_axis=0, concat_axis=0, tiled=True
    )
    return moved.reshape(ARR, width)


def body(queries, prompt_ids, suffix_len, page_table, suffix_pool, prefix_kv):
    c = lax.axis_index("pre") % NC
    z = lax.axis_index("row") // NY
    y = lax.axis_index("row") % NY
    heads = jnp.stack(
        [
            jnp.where(c ^ cross == 0, (z + k) % NZ, NZ + (y + k) % NY)
            for k in range(4)
            for cross in range(2)
        ]
    ).astype(jnp.int32)
    sends = fill_sends(prompt_ids, queries)
    sends, prefix_kv = lax.optimization_barrier((sends, prefix_kv))
    arrived = exchange(sends)
    pieces = split_heads(heads, prefix_kv)

    def move(n, piece):
        return lax.ppermute(piece, AXES, routes(n // 2, n % 2))

    kv = list(pieces)
    for n in (2, 3, 6, 7, 1):
        kv[n] = move(n, pieces[n])
    kv[1], later, queries = lax.optimization_barrier((kv[1], pieces[4], queries))
    kv[4] = move(4, later)
    so, sl = suffix(page_table, suffix_len, queries, suffix_pool)
    arrived, so, sl = lax.optimization_barrier((arrived, so, sl))
    rows, place = gather_rows(arrived)
    state = add_sums(rows, place, kv[0:2], ())
    state, kv[2], kv[3], kv[6], kv[7], later = lax.optimization_barrier(
        (state, kv[2], kv[3], kv[6], kv[7], pieces[5])
    )
    kv[5] = move(5, later)
    state = add_sums(rows, place, kv[2:4] + kv[6:8], state)
    back = exchange(finish_prefix(rows, place, state, kv[4:6], kv))
    return merge(prompt_ids, back, so, sl)


def solution(mesh):
    return jax.shard_map(
        body,
        mesh=mesh,
        in_specs=(
            P(("pre", "row"), None),
            P(("pre", "row"), None),
            P(("pre", "row")),
            P(("pre", "row"), None),
            P(("pre", "row"), None, None),
            P("pre", "row", None),
        ),
        out_specs=P(("pre", "row"), None),
        check_vma=False,
    )
```

```python
import functools
import math

import jax
import jax.numpy as jnp
from jax import lax
from jax.experimental import pallas as pl
from jax.experimental.pallas import tpu as pltpu
from jax.sharding import PartitionSpec as P

KVH = 8
HD = 128
CAP = 2
GROUP = 12
ROWS = 8
WIDE = GROUP * HD
KVW = KVH * HD
NX, NC, NZ, NY = 4, 2, 4, 4
DEVS = NX * NC * NZ * NY
BLOCK = 1024
PAGE = 16
MAXP = 16
SPAN = PAGE * MAXP
SLOTS = 2 * CAP
HALVES = 2
PER_HALF = GROUP // HALVES
PAIRS = PER_HALF // 2
PART = PER_HALF * HD
LINES = HALVES * SLOTS
ARR = DEVS * LINES
HALF = DEVS * CAP
TILE = 64
STRIPS = 4
EMPTY = 256.0
SCALE = 1.0 / math.sqrt(HD)
FACTOR = SCALE / math.log(2.0)
LEAST = 1e-26
MOST = 1e30
AXES = ("pre", "row")
MB = 1 << 20
F32 = jnp.float32
BF16 = jnp.bfloat16


def dot(a, b):
    return jnp.dot(a, b, preferred_element_type=F32)


def dot_t(a, b):
    return lax.dot_general(a, b, (((1,), (1,)), ((), ())), preferred_element_type=F32)


def iota(shape, dim):
    return lax.broadcasted_iota(jnp.int32, shape, dim)


def device_number(x, c, z, y):
    return ((x * NC + c) * NZ + z) * NY + y


def routes(k, cross):
    pairs = []
    for x in range(NX):
        for c in range(NC):
            for z in range(NZ):
                for y in range(NY):
                    if (c ^ cross) == 0:
                        to = device_number(x, 0, (z + k) % NZ, y)
                    else:
                        to = device_number(x, 1, z, (y + k) % NY)
                    pairs.append((device_number(x, c, z, y), to))
    return pairs


def split_heads_kernel(head_ref, kv_ref, *refs):
    outs, (held, sems) = refs[:-2], refs[-2:]
    inward, outward = [], []
    for i, out in enumerate(outs):
        for part in range(2):
            start = pl.multiple_of(part * KVW + head_ref[i] * HD, HD)
            inward.append(
                pltpu.make_async_copy(
                    kv_ref.at[0, :, pl.ds(start, HD)], held.at[i, part], sems.at[0, i, part]
                )
            )
            outward.append(
                pltpu.make_async_copy(held.at[i, part], out.at[part], sems.at[1, i, part])
            )
    for copy in inward:
        copy.start()
    for copy, onward in zip(inward, outward):
        copy.wait()
        onward.start()
    for copy in outward:
        copy.wait()


def split_heads(heads, prefix_kv):
    n = heads.shape[0]
    return pl.pallas_call(
        split_heads_kernel,
        out_shape=[jax.ShapeDtypeStruct((2, BLOCK, HD), BF16)] * n,
        in_specs=[pl.BlockSpec(memory_space=pltpu.SMEM), pl.BlockSpec(memory_space=pltpu.HBM)],
        out_specs=[pl.BlockSpec(memory_space=pltpu.HBM)] * n,
        scratch_shapes=[
            pltpu.VMEM((n, 2, BLOCK, HD), BF16),
            pltpu.SemaphoreType.DMA((2, n, 2)),
        ],
        compiler_params=pltpu.CompilerParams(vmem_limit_bytes=8 * MB),
        name="split_heads",
    )(heads, prefix_kv)


def send_kernel(prompt_ref, q_ref, out_ref):
    wide = HALVES * NY * ROWS
    lane = iota((1, wide), 1) % ROWS
    slot = jnp.zeros((1, wide), jnp.int32)
    for i in range(ROWS):
        rank = sum((prompt_ref[j] == prompt_ref[i]).astype(jnp.int32) for j in range(i))
        slot = jnp.where(lane == i, prompt_ref[i] * CAP + rank, slot)
    unit = NY * LINES
    rows = NX * unit
    r = iota((rows, wide), 0)
    lane = iota((rows, wide), 1)
    base = r // unit * SLOTS
    half_fits = r // SLOTS % HALVES == lane // ROWS % HALVES
    first = (base + r % SLOTS == slot) & half_fits & (lane < HALVES * ROWS)
    second = (
        (base + (r + CAP) % SLOTS == slot)
        & half_fits
        & (r // LINES % NY == lane // (HALVES * ROWS))
    )
    first = first.astype(F32)
    second = second.astype(F32)
    empty_first = (1.0 - jnp.sum(first, axis=1, keepdims=True)) * EMPTY
    empty_second = (1.0 - jnp.sum(second, axis=1, keepdims=True)) * EMPTY
    first = first[:, : HALVES * ROWS].astype(BF16)
    second = second.astype(BF16)

    def stacked(heads):
        return jnp.concatenate(
            [
                q_ref[:, h * WIDE + half * PART : h * WIDE + (half + 1) * PART].astype(F32)
                for h in heads
                for half in range(HALVES)
            ],
            axis=0,
        ).astype(BF16)

    for z in range(NZ):
        piece = (dot(first, stacked([z])) + empty_first).astype(BF16)
        for x in range(NX):
            at = device_number(x, 0, z, 0) * LINES
            out_ref[at : at + unit, :] = piece[x * unit : (x + 1) * unit]
    piece = dot(second, stacked([NZ + y for y in range(NY)])) + empty_second
    piece = piece.astype(BF16)
    for x in range(NX):
        for z in range(NZ):
            at = device_number(x, 1, z, 0) * LINES
            out_ref[at : at + unit, :] = piece[x * unit : (x + 1) * unit]


def fill_sends(prompt_ids, queries):
    return pl.pallas_call(
        send_kernel,
        out_shape=jax.ShapeDtypeStruct((ARR, PART), BF16),
        in_specs=[
            pl.BlockSpec(memory_space=pltpu.SMEM),
            pl.BlockSpec(memory_space=pltpu.VMEM),
        ],
        compiler_params=pltpu.CompilerParams(vmem_limit_bytes=12 * MB),
        name="fill_sends",
    )(prompt_ids[:, 0], queries)


def suffix_kernel(table_ref, len_ref, q_ref, pool_ref, out_ref, lse_ref, kv, sems):
    for row in range(ROWS):
        for p in range(MAXP):
            pltpu.make_async_copy(
                pool_ref.at[table_ref[row, p]],
                kv.at[row, pl.ds(p * PAGE, PAGE), :],
                sems.at[row],
            ).start()

    def one(row, carry):
        pltpu.make_async_copy(kv.at[row], kv.at[row], sems.at[row]).wait()
        scores = jnp.concatenate(
            [
                dot_t(q_ref[row, h], kv[row, :, h * HD : (h + 1) * HD])
                for h in range(KVH)
            ],
            axis=0,
        )
        in_range = iota((KVH * 16, SPAN), 1) < len_ref[row]
        scores = jnp.where(in_range, scores * SCALE, -1e30)
        top = jnp.max(scores, axis=1, keepdims=True)
        weights = jnp.where(in_range, jnp.exp(scores - top), 0.0)
        total = jnp.sum(weights, axis=1, keepdims=True)
        scale = 1.0 / total
        lse = top + jnp.log(total)
        weights = weights.astype(BF16)
        for h in range(KVH):
            cut = slice(h * 16, (h + 1) * 16)
            values = kv[row, :, KVW + h * HD : KVW + (h + 1) * HD]
            out_ref[row, h] = dot(weights[cut], values) * scale[cut]
            lse_ref[row, h] = jnp.broadcast_to(lse[cut], (16, HD))
        return carry

    lax.fori_loop(0, ROWS, one, 0)


def suffix(page_table, suffix_len, queries, suffix_pool):
    q = queries.reshape(ROWS, KVH, GROUP, HD)
    q = jnp.pad(q, ((0, 0), (0, 0), (0, 16 - GROUP), (0, 0)))
    smem = pl.BlockSpec(memory_space=pltpu.SMEM)
    vmem = pl.BlockSpec(memory_space=pltpu.VMEM)
    shape = jax.ShapeDtypeStruct((ROWS, KVH, 16, HD), F32)
    out, lse = pl.pallas_call(
        suffix_kernel,
        out_shape=[shape, shape],
        in_specs=[smem, smem, vmem, pl.BlockSpec(memory_space=pl.ANY)],
        out_specs=[vmem, vmem],
        scratch_shapes=[
            pltpu.VMEM((ROWS, SPAN, 2 * KVW), BF16),
            pltpu.SemaphoreType.DMA((ROWS,)),
        ],
        compiler_params=pltpu.CompilerParams(vmem_limit_bytes=20 * MB),
        cost_estimate=pl.CostEstimate(
            flops=10**9, bytes_accessed=9 * MB, transcendentals=0
        ),
        name="suffix",
    )(page_table, suffix_len, q, suffix_pool)
    return (
        out[:, :, :GROUP].reshape(ROWS, KVH * WIDE),
        lse[:, :, :GROUP].reshape(ROWS, KVH * WIDE),
    )


def line_turn(line):
    return line // CAP % 2


def line_half(line):
    return line // SLOTS % HALVES


def gather_kernel(x_ref, q_ref, place_ref):
    pick = (iota((8, HD), 1) == 0).astype(BF16)
    held = dot_t(pick, x_ref[:, :HD]) < EMPTY / 2
    a, b = iota((ARR, ARR), 0), iota((ARR, ARR), 1)
    before = (a <= b) & (((a ^ b) & (LINES - CAP)) == 0)
    place = dot(held.astype(BF16), before.astype(BF16)).astype(jnp.int32) - 1
    place = jnp.where(held, place, -1)
    place_ref[...] = place
    line = iota((1, ARR), 1)
    for turn in range(2):
        for half in range(HALVES):
            mine = (line_turn(line) == turn) & (line_half(line) == half)
            row = jnp.where(mine, place[0:1], -1)
            gather = (row == iota((HALF, ARR), 0)).astype(BF16)
            for p in range(PAIRS):
                two = dot(gather, x_ref[:, p * 2 * HD : (p + 1) * 2 * HD]).astype(BF16)
                q_ref[turn, half * PER_HALF + 2 * p] = two[:, :HD]
                q_ref[turn, half * PER_HALF + 2 * p + 1] = two[:, HD:]


def gather_rows(arrived):
    return pl.pallas_call(
        gather_kernel,
        out_shape=[
            jax.ShapeDtypeStruct((2, GROUP, HALF, HD), BF16),
            jax.ShapeDtypeStruct((8, ARR), jnp.int32),
        ],
        compiler_params=pltpu.CompilerParams(vmem_limit_bytes=16 * MB),
        name="gather_rows",
    )(arrived)


def row_counts(place_ref):
    line = iota((1, ARR), 1)
    return [
        jnp.max(jnp.where(line_turn(line) == turn, place_ref[0:1], -1)) + 1
        for turn in range(2)
    ]


def widen(column):
    column = column.reshape(GROUP, TILE, 1)
    lane = iota((TILE, HD), 1)
    wide = jnp.zeros((TILE, HD), F32)
    for g in range(GROUP):
        mine = (lane == g) | (lane == g + GROUP) | (lane == g + 2 * GROUP)
        wide = wide + jnp.where(mine, column[g], 0.0)
    return wide


def plain_part(q, keys, values):
    strip = GROUP * TILE // STRIPS
    outs, totals = [], []
    for i in range(STRIPS):
        score = dot_t(q[i * strip : (i + 1) * strip], keys)
        weights = jnp.exp2(score * FACTOR)
        cuts = [weights[:, c : c + HD] for c in range(0, weights.shape[1], HD)]
        totals.append(jnp.sum(functools.reduce(jnp.add, cuts), axis=1, keepdims=True))
        outs.append(dot(weights.astype(BF16), values))
    out = jnp.concatenate(outs, axis=0).reshape(GROUP, TILE, HD)
    return out, widen(jnp.concatenate(totals, axis=0))


def tile_part(q_ref, kv_refs, turn, at):
    q = q_ref[turn, :, pl.ds(at, TILE), :].reshape(GROUP * TILE, HD)
    mine = kv_refs[turn::2]
    keys = jnp.concatenate([ref[0] for ref in mine], axis=0)
    values = jnp.concatenate([ref[1] for ref in mine], axis=0)
    return plain_part(q, keys, values)


def over_tiles(count, step):
    def tile(t, carry):
        step(pl.multiple_of(t * TILE, TILE))
        return carry

    lax.fori_loop(0, (count + TILE - 1) // TILE, tile, 0)


def sums_kernel(blocks, first, q_ref, place_ref, *refs):
    kv_refs, refs = refs[: 2 * blocks], refs[2 * blocks :]
    out_ref, total_ref = refs[-2:]
    for turn, count in enumerate(row_counts(place_ref)):

        def step(at, turn=turn):
            out, total = tile_part(q_ref, kv_refs, turn, at)
            if not first:
                out = out + refs[0][turn, :, pl.ds(at, TILE), :]
                total = total + refs[1][turn, pl.ds(at, TILE), :]
            out_ref[turn, :, pl.ds(at, TILE), :] = out
            total_ref[turn, pl.ds(at, TILE), :] = total

        over_tiles(count, step)


def add_sums(rows, place, kv, state):
    blocks = len(kv) // 2
    vmem = pl.BlockSpec(memory_space=pltpu.VMEM)
    return pl.pallas_call(
        functools.partial(sums_kernel, blocks, not state),
        out_shape=[
            jax.ShapeDtypeStruct((2, GROUP, HALF, HD), F32),
            jax.ShapeDtypeStruct((2, HALF, HD), F32),
        ],
        in_specs=[vmem] * (2 + len(kv) + len(state)),
        out_specs=[vmem, vmem],
        compiler_params=pltpu.CompilerParams(vmem_limit_bytes=16 * MB),
        cost_estimate=pl.CostEstimate(
            flops=blocks * 4 * 10**9, bytes_accessed=8 * MB, transcendentals=0
        ),
        name="sums_%d" % blocks,
    )(rows, place, *kv, *state)


def last_kernel(q_ref, place_ref, sum_ref, total_ref, *refs):
    kv_refs, all_refs, (final_ref, os, ls, held, sems, out_ref, out_sems) = refs[:2], refs[2:10], refs[10:]
    for turn in range(2):
        os[turn] = jnp.zeros((GROUP // 2, HALF, 2 * HD), BF16)
        ls[turn] = jnp.zeros((HALF, HD), BF16)
    lane = iota((TILE, HD), 1)

    def finish(turn, at, out, total, shift):
        for g in range(GROUP):
            os[turn, g // 2, pl.ds(at, TILE), g % 2 * HD : (g % 2 + 1) * HD] = (
                out[g] / total[:, g : g + 1]
            ).astype(BF16)
        lse = jnp.where(lane < 3 * GROUP, shift + jnp.log(total), 0.0)
        one = lse.astype(BF16).astype(F32)
        two = (lse - one).astype(BF16).astype(F32)
        three = lse - one - two
        split = jnp.where(lane < GROUP, one, jnp.where(lane < 2 * GROUP, two, three))
        ls[turn, pl.ds(at, TILE), :] = split.astype(BF16)

    for turn, count in enumerate(row_counts(place_ref)):

        def step(at, turn=turn):
            out, total = tile_part(q_ref, kv_refs, turn, at)
            out = out + sum_ref[turn, :, pl.ds(at, TILE), :]
            total = total + total_ref[turn, pl.ds(at, TILE), :]
            finish(turn, at, out, total, 0.0)
            known = jnp.where(lane < 3 * GROUP, total, 1.0)
            plain = (jnp.min(known) > LEAST) & (jnp.max(known) < MOST)

            @pl.when(jnp.logical_not(plain))
            def _():
                q = q_ref[turn, :, pl.ds(at, TILE), :].reshape(GROUP * TILE, HD)
                top = amount = acc = None
                for k in range(4):
                    copy = pltpu.make_async_copy(all_refs[k * 2 + turn], held, sems.at[0])
                    copy.start()
                    copy.wait()
                    score = dot_t(q, held[0])
                    high = jnp.max(score, axis=1, keepdims=True)
                    if k > 0:
                        high = jnp.maximum(top, high)
                    weights = jnp.exp2(score * FACTOR - high * FACTOR)
                    part_amount = jnp.sum(weights, axis=1, keepdims=True)
                    part = dot(weights.astype(BF16), held[1])
                    if k > 0:
                        fade = jnp.exp2((top - high) * FACTOR)
                        part = acc * fade + part
                        part_amount = amount * fade + part_amount
                    top, amount, acc = high, part_amount, part
                acc = acc.reshape(GROUP, TILE, HD)
                finish(turn, at, acc, widen(amount), widen(top * SCALE))

        over_tiles(count, step)

    place_col = jnp.transpose(place_ref[...].astype(F32))[:, 0:1].astype(jnp.int32)
    line = iota((ARR, 1), 0)
    scatter = jnp.concatenate(
        [
            (
                jnp.where((line_turn(line) == turn) & (line_half(line) == half), place_col, -1)
                == iota((ARR, HALF), 1)
            ).astype(BF16)
            for turn in range(2)
            for half in range(HALVES)
        ],
        axis=1,
    )
    copies = []

    def send(p, width, piece):
        cut = pl.ds(p * 2 * HD, width)
        out_ref[:, cut] = piece.astype(BF16)
        copy = pltpu.make_async_copy(out_ref.at[:, cut], final_ref.at[:, cut], out_sems.at[p])
        copy.start()
        copies.append(copy)

    for p in range(PAIRS):
        source = jnp.concatenate(
            [os[turn, half * PAIRS + p] for turn in range(2) for half in range(HALVES)], axis=0
        )
        send(p, 2 * HD, dot(scatter, source))
    source = jnp.concatenate([ls[0], ls[0], ls[1], ls[1]], axis=0)
    send(PAIRS, HD, dot(scatter, source))
    for copy in copies:
        copy.wait()


def finish_prefix(rows, place, state, last, everything):
    vmem = pl.BlockSpec(memory_space=pltpu.VMEM)
    return pl.pallas_call(
        last_kernel,
        out_shape=jax.ShapeDtypeStruct((ARR, PART + HD), BF16),
        in_specs=[vmem] * 6 + [pl.BlockSpec(memory_space=pl.ANY)] * 8,
        out_specs=pl.BlockSpec(memory_space=pltpu.HBM),
        scratch_shapes=[
            pltpu.VMEM((2, GROUP // 2, HALF, 2 * HD), BF16),
            pltpu.VMEM((2, HALF, HD), BF16),
            pltpu.VMEM((2, BLOCK, HD), BF16),
            pltpu.SemaphoreType.DMA((1,)),
            pltpu.VMEM((ARR, PART + HD), BF16),
            pltpu.SemaphoreType.DMA((PAIRS + 1,)),
        ],
        compiler_params=pltpu.CompilerParams(vmem_limit_bytes=20 * MB),
        cost_estimate=pl.CostEstimate(
            flops=6 * 10**9, bytes_accessed=8 * MB, transcendentals=0
        ),
        name="finish_prefix",
    )(rows, place, *state, *last, *everything)


def merge_kernel(at_ref, back_ref, so_ref, sl_ref, out_ref):
    picked = KVH * 4 * ROWS
    line = iota((picked, ARR), 1)
    first = dot((at_ref[...] == line).astype(BF16), back_ref[...])
    second = dot((at_ref[...] + SLOTS == line).astype(BF16), back_ref[:, :PART])
    spread = (
        (iota((HD, WIDE), 0) % GROUP == iota((HD, WIDE), 1) // HD)
        & (iota((HD, WIDE), 0) < 3 * GROUP)
    ).astype(BF16)
    lse = dot(first[:, PART:].astype(BF16), spread)
    for h in range(KVH):
        cut = slice(h * WIDE, (h + 1) * WIDE)
        rows = [slice((h * 4 + j) * ROWS, (h * 4 + j + 1) * ROWS) for j in range(4)]
        parts = [
            (lse[r], jnp.concatenate([first[r, :PART], second[r]], axis=1)) for r in rows
        ]
        parts.append((sl_ref[:, cut], so_ref[:, cut]))
        top = functools.reduce(jnp.maximum, [p[0] for p in parts])
        weights = [jnp.exp(p[0] - top) for p in parts]
        total = functools.reduce(jnp.add, weights)
        acc = functools.reduce(jnp.add, [w * p[1] for w, p in zip(weights, parts)])
        out_ref[:, cut] = (acc / total).astype(BF16)


def merge(prompt_ids, back, so, sl):
    prompt = prompt_ids[:, 0]
    earlier = jnp.arange(ROWS)[None, :] < jnp.arange(ROWS)[:, None]
    rank = jnp.sum(((prompt[:, None] == prompt[None, :]) & earlier).astype(jnp.int32), axis=1)
    h = jnp.arange(KVH)[:, None, None]
    j = jnp.arange(4)[None, :, None]
    c = h // 4
    z = jnp.where(c == 0, h, j)
    y = jnp.where(c == 0, j, h - 4)
    place = (prompt % 2 != c).astype(jnp.int32) * CAP + rank
    at = device_number(prompt // 2, c, z, y) * LINES + place
    return pl.pallas_call(
        merge_kernel,
        out_shape=jax.ShapeDtypeStruct((ROWS, KVH * WIDE), BF16),
        compiler_params=pltpu.CompilerParams(vmem_limit_bytes=16 * MB),
        name="merge",
    )(at.reshape(-1, 1), back, so, sl)


def exchange(array):
    width = array.shape[1]
    moved = lax.all_to_all(
        array.reshape(DEVS, LINES, width), AXES, split_axis=0, concat_axis=0, tiled=True
    )
    return moved.reshape(ARR, width)


def body(queries, prompt_ids, suffix_len, page_table, suffix_pool, prefix_kv):
    c = lax.axis_index("pre") % NC
    z = lax.axis_index("row") // NY
    y = lax.axis_index("row") % NY
    heads = jnp.stack(
        [
            jnp.where(c ^ cross == 0, (z + k) % NZ, NZ + (y + k) % NY)
            for k in range(4)
            for cross in range(2)
        ]
    ).astype(jnp.int32)
    sends = fill_sends(prompt_ids, queries)
    sends, heads = lax.optimization_barrier((sends, heads))
    arrived = exchange(sends)
    pieces = split_heads(heads, prefix_kv)

    def move(n, piece):
        return lax.ppermute(piece, AXES, routes(n // 2, n % 2))

    kv = list(pieces)
    for n in (1, 2, 3, 6, 7):
        kv[n] = move(n, pieces[n])
    arrived, kv[1], later = lax.optimization_barrier((arrived, kv[1], pieces[4]))
    kv[4] = move(4, later)
    rows, place = gather_rows(arrived)
    state = add_sums(rows, place, kv[0:2], ())
    state, kv[2], kv[3], kv[6], kv[7], later = lax.optimization_barrier(
        (state, kv[2], kv[3], kv[6], kv[7], pieces[5])
    )
    kv[5] = move(5, later)
    state = add_sums(rows, place, kv[2:4] + kv[6:8], state)
    parts = finish_prefix(rows, place, state, kv[4:6], kv)
    parts, queries = lax.optimization_barrier((parts, queries))
    so, sl = suffix(page_table, suffix_len, queries, suffix_pool)
    return merge(prompt_ids, exchange(parts), so, sl)


def solution(mesh):
    return jax.shard_map(
        body,
        mesh=mesh,
        in_specs=(
            P(("pre", "row"), None),
            P(("pre", "row"), None),
            P(("pre", "row")),
            P(("pre", "row"), None),
            P(("pre", "row"), None, None),
            P("pre", "row", None),
        ),
        out_specs=P(("pre", "row"), None),
        check_vma=False,
    )
```

```python
import functools
import math

import jax
import jax.numpy as jnp
from jax import lax
from jax.experimental import pallas as pl
from jax.experimental.pallas import tpu as pltpu
from jax.sharding import PartitionSpec as P

KVH = 8
HD = 128
CAP = 2
GROUP = 12
ROWS = 8
WIDE = GROUP * HD
KVW = KVH * HD
NX, NC, NZ, NY = 4, 2, 4, 4
DEVS = NX * NC * NZ * NY
BLOCK = 1024
PAGE = 16
MAXP = 16
SPAN = PAGE * MAXP
SLOTS = 2 * CAP
HALVES = 2
PER_HALF = GROUP // HALVES
PAIRS = PER_HALF // 2
PART = PER_HALF * HD
LINES = HALVES * SLOTS
ARR = DEVS * LINES
HALF = DEVS * CAP
TILE = 64
STRIPS = 4
EMPTY = 256.0
SCALE = 1.0 / math.sqrt(HD)
FACTOR = SCALE / math.log(2.0)
LEAST = 1e-26
MOST = 1e30
AXES = ("pre", "row")
MB = 1 << 20
F32 = jnp.float32
BF16 = jnp.bfloat16


def dot(a, b):
    return jnp.dot(a, b, preferred_element_type=F32)


def dot_t(a, b):
    return lax.dot_general(a, b, (((1,), (1,)), ((), ())), preferred_element_type=F32)


def iota(shape, dim):
    return lax.broadcasted_iota(jnp.int32, shape, dim)


def device_number(x, c, z, y):
    return ((x * NC + c) * NZ + z) * NY + y


def routes(step):
    pairs = []
    for x in range(NX):
        for c in range(NC):
            for z in range(NZ):
                for y in range(NY):
                    if step is None:
                        to = device_number(x, 1 - c, z, y)
                    elif c == 0:
                        to = device_number(x, 0, (z + step) % NZ, y)
                    else:
                        to = device_number(x, 1, z, (y + step) % NY)
                    pairs.append((device_number(x, c, z, y), to))
    return pairs


def split_heads_kernel(head_ref, kv_ref, *refs):
    outs, (held, sems) = refs[:-2], refs[-2:]
    places = [out for out in outs[:4]] + [outs[4].at[k] for k in range(4)]
    inward, outward = [], []
    for i, out in enumerate(places):
        for part in range(2):
            start = pl.multiple_of(part * KVW + head_ref[i] * HD, HD)
            inward.append(
                pltpu.make_async_copy(
                    kv_ref.at[0, :, pl.ds(start, HD)], held.at[i, part], sems.at[0, i, part]
                )
            )
            outward.append(
                pltpu.make_async_copy(held.at[i, part], out.at[part], sems.at[1, i, part])
            )
    inward, outward = inward[8:] + inward[:8], outward[8:] + outward[:8]
    for copy in inward:
        copy.start()
    for copy, onward in zip(inward, outward):
        copy.wait()
        onward.start()
    for copy in outward:
        copy.wait()


def split_heads(heads, prefix_kv):
    n = heads.shape[0]
    any_place = pl.BlockSpec(memory_space=pl.ANY)
    return pl.pallas_call(
        split_heads_kernel,
        out_shape=[jax.ShapeDtypeStruct((2, BLOCK, HD), BF16)] * 4
        + [jax.ShapeDtypeStruct((4, 2, BLOCK, HD), BF16)],
        in_specs=[pl.BlockSpec(memory_space=pltpu.SMEM), any_place],
        out_specs=[any_place] * 5,
        scratch_shapes=[
            pltpu.VMEM((n, 2, BLOCK, HD), BF16),
            pltpu.SemaphoreType.DMA((2, n, 2)),
        ],
        compiler_params=pltpu.CompilerParams(vmem_limit_bytes=60 * MB),
        name="split_heads",
    )(heads, prefix_kv)


def pair_kernel(*refs):
    other_ref = refs[4]
    for k in range(4):
        refs[5 + k][0] = refs[k][...]
        refs[5 + k][1] = other_ref[k]


def pair_up(own, other):
    return pl.pallas_call(
        pair_kernel,
        out_shape=[jax.ShapeDtypeStruct((2, 2, BLOCK, HD), BF16)] * 4,
        compiler_params=pltpu.CompilerParams(vmem_limit_bytes=20 * MB),
        name="pair_up",
    )(*own, other)


def send_kernel(prompt_ref, q_ref, out_ref):
    wide = HALVES * NY * ROWS
    lane = iota((1, wide), 1) % ROWS
    slot = jnp.zeros((1, wide), jnp.int32)
    for i in range(ROWS):
        rank = sum((prompt_ref[j] == prompt_ref[i]).astype(jnp.int32) for j in range(i))
        slot = jnp.where(lane == i, prompt_ref[i] * CAP + rank, slot)
    unit = NY * LINES
    rows = NX * unit
    r = iota((rows, wide), 0)
    lane = iota((rows, wide), 1)
    base = r // unit * SLOTS
    half_fits = r // SLOTS % HALVES == lane // ROWS % HALVES
    first = (base + r % SLOTS == slot) & half_fits & (lane < HALVES * ROWS)
    second = (
        (base + (r + CAP) % SLOTS == slot)
        & half_fits
        & (r // LINES % NY == lane // (HALVES * ROWS))
    )
    first = first.astype(F32)
    second = second.astype(F32)
    empty_first = (1.0 - jnp.sum(first, axis=1, keepdims=True)) * EMPTY
    empty_second = (1.0 - jnp.sum(second, axis=1, keepdims=True)) * EMPTY
    first = first[:, : HALVES * ROWS].astype(BF16)
    second = second.astype(BF16)

    def stacked(heads):
        return jnp.concatenate(
            [
                q_ref[:, h * WIDE + half * PART : h * WIDE + (half + 1) * PART].astype(F32)
                for h in heads
                for half in range(HALVES)
            ],
            axis=0,
        ).astype(BF16)

    for z in range(NZ):
        piece = (dot(first, stacked([z])) + empty_first).astype(BF16)
        for x in range(NX):
            at = device_number(x, 0, z, 0) * LINES
            out_ref[at : at + unit, :] = piece[x * unit : (x + 1) * unit]
    piece = dot(second, stacked([NZ + y for y in range(NY)])) + empty_second
    piece = piece.astype(BF16)
    for x in range(NX):
        for z in range(NZ):
            at = device_number(x, 1, z, 0) * LINES
            out_ref[at : at + unit, :] = piece[x * unit : (x + 1) * unit]


def fill_sends(prompt_ids, queries):
    return pl.pallas_call(
        send_kernel,
        out_shape=jax.ShapeDtypeStruct((ARR, PART), BF16),
        in_specs=[
            pl.BlockSpec(memory_space=pltpu.SMEM),
            pl.BlockSpec(memory_space=pltpu.VMEM),
        ],
        compiler_params=pltpu.CompilerParams(vmem_limit_bytes=12 * MB),
        name="fill_sends",
    )(prompt_ids[:, 0], queries)


def suffix_kernel(table_ref, len_ref, q_ref, pool_ref, out_ref, lse_ref, kv, sems):
    for row in range(ROWS):
        for p in range(MAXP):
            pltpu.make_async_copy(
                pool_ref.at[table_ref[row, p]],
                kv.at[row, pl.ds(p * PAGE, PAGE), :],
                sems.at[row],
            ).start()

    def one(row, carry):
        pltpu.make_async_copy(kv.at[row], kv.at[row], sems.at[row]).wait()
        scores = jnp.concatenate(
            [
                dot_t(q_ref[row, h], kv[row, :, h * HD : (h + 1) * HD])
                for h in range(KVH)
            ],
            axis=0,
        )
        in_range = iota((KVH * 16, SPAN), 1) < len_ref[row]
        scores = jnp.where(in_range, scores * SCALE, -1e30)
        top = jnp.max(scores, axis=1, keepdims=True)
        weights = jnp.where(in_range, jnp.exp(scores - top), 0.0)
        total = jnp.sum(weights, axis=1, keepdims=True)
        scale = 1.0 / total
        lse = top + jnp.log(total)
        weights = weights.astype(BF16)
        for h in range(KVH):
            cut = slice(h * 16, (h + 1) * 16)
            values = kv[row, :, KVW + h * HD : KVW + (h + 1) * HD]
            out_ref[row, h] = dot(weights[cut], values) * scale[cut]
            lse_ref[row, h] = jnp.broadcast_to(lse[cut], (16, HD))
        return carry

    lax.fori_loop(0, ROWS, one, 0)


def suffix(page_table, suffix_len, queries, suffix_pool):
    q = queries.reshape(ROWS, KVH, GROUP, HD)
    q = jnp.pad(q, ((0, 0), (0, 0), (0, 16 - GROUP), (0, 0)))
    smem = pl.BlockSpec(memory_space=pltpu.SMEM)
    vmem = pl.BlockSpec(memory_space=pltpu.VMEM)
    shape = jax.ShapeDtypeStruct((ROWS, KVH, 16, HD), F32)
    out, lse = pl.pallas_call(
        suffix_kernel,
        out_shape=[shape, shape],
        in_specs=[smem, smem, vmem, pl.BlockSpec(memory_space=pl.ANY)],
        out_specs=[vmem, vmem],
        scratch_shapes=[
            pltpu.VMEM((ROWS, SPAN, 2 * KVW), BF16),
            pltpu.SemaphoreType.DMA((ROWS,)),
        ],
        compiler_params=pltpu.CompilerParams(vmem_limit_bytes=56 * MB),
        cost_estimate=pl.CostEstimate(
            flops=10**9, bytes_accessed=9 * MB, transcendentals=0
        ),
        name="suffix",
    )(page_table, suffix_len, q, suffix_pool)
    return (
        out[:, :, :GROUP].reshape(ROWS, KVH * WIDE),
        lse[:, :, :GROUP].reshape(ROWS, KVH * WIDE),
    )


def line_turn(line):
    return line // CAP % 2


def line_half(line):
    return line // SLOTS % HALVES


def gather_kernel(x_ref, q_ref, place_ref):
    pick = (iota((8, HD), 1) == 0).astype(BF16)
    held = dot_t(pick, x_ref[:, :HD]) < EMPTY / 2
    a, b = iota((ARR, ARR), 0), iota((ARR, ARR), 1)
    before = (a <= b) & (((a ^ b) & (LINES - CAP)) == 0)
    place = dot(held.astype(BF16), before.astype(BF16)).astype(jnp.int32) - 1
    place = jnp.where(held, place, -1)
    place_ref[...] = place
    line = iota((1, ARR), 1)
    for turn in range(2):
        for half in range(HALVES):
            mine = (line_turn(line) == turn) & (line_half(line) == half)
            row = jnp.where(mine, place[0:1], -1)
            gather = (row == iota((HALF, ARR), 0)).astype(BF16)
            for p in range(PAIRS):
                two = dot(gather, x_ref[:, p * 2 * HD : (p + 1) * 2 * HD]).astype(BF16)
                q_ref[turn, half * PER_HALF + 2 * p] = two[:, :HD]
                q_ref[turn, half * PER_HALF + 2 * p + 1] = two[:, HD:]


def gather_rows(arrived):
    return pl.pallas_call(
        gather_kernel,
        out_shape=[
            jax.ShapeDtypeStruct((2, GROUP, HALF, HD), BF16),
            jax.ShapeDtypeStruct((8, ARR), jnp.int32),
        ],
        compiler_params=pltpu.CompilerParams(vmem_limit_bytes=16 * MB),
        name="gather_rows",
    )(arrived)


def row_counts(place_ref):
    line = iota((1, ARR), 1)
    return [
        jnp.max(jnp.where(line_turn(line) == turn, place_ref[0:1], -1)) + 1
        for turn in range(2)
    ]


def widen(column):
    column = column.reshape(GROUP, TILE, 1)
    lane = iota((TILE, HD), 1)
    wide = jnp.zeros((TILE, HD), F32)
    for g in range(GROUP):
        mine = (lane == g) | (lane == g + GROUP) | (lane == g + 2 * GROUP)
        wide = wide + jnp.where(mine, column[g], 0.0)
    return wide


def plain_part(q, keys, values):
    strip = GROUP * TILE // STRIPS
    outs, totals = [], []
    for i in range(STRIPS):
        score = dot_t(q[i * strip : (i + 1) * strip], keys)
        weights = jnp.exp2(score * FACTOR)
        cuts = [weights[:, c : c + HD] for c in range(0, weights.shape[1], HD)]
        totals.append(jnp.sum(functools.reduce(jnp.add, cuts), axis=1, keepdims=True))
        outs.append(dot(weights.astype(BF16), values))
    out = jnp.concatenate(outs, axis=0).reshape(GROUP, TILE, HD)
    return out, widen(jnp.concatenate(totals, axis=0))


def tile_part(q_ref, kv_refs, turn, at):
    q = q_ref[turn, :, pl.ds(at, TILE), :].reshape(GROUP * TILE, HD)
    keys = jnp.concatenate([ref[turn, 0] for ref in kv_refs], axis=0)
    values = jnp.concatenate([ref[turn, 1] for ref in kv_refs], axis=0)
    return plain_part(q, keys, values)


def over_tiles(count, step):
    def tile(t, carry):
        step(pl.multiple_of(t * TILE, TILE))
        return carry

    lax.fori_loop(0, (count + TILE - 1) // TILE, tile, 0)


def sums_kernel(blocks, first, q_ref, place_ref, *refs):
    kv_refs, refs = refs[:blocks], refs[blocks:]
    out_ref, total_ref = refs[-2:]
    for turn, count in enumerate(row_counts(place_ref)):

        def step(at, turn=turn):
            out, total = tile_part(q_ref, kv_refs, turn, at)
            if not first:
                out = out + refs[0][turn, :, pl.ds(at, TILE), :]
                total = total + refs[1][turn, pl.ds(at, TILE), :]
            out_ref[turn, :, pl.ds(at, TILE), :] = out
            total_ref[turn, pl.ds(at, TILE), :] = total

        over_tiles(count, step)


def add_sums(rows, place, kv, state):
    blocks = len(kv)
    vmem = pl.BlockSpec(memory_space=pltpu.VMEM)
    return pl.pallas_call(
        functools.partial(sums_kernel, blocks, not state),
        out_shape=[
            jax.ShapeDtypeStruct((2, GROUP, HALF, HD), F32),
            jax.ShapeDtypeStruct((2, HALF, HD), F32),
        ],
        in_specs=[vmem] * (2 + len(kv) + len(state)),
        out_specs=[vmem, vmem],
        compiler_params=pltpu.CompilerParams(vmem_limit_bytes=16 * MB),
        cost_estimate=pl.CostEstimate(
            flops=blocks * 4 * 10**9, bytes_accessed=8 * MB, transcendentals=0
        ),
        name="sums_%d" % blocks,
    )(rows, place, *kv, *state)


def last_kernel(q_ref, place_ref, sum_ref, total_ref, *refs):
    kv_refs, all_refs, (out_ref, os, ls, held, sems) = refs[:1], refs[1:5], refs[5:]
    for turn in range(2):
        os[turn] = jnp.zeros((GROUP // 2, HALF, 2 * HD), BF16)
        ls[turn] = jnp.zeros((HALF, HD), BF16)
    lane = iota((TILE, HD), 1)

    def finish(turn, at, out, total, shift):
        for g in range(GROUP):
            os[turn, g // 2, pl.ds(at, TILE), g % 2 * HD : (g % 2 + 1) * HD] = (
                out[g] / total[:, g : g + 1]
            ).astype(BF16)
        lse = jnp.where(lane < 3 * GROUP, shift + jnp.log(total), 0.0)
        one = lse.astype(BF16).astype(F32)
        two = (lse - one).astype(BF16).astype(F32)
        three = lse - one - two
        split = jnp.where(lane < GROUP, one, jnp.where(lane < 2 * GROUP, two, three))
        ls[turn, pl.ds(at, TILE), :] = split.astype(BF16)

    for turn, count in enumerate(row_counts(place_ref)):

        def step(at, turn=turn):
            out, total = tile_part(q_ref, kv_refs, turn, at)
            out = out + sum_ref[turn, :, pl.ds(at, TILE), :]
            total = total + total_ref[turn, pl.ds(at, TILE), :]
            finish(turn, at, out, total, 0.0)
            known = jnp.where(lane < 3 * GROUP, total, 1.0)
            plain = (jnp.min(known) > LEAST) & (jnp.max(known) < MOST)

            @pl.when(jnp.logical_not(plain))
            def _():
                q = q_ref[turn, :, pl.ds(at, TILE), :].reshape(GROUP * TILE, HD)
                top = amount = acc = None
                for k in range(4):
                    copy = pltpu.make_async_copy(all_refs[k].at[turn], held, sems.at[0])
                    copy.start()
                    copy.wait()
                    score = dot_t(q, held[0])
                    high = jnp.max(score, axis=1, keepdims=True)
                    if k > 0:
                        high = jnp.maximum(top, high)
                    weights = jnp.exp2(score * FACTOR - high * FACTOR)
                    part_amount = jnp.sum(weights, axis=1, keepdims=True)
                    part = dot(weights.astype(BF16), held[1])
                    if k > 0:
                        fade = jnp.exp2((top - high) * FACTOR)
                        part = acc * fade + part
                        part_amount = amount * fade + part_amount
                    top, amount, acc = high, part_amount, part
                acc = acc.reshape(GROUP, TILE, HD)
                finish(turn, at, acc, widen(amount), widen(top * SCALE))

        over_tiles(count, step)

    place_col = jnp.transpose(place_ref[...].astype(F32))[:, 0:1].astype(jnp.int32)
    line = iota((ARR, 1), 0)
    scatter = jnp.concatenate(
        [
            (
                jnp.where((line_turn(line) == turn) & (line_half(line) == half), place_col, -1)
                == iota((ARR, HALF), 1)
            ).astype(BF16)
            for turn in range(2)
            for half in range(HALVES)
        ],
        axis=1,
    )
    for p in range(PAIRS):
        source = jnp.concatenate(
            [os[turn, half * PAIRS + p] for turn in range(2) for half in range(HALVES)], axis=0
        )
        out_ref[:, p * 2 * HD : (p + 1) * 2 * HD] = dot(scatter, source).astype(BF16)
    source = jnp.concatenate([ls[0], ls[0], ls[1], ls[1]], axis=0)
    out_ref[:, PART:] = dot(scatter, source).astype(BF16)


def finish_prefix(rows, place, state, last, everything):
    vmem = pl.BlockSpec(memory_space=pltpu.VMEM)
    return pl.pallas_call(
        last_kernel,
        out_shape=jax.ShapeDtypeStruct((ARR, PART + HD), BF16),
        in_specs=[vmem] * 5 + [pl.BlockSpec(memory_space=pl.ANY)] * 4,
        scratch_shapes=[
            pltpu.VMEM((2, GROUP // 2, HALF, 2 * HD), BF16),
            pltpu.VMEM((2, HALF, HD), BF16),
            pltpu.VMEM((2, BLOCK, HD), BF16),
            pltpu.SemaphoreType.DMA((1,)),
        ],
        compiler_params=pltpu.CompilerParams(vmem_limit_bytes=36 * MB),
        cost_estimate=pl.CostEstimate(
            flops=6 * 10**9, bytes_accessed=8 * MB, transcendentals=0
        ),
        name="finish_prefix",
    )(rows, place, *state, *last, *everything)


def merge_kernel(at_ref, back_ref, so_ref, sl_ref, out_ref):
    picked = KVH * 4 * ROWS
    line = iota((picked, ARR), 1)
    first = dot((at_ref[...] == line).astype(BF16), back_ref[...])
    second = dot((at_ref[...] + SLOTS == line).astype(BF16), back_ref[:, :PART])
    spread = (
        (iota((HD, WIDE), 0) % GROUP == iota((HD, WIDE), 1) // HD)
        & (iota((HD, WIDE), 0) < 3 * GROUP)
    ).astype(BF16)
    lse = dot(first[:, PART:].astype(BF16), spread)
    for h in range(KVH):
        cut = slice(h * WIDE, (h + 1) * WIDE)
        rows = [slice((h * 4 + j) * ROWS, (h * 4 + j + 1) * ROWS) for j in range(4)]
        parts = [
            (lse[r], jnp.concatenate([first[r, :PART], second[r]], axis=1)) for r in rows
        ]
        parts.append((sl_ref[:, cut], so_ref[:, cut]))
        top = functools.reduce(jnp.maximum, [p[0] for p in parts])
        weights = [jnp.exp(p[0] - top) for p in parts]
        total = functools.reduce(jnp.add, weights)
        acc = functools.reduce(jnp.add, [w * p[1] for w, p in zip(weights, parts)])
        out_ref[:, cut] = (acc / total).astype(BF16)


def merge(prompt_ids, back, so, sl):
    prompt = prompt_ids[:, 0]
    earlier = jnp.arange(ROWS)[None, :] < jnp.arange(ROWS)[:, None]
    rank = jnp.sum(((prompt[:, None] == prompt[None, :]) & earlier).astype(jnp.int32), axis=1)
    h = jnp.arange(KVH)[:, None, None]
    j = jnp.arange(4)[None, :, None]
    c = h // 4
    z = jnp.where(c == 0, h, j)
    y = jnp.where(c == 0, j, h - 4)
    place = (prompt % 2 != c).astype(jnp.int32) * CAP + rank
    at = device_number(prompt // 2, c, z, y) * LINES + place
    return pl.pallas_call(
        merge_kernel,
        out_shape=jax.ShapeDtypeStruct((ROWS, KVH * WIDE), BF16),
        compiler_params=pltpu.CompilerParams(vmem_limit_bytes=16 * MB),
        name="merge",
    )(at.reshape(-1, 1), back, so, sl)


def exchange(array):
    width = array.shape[1]
    moved = lax.all_to_all(
        array.reshape(DEVS, LINES, width), AXES, split_axis=0, concat_axis=0, tiled=True
    )
    return moved.reshape(ARR, width)


def body(queries, prompt_ids, suffix_len, page_table, suffix_pool, prefix_kv):
    c = lax.axis_index("pre") % NC
    z = lax.axis_index("row") // NY
    y = lax.axis_index("row") % NY
    heads = jnp.stack(
        [
            jnp.where(c ^ cross == 0, (z + k) % NZ, NZ + (y + k) % NY)
            for cross in range(2)
            for k in range(4)
        ]
    ).astype(jnp.int32)
    sends = fill_sends(prompt_ids, queries)
    sends, heads = lax.optimization_barrier((sends, heads))
    arrived = exchange(sends)
    *own, other = split_heads(heads, prefix_kv)
    other = lax.ppermute(other, AXES, routes(None))
    pairs = pair_up(own, other)
    arrived, first = lax.optimization_barrier((arrived, pairs[0]))
    kv = [first] + [None] * 3
    kv[1] = lax.ppermute(pairs[1], AXES, routes(1))
    kv[3] = lax.ppermute(pairs[3], AXES, routes(3))
    rows, place = gather_rows(arrived)
    place, late = lax.optimization_barrier((place, pairs[2]))
    kv[2] = lax.ppermute(late, AXES, routes(2))
    state = add_sums(rows, place, kv[0:1], ())
    state = add_sums(rows, place, [kv[1], kv[3]], state)
    parts = finish_prefix(rows, place, state, kv[2:3], kv)
    parts, queries = lax.optimization_barrier((parts, queries))
    so, sl = suffix(page_table, suffix_len, queries, suffix_pool)
    return merge(prompt_ids, exchange(parts), so, sl)


def solution(mesh):
    return jax.shard_map(
        body,
        mesh=mesh,
        in_specs=(
            P(("pre", "row"), None),
            P(("pre", "row"), None),
            P(("pre", "row")),
            P(("pre", "row"), None),
            P(("pre", "row"), None, None),
            P("pre", "row", None),
        ),
        out_specs=P(("pre", "row"), None),
        check_vma=False,
    )
```

```python
import functools
import math

import jax
import jax.numpy as jnp
from jax import lax
from jax.experimental import pallas as pl
from jax.experimental.pallas import tpu as pltpu
from jax.sharding import PartitionSpec as P

KVH = 8
HD = 128
CAP = 2
GROUP = 12
ROWS = 8
WIDE = GROUP * HD
KVW = KVH * HD
NX, NC, NZ, NY = 4, 2, 4, 4
DEVS = NX * NC * NZ * NY
BLOCK = 1024
PAGE = 16
MAXP = 16
SPAN = PAGE * MAXP
SLOTS = 2 * CAP
HALVES = 2
PER_HALF = GROUP // HALVES
PAIRS = PER_HALF // 2
PART = PER_HALF * HD
LINES = HALVES * SLOTS
ARR = DEVS * LINES
HALF = DEVS * CAP
TILE = 128
STRIPS = 6
EMPTY = 256.0
SCALE = 1.0 / math.sqrt(HD)
FACTOR = SCALE / math.log(2.0)
LEAST = 1e-26
MOST = 1e30
AXES = ("pre", "row")
MB = 1 << 20
F32 = jnp.float32
BF16 = jnp.bfloat16


def dot(a, b):
    return jnp.dot(a, b, preferred_element_type=F32)


def dot_t(a, b):
    return lax.dot_general(a, b, (((1,), (1,)), ((), ())), preferred_element_type=F32)


def iota(shape, dim):
    return lax.broadcasted_iota(jnp.int32, shape, dim)


def device_number(x, c, z, y):
    return ((x * NC + c) * NZ + z) * NY + y


def routes(k, cross):
    pairs = []
    for x in range(NX):
        for c in range(NC):
            for z in range(NZ):
                for y in range(NY):
                    if (c ^ cross) == 0:
                        to = device_number(x, 0, (z + k) % NZ, y)
                    else:
                        to = device_number(x, 1, z, (y + k) % NY)
                    pairs.append((device_number(x, c, z, y), to))
    return pairs


def split_heads_kernel(head_ref, kv_ref, *refs):
    outs, (held, sems) = refs[:-2], refs[-2:]
    inward, outward = [], []
    for i, out in enumerate(outs):
        for part in range(2):
            start = pl.multiple_of(part * KVW + head_ref[i] * HD, HD)
            inward.append(
                pltpu.make_async_copy(
                    kv_ref.at[0, :, pl.ds(start, HD)], held.at[i, part], sems.at[0, i, part]
                )
            )
            outward.append(
                pltpu.make_async_copy(held.at[i, part], out.at[part], sems.at[1, i, part])
            )
    for copy in inward:
        copy.start()
    for copy, onward in zip(inward, outward):
        copy.wait()
        onward.start()
    for copy in outward:
        copy.wait()


def split_heads(heads, prefix_kv):
    n = heads.shape[0]
    return pl.pallas_call(
        split_heads_kernel,
        out_shape=[jax.ShapeDtypeStruct((2, BLOCK, HD), BF16)] * n,
        in_specs=[pl.BlockSpec(memory_space=pltpu.SMEM), pl.BlockSpec(memory_space=pltpu.HBM)],
        out_specs=[pl.BlockSpec(memory_space=pltpu.HBM)] * n,
        scratch_shapes=[
            pltpu.VMEM((n, 2, BLOCK, HD), BF16),
            pltpu.SemaphoreType.DMA((2, n, 2)),
        ],
        compiler_params=pltpu.CompilerParams(vmem_limit_bytes=8 * MB),
        name="split_heads",
    )(heads, prefix_kv)


def send_kernel(prompt_ref, q_ref, out_ref):
    wide = HALVES * NY * ROWS
    lane = iota((1, wide), 1) % ROWS
    slot = jnp.zeros((1, wide), jnp.int32)
    for i in range(ROWS):
        rank = sum((prompt_ref[j] == prompt_ref[i]).astype(jnp.int32) for j in range(i))
        slot = jnp.where(lane == i, prompt_ref[i] * CAP + rank, slot)
    unit = NY * LINES
    rows = NX * unit
    r = iota((rows, wide), 0)
    lane = iota((rows, wide), 1)
    base = r // unit * SLOTS
    half_fits = r // SLOTS % HALVES == lane // ROWS % HALVES
    first = (base + r % SLOTS == slot) & half_fits & (lane < HALVES * ROWS)
    second = (
        (base + (r + CAP) % SLOTS == slot)
        & half_fits
        & (r // LINES % NY == lane // (HALVES * ROWS))
    )
    first = first.astype(F32)
    second = second.astype(F32)
    empty_first = (1.0 - jnp.sum(first, axis=1, keepdims=True)) * EMPTY
    empty_second = (1.0 - jnp.sum(second, axis=1, keepdims=True)) * EMPTY
    first = first[:, : HALVES * ROWS].astype(BF16)
    second = second.astype(BF16)

    def stacked(heads):
        return jnp.concatenate(
            [
                q_ref[:, h * WIDE + half * PART : h * WIDE + (half + 1) * PART].astype(F32)
                for h in heads
                for half in range(HALVES)
            ],
            axis=0,
        ).astype(BF16)

    for z in range(NZ):
        piece = (dot(first, stacked([z])) + empty_first).astype(BF16)
        for x in range(NX):
            at = device_number(x, 0, z, 0) * LINES
            out_ref[at : at + unit, :] = piece[x * unit : (x + 1) * unit]
    piece = dot(second, stacked([NZ + y for y in range(NY)])) + empty_second
    piece = piece.astype(BF16)
    for x in range(NX):
        for z in range(NZ):
            at = device_number(x, 1, z, 0) * LINES
            out_ref[at : at + unit, :] = piece[x * unit : (x + 1) * unit]


def fill_sends(prompt_ids, queries):
    return pl.pallas_call(
        send_kernel,
        out_shape=jax.ShapeDtypeStruct((ARR, PART), BF16),
        in_specs=[
            pl.BlockSpec(memory_space=pltpu.SMEM),
            pl.BlockSpec(memory_space=pltpu.VMEM),
        ],
        compiler_params=pltpu.CompilerParams(vmem_limit_bytes=60 * MB),
        name="fill_sends",
    )(prompt_ids[:, 0], queries)


def suffix_kernel(table_ref, len_ref, q_ref, pool_ref, out_ref, lse_ref, kv, sems):
    for row in range(ROWS):
        for p in range(MAXP):
            pltpu.make_async_copy(
                pool_ref.at[table_ref[row, p]],
                kv.at[row, pl.ds(p * PAGE, PAGE), :],
                sems.at[row],
            ).start()

    def one(row, carry):
        pltpu.make_async_copy(kv.at[row], kv.at[row], sems.at[row]).wait()
        scores = jnp.concatenate(
            [
                dot_t(q_ref[row, h], kv[row, :, h * HD : (h + 1) * HD])
                for h in range(KVH)
            ],
            axis=0,
        )
        in_range = iota((KVH * 16, SPAN), 1) < len_ref[row]
        scores = jnp.where(in_range, scores * SCALE, -1e30)
        top = jnp.max(scores, axis=1, keepdims=True)
        weights = jnp.where(in_range, jnp.exp(scores - top), 0.0)
        total = jnp.sum(weights, axis=1, keepdims=True)
        scale = 1.0 / total
        lse = top + jnp.log(total)
        weights = weights.astype(BF16)
        for h in range(KVH):
            cut = slice(h * 16, (h + 1) * 16)
            values = kv[row, :, KVW + h * HD : KVW + (h + 1) * HD]
            out_ref[row, h] = dot(weights[cut], values) * scale[cut]
            lse_ref[row, h] = jnp.broadcast_to(lse[cut], (16, HD))
        return carry

    lax.fori_loop(0, ROWS, one, 0)


def suffix(page_table, suffix_len, queries, suffix_pool):
    q = queries.reshape(ROWS, KVH, GROUP, HD)
    q = jnp.pad(q, ((0, 0), (0, 0), (0, 16 - GROUP), (0, 0)))
    smem = pl.BlockSpec(memory_space=pltpu.SMEM)
    vmem = pl.BlockSpec(memory_space=pltpu.VMEM)
    shape = jax.ShapeDtypeStruct((ROWS, KVH, 16, HD), F32)
    out, lse = pl.pallas_call(
        suffix_kernel,
        out_shape=[shape, shape],
        in_specs=[smem, smem, vmem, pl.BlockSpec(memory_space=pl.ANY)],
        out_specs=[vmem, vmem],
        scratch_shapes=[
            pltpu.VMEM((ROWS, SPAN, 2 * KVW), BF16),
            pltpu.SemaphoreType.DMA((ROWS,)),
        ],
        compiler_params=pltpu.CompilerParams(vmem_limit_bytes=56 * MB),
        cost_estimate=pl.CostEstimate(
            flops=10**9, bytes_accessed=9 * MB, transcendentals=0
        ),
        name="suffix",
    )(page_table, suffix_len, q, suffix_pool)
    return (
        out[:, :, :GROUP].reshape(ROWS, KVH * WIDE),
        lse[:, :, :GROUP].reshape(ROWS, KVH * WIDE),
    )


def line_turn(line):
    return line // CAP % 2


def line_half(line):
    return line // SLOTS % HALVES


def gather_kernel(x_ref, q_ref, place_ref):
    pick = (iota((8, HD), 1) == 0).astype(BF16)
    held = dot_t(pick, x_ref[:, :HD]) < EMPTY / 2
    a, b = iota((ARR, ARR), 0), iota((ARR, ARR), 1)
    before = (a <= b) & (((a ^ b) & (LINES - CAP)) == 0)
    place = dot(held.astype(BF16), before.astype(BF16)).astype(jnp.int32) - 1
    place = jnp.where(held, place, -1)
    place_ref[...] = place
    line = iota((1, ARR), 1)
    for turn in range(2):
        for half in range(HALVES):
            mine = (line_turn(line) == turn) & (line_half(line) == half)
            row = jnp.where(mine, place[0:1], -1)
            gather = (row == iota((HALF, ARR), 0)).astype(BF16)
            for p in range(PAIRS):
                two = dot(gather, x_ref[:, p * 2 * HD : (p + 1) * 2 * HD]).astype(BF16)
                q_ref[turn, half * PER_HALF + 2 * p] = two[:, :HD]
                q_ref[turn, half * PER_HALF + 2 * p + 1] = two[:, HD:]


def gather_rows(arrived):
    return pl.pallas_call(
        gather_kernel,
        out_shape=[
            jax.ShapeDtypeStruct((2, GROUP, HALF, HD), BF16),
            jax.ShapeDtypeStruct((8, ARR), jnp.int32),
        ],
        compiler_params=pltpu.CompilerParams(vmem_limit_bytes=16 * MB),
        name="gather_rows",
    )(arrived)


def row_counts(place_ref):
    line = iota((1, ARR), 1)
    return [
        jnp.max(jnp.where(line_turn(line) == turn, place_ref[0:1], -1)) + 1
        for turn in range(2)
    ]


def widen(column):
    column = column.reshape(GROUP, TILE, 1)
    lane = iota((TILE, HD), 1)
    wide = jnp.zeros((TILE, HD), F32)
    for g in range(GROUP):
        mine = (lane == g) | (lane == g + GROUP) | (lane == g + 2 * GROUP)
        wide = wide + jnp.where(mine, column[g], 0.0)
    return wide


def plain_part(q, keys, values):
    strip = GROUP * TILE // STRIPS
    outs, totals = [], []
    for i in range(STRIPS):
        score = dot_t(q[i * strip : (i + 1) * strip], keys)
        weights = jnp.exp2(score * FACTOR)
        cuts = [weights[:, c : c + HD] for c in range(0, weights.shape[1], HD)]
        totals.append(jnp.sum(functools.reduce(jnp.add, cuts), axis=1, keepdims=True))
        outs.append(dot(weights.astype(BF16), values))
    out = jnp.concatenate(outs, axis=0).reshape(GROUP, TILE, HD)
    return out, widen(jnp.concatenate(totals, axis=0))


def tile_part(q_ref, kv_refs, turn, at):
    q = q_ref[turn, :, pl.ds(at, TILE), :].reshape(GROUP * TILE, HD)
    mine = kv_refs[turn::2]
    keys = jnp.concatenate([ref[0] for ref in mine], axis=0)
    values = jnp.concatenate([ref[1] for ref in mine], axis=0)
    return plain_part(q, keys, values)


def over_tiles(count, step):
    def tile(t, carry):
        step(pl.multiple_of(t * TILE, TILE))
        return carry

    lax.fori_loop(0, (count + TILE - 1) // TILE, tile, 0)


def sums_kernel(blocks, first, q_ref, place_ref, *refs):
    kv_refs, refs = refs[: 2 * blocks], refs[2 * blocks :]
    out_ref, total_ref = refs[-2:]
    for turn, count in enumerate(row_counts(place_ref)):

        def step(at, turn=turn):
            out, total = tile_part(q_ref, kv_refs, turn, at)
            if not first:
                out = out + refs[0][turn, :, pl.ds(at, TILE), :]
                total = total + refs[1][turn, pl.ds(at, TILE), :]
            out_ref[turn, :, pl.ds(at, TILE), :] = out
            total_ref[turn, pl.ds(at, TILE), :] = total

        over_tiles(count, step)


def add_sums(rows, place, kv, state):
    blocks = len(kv) // 2
    vmem = pl.BlockSpec(memory_space=pltpu.VMEM)
    return pl.pallas_call(
        functools.partial(sums_kernel, blocks, not state),
        out_shape=[
            jax.ShapeDtypeStruct((2, GROUP, HALF, HD), F32),
            jax.ShapeDtypeStruct((2, HALF, HD), F32),
        ],
        in_specs=[vmem] * (2 + len(kv) + len(state)),
        out_specs=[vmem, vmem],
        compiler_params=pltpu.CompilerParams(vmem_limit_bytes=16 * MB),
        cost_estimate=pl.CostEstimate(
            flops=blocks * 4 * 10**9, bytes_accessed=8 * MB, transcendentals=0
        ),
        name="sums_%d" % blocks,
    )(rows, place, *kv, *state)


def last_kernel(q_ref, place_ref, sum_ref, total_ref, *refs):
    kv_refs, all_refs, (out_ref, os, ls, held, sems) = refs[:2], refs[2:10], refs[10:]
    for turn in range(2):
        os[turn] = jnp.zeros((GROUP // 2, HALF, 2 * HD), BF16)
        ls[turn] = jnp.zeros((HALF, HD), BF16)
    lane = iota((TILE, HD), 1)

    def finish(turn, at, out, total, shift):
        for g in range(GROUP):
            os[turn, g // 2, pl.ds(at, TILE), g % 2 * HD : (g % 2 + 1) * HD] = (
                out[g] / total[:, g : g + 1]
            ).astype(BF16)
        lse = jnp.where(lane < 3 * GROUP, shift + jnp.log(total), 0.0)
        one = lse.astype(BF16).astype(F32)
        two = (lse - one).astype(BF16).astype(F32)
        three = lse - one - two
        split = jnp.where(lane < GROUP, one, jnp.where(lane < 2 * GROUP, two, three))
        ls[turn, pl.ds(at, TILE), :] = split.astype(BF16)

    for turn, count in enumerate(row_counts(place_ref)):

        def step(at, turn=turn):
            out, total = tile_part(q_ref, kv_refs, turn, at)
            out = out + sum_ref[turn, :, pl.ds(at, TILE), :]
            total = total + total_ref[turn, pl.ds(at, TILE), :]
            finish(turn, at, out, total, 0.0)
            known = jnp.where(lane < 3 * GROUP, total, 1.0)
            plain = (jnp.min(known) > LEAST) & (jnp.max(known) < MOST)

            @pl.when(jnp.logical_not(plain))
            def _():
                q = q_ref[turn, :, pl.ds(at, TILE), :].reshape(GROUP * TILE, HD)
                top = amount = acc = None
                for k in range(4):
                    copy = pltpu.make_async_copy(all_refs[k * 2 + turn], held, sems.at[0])
                    copy.start()
                    copy.wait()
                    score = dot_t(q, held[0])
                    high = jnp.max(score, axis=1, keepdims=True)
                    if k > 0:
                        high = jnp.maximum(top, high)
                    weights = jnp.exp2(score * FACTOR - high * FACTOR)
                    part_amount = jnp.sum(weights, axis=1, keepdims=True)
                    part = dot(weights.astype(BF16), held[1])
                    if k > 0:
                        fade = jnp.exp2((top - high) * FACTOR)
                        part = acc * fade + part
                        part_amount = amount * fade + part_amount
                    top, amount, acc = high, part_amount, part
                acc = acc.reshape(GROUP, TILE, HD)
                finish(turn, at, acc, widen(amount), widen(top * SCALE))

        over_tiles(count, step)

    place_col = jnp.transpose(place_ref[...].astype(F32))[:, 0:1].astype(jnp.int32)
    line = iota((ARR, 1), 0)
    scatter = jnp.concatenate(
        [
            (
                jnp.where((line_turn(line) == turn) & (line_half(line) == half), place_col, -1)
                == iota((ARR, HALF), 1)
            ).astype(BF16)
            for turn in range(2)
            for half in range(HALVES)
        ],
        axis=1,
    )
    for p in range(PAIRS):
        source = jnp.concatenate(
            [os[turn, half * PAIRS + p] for turn in range(2) for half in range(HALVES)], axis=0
        )
        out_ref[:, p * 2 * HD : (p + 1) * 2 * HD] = dot(scatter, source).astype(BF16)
    source = jnp.concatenate([ls[0], ls[0], ls[1], ls[1]], axis=0)
    out_ref[:, PART:] = dot(scatter, source).astype(BF16)


def finish_prefix(rows, place, state, last, everything):
    vmem = pl.BlockSpec(memory_space=pltpu.VMEM)
    return pl.pallas_call(
        last_kernel,
        out_shape=jax.ShapeDtypeStruct((ARR, PART + HD), BF16),
        in_specs=[vmem] * 6 + [pl.BlockSpec(memory_space=pl.ANY)] * 8,
        scratch_shapes=[
            pltpu.VMEM((2, GROUP // 2, HALF, 2 * HD), BF16),
            pltpu.VMEM((2, HALF, HD), BF16),
            pltpu.VMEM((2, BLOCK, HD), BF16),
            pltpu.SemaphoreType.DMA((1,)),
        ],
        compiler_params=pltpu.CompilerParams(vmem_limit_bytes=48 * MB),
        cost_estimate=pl.CostEstimate(
            flops=6 * 10**9, bytes_accessed=8 * MB, transcendentals=0
        ),
        name="finish_prefix",
    )(rows, place, *state, *last, *everything)


def merge_kernel(at_ref, back_ref, so_ref, sl_ref, out_ref):
    picked = KVH * 4 * ROWS
    line = iota((picked, ARR), 1)
    first = dot((at_ref[...] == line).astype(BF16), back_ref[...])
    second = dot((at_ref[...] + SLOTS == line).astype(BF16), back_ref[:, :PART])
    spread = (
        (iota((HD, WIDE), 0) % GROUP == iota((HD, WIDE), 1) // HD)
        & (iota((HD, WIDE), 0) < 3 * GROUP)
    ).astype(BF16)
    lse = dot(first[:, PART:].astype(BF16), spread)
    for h in range(KVH):
        cut = slice(h * WIDE, (h + 1) * WIDE)
        rows = [slice((h * 4 + j) * ROWS, (h * 4 + j + 1) * ROWS) for j in range(4)]
        parts = [
            (lse[r], jnp.concatenate([first[r, :PART], second[r]], axis=1)) for r in rows
        ]
        parts.append((sl_ref[:, cut], so_ref[:, cut]))
        top = functools.reduce(jnp.maximum, [p[0] for p in parts])
        weights = [jnp.exp(p[0] - top) for p in parts]
        total = functools.reduce(jnp.add, weights)
        acc = functools.reduce(jnp.add, [w * p[1] for w, p in zip(weights, parts)])
        out_ref[:, cut] = (acc / total).astype(BF16)


def merge(prompt_ids, back, so, sl):
    prompt = prompt_ids[:, 0]
    earlier = jnp.arange(ROWS)[None, :] < jnp.arange(ROWS)[:, None]
    rank = jnp.sum(((prompt[:, None] == prompt[None, :]) & earlier).astype(jnp.int32), axis=1)
    h = jnp.arange(KVH)[:, None, None]
    j = jnp.arange(4)[None, :, None]
    c = h // 4
    z = jnp.where(c == 0, h, j)
    y = jnp.where(c == 0, j, h - 4)
    place = (prompt % 2 != c).astype(jnp.int32) * CAP + rank
    at = device_number(prompt // 2, c, z, y) * LINES + place
    return pl.pallas_call(
        merge_kernel,
        out_shape=jax.ShapeDtypeStruct((ROWS, KVH * WIDE), BF16),
        compiler_params=pltpu.CompilerParams(vmem_limit_bytes=16 * MB),
        name="merge",
    )(at.reshape(-1, 1), back, so, sl)


def exchange(array):
    width = array.shape[1]
    moved = lax.all_to_all(
        array.reshape(DEVS, LINES, width), AXES, split_axis=0, concat_axis=0, tiled=True
    )
    return moved.reshape(ARR, width)


def body(queries, prompt_ids, suffix_len, page_table, suffix_pool, prefix_kv):
    c = lax.axis_index("pre") % NC
    z = lax.axis_index("row") // NY
    y = lax.axis_index("row") % NY
    heads = jnp.stack(
        [
            jnp.where(c ^ cross == 0, (z + k) % NZ, NZ + (y + k) % NY)
            for k in range(4)
            for cross in range(2)
        ]
    ).astype(jnp.int32)
    sends = fill_sends(prompt_ids, queries)
    sends, heads = lax.optimization_barrier((sends, heads))
    arrived = exchange(sends)
    pieces = split_heads(heads, prefix_kv)

    def move(n, piece):
        return lax.ppermute(piece, AXES, routes(n // 2, n % 2))

    kv = list(pieces)
    for n in (1, 2, 3, 6, 7):
        kv[n] = move(n, pieces[n])
    kv[1], later = lax.optimization_barrier((kv[1], pieces[4]))
    kv[4] = move(4, later)
    arrived, kv[1] = lax.optimization_barrier((arrived, kv[1]))
    rows, place = gather_rows(arrived)
    place, kv[2], later = lax.optimization_barrier((place, kv[2], pieces[5]))
    kv[5] = move(5, later)
    state = add_sums(rows, place, kv[0:2], ())
    state, kv[3], kv[6], kv[7] = lax.optimization_barrier((state, kv[3], kv[6], kv[7]))
    state = add_sums(rows, place, kv[2:4] + kv[6:8], state)
    parts = finish_prefix(rows, place, state, kv[4:6], kv)
    parts, queries = lax.optimization_barrier((parts, queries))
    so, sl = suffix(page_table, suffix_len, queries, suffix_pool)
    return merge(prompt_ids, exchange(parts), so, sl)


def solution(mesh):
    return jax.shard_map(
        body,
        mesh=mesh,
        in_specs=(
            P(("pre", "row"), None),
            P(("pre", "row"), None),
            P(("pre", "row")),
            P(("pre", "row"), None),
            P(("pre", "row"), None, None),
            P("pre", "row", None),
        ),
        out_specs=P(("pre", "row"), None),
        check_vma=False,
    )
```

```python
import functools
import math

import jax
import jax.numpy as jnp
from jax import lax
from jax.experimental import pallas as pl
from jax.experimental.pallas import tpu as pltpu
from jax.sharding import PartitionSpec as P

KVH = 8
HD = 128
CAP = 2
GROUP = 12
ROWS = 8
WIDE = GROUP * HD
KVW = KVH * HD
NX, NC, NZ, NY = 4, 2, 4, 4
DEVS = NX * NC * NZ * NY
BLOCK = 1024
PAGE = 16
MAXP = 16
SPAN = PAGE * MAXP
SLOTS = 2 * CAP
HALVES = 2
PER_HALF = GROUP // HALVES
PAIRS = PER_HALF // 2
PART = PER_HALF * HD
LINES = HALVES * SLOTS
ARR = DEVS * LINES
HALF = DEVS * CAP
TILE = 128
UNROLL = 3
EMPTY = 256.0
SCALE = 1.0 / math.sqrt(HD)
FACTOR = SCALE / math.log(2.0)
LEAST = 1e-26
MOST = 1e30
AXES = ("pre", "row")
MB = 1 << 20
F32 = jnp.float32
BF16 = jnp.bfloat16


def dot(a, b):
    return jnp.dot(a, b, preferred_element_type=F32)


def dot_t(a, b):
    return lax.dot_general(a, b, (((1,), (1,)), ((), ())), preferred_element_type=F32)


def iota(shape, dim):
    return lax.broadcasted_iota(jnp.int32, shape, dim)


def device_number(x, c, z, y):
    return ((x * NC + c) * NZ + z) * NY + y


def routes(k, cross):
    pairs = []
    for x in range(NX):
        for c in range(NC):
            for z in range(NZ):
                for y in range(NY):
                    if (c ^ cross) == 0:
                        to = device_number(x, 0, (z + k) % NZ, y)
                    else:
                        to = device_number(x, 1, z, (y + k) % NY)
                    pairs.append((device_number(x, c, z, y), to))
    return pairs


def split_heads_kernel(head_ref, kv_ref, *refs):
    outs, (held, sems) = refs[:-2], refs[-2:]
    inward, outward = [], []
    for i, out in enumerate(outs):
        for part in range(2):
            start = pl.multiple_of(part * KVW + head_ref[i] * HD, HD)
            inward.append(
                pltpu.make_async_copy(
                    kv_ref.at[0, :, pl.ds(start, HD)], held.at[i, part], sems.at[0, i, part]
                )
            )
            outward.append(
                pltpu.make_async_copy(held.at[i, part], out.at[part], sems.at[1, i, part])
            )
    for copy in inward:
        copy.start()
    for copy, onward in zip(inward, outward):
        copy.wait()
        onward.start()
    for copy in outward:
        copy.wait()


def split_heads(heads, prefix_kv):
    n = heads.shape[0]
    return pl.pallas_call(
        split_heads_kernel,
        out_shape=[jax.ShapeDtypeStruct((2, BLOCK, HD), BF16)] * n,
        in_specs=[pl.BlockSpec(memory_space=pltpu.SMEM), pl.BlockSpec(memory_space=pltpu.HBM)],
        out_specs=[pl.BlockSpec(memory_space=pltpu.HBM)] * n,
        scratch_shapes=[
            pltpu.VMEM((n, 2, BLOCK, HD), BF16),
            pltpu.SemaphoreType.DMA((2, n, 2)),
        ],
        compiler_params=pltpu.CompilerParams(vmem_limit_bytes=8 * MB),
        name="split_heads",
    )(heads, prefix_kv)


def send_kernel(prompt_ref, q_ref, out_ref):
    wide = HALVES * NY * ROWS
    lane = iota((1, wide), 1) % ROWS
    slot = jnp.zeros((1, wide), jnp.int32)
    for i in range(ROWS):
        rank = sum((prompt_ref[j] == prompt_ref[i]).astype(jnp.int32) for j in range(i))
        slot = jnp.where(lane == i, prompt_ref[i] * CAP + rank, slot)
    unit = NY * LINES
    rows = NX * unit
    r = iota((rows, wide), 0)
    lane = iota((rows, wide), 1)
    base = r // unit * SLOTS
    half_fits = r // SLOTS % HALVES == lane // ROWS % HALVES
    first = (base + r % SLOTS == slot) & half_fits & (lane < HALVES * ROWS)
    second = (
        (base + (r + CAP) % SLOTS == slot)
        & half_fits
        & (r // LINES % NY == lane // (HALVES * ROWS))
    )
    first = first.astype(F32)
    second = second.astype(F32)
    empty_first = (1.0 - jnp.sum(first, axis=1, keepdims=True)) * EMPTY
    empty_second = (1.0 - jnp.sum(second, axis=1, keepdims=True)) * EMPTY
    first = first[:, : HALVES * ROWS].astype(BF16)
    second = second.astype(BF16)

    def stacked(heads):
        return jnp.concatenate(
            [
                q_ref[:, h * WIDE + half * PART : h * WIDE + (half + 1) * PART].astype(F32)
                for h in heads
                for half in range(HALVES)
            ],
            axis=0,
        ).astype(BF16)

    for z in range(NZ):
        piece = (dot(first, stacked([z])) + empty_first).astype(BF16)
        for x in range(NX):
            at = device_number(x, 0, z, 0) * LINES
            out_ref[at : at + unit, :] = piece[x * unit : (x + 1) * unit]
    piece = dot(second, stacked([NZ + y for y in range(NY)])) + empty_second
    piece = piece.astype(BF16)
    for x in range(NX):
        for z in range(NZ):
            at = device_number(x, 1, z, 0) * LINES
            out_ref[at : at + unit, :] = piece[x * unit : (x + 1) * unit]


def fill_sends(prompt_ids, queries):
    return pl.pallas_call(
        send_kernel,
        out_shape=jax.ShapeDtypeStruct((ARR, PART), BF16),
        in_specs=[
            pl.BlockSpec(memory_space=pltpu.SMEM),
            pl.BlockSpec(memory_space=pltpu.VMEM),
        ],
        compiler_params=pltpu.CompilerParams(vmem_limit_bytes=60 * MB),
        name="fill_sends",
    )(prompt_ids[:, 0], queries)


def suffix_kernel(table_ref, len_ref, q_ref, pool_ref, out_ref, lse_ref, kv, sems):
    for row in range(ROWS):
        for p in range(MAXP):
            pltpu.make_async_copy(
                pool_ref.at[table_ref[row, p]],
                kv.at[row, pl.ds(p * PAGE, PAGE), :],
                sems.at[row],
            ).start()

    def one(row, carry):
        pltpu.make_async_copy(kv.at[row], kv.at[row], sems.at[row]).wait()
        scores = jnp.concatenate(
            [
                dot_t(q_ref[row, h], kv[row, :, h * HD : (h + 1) * HD])
                for h in range(KVH)
            ],
            axis=0,
        )
        in_range = iota((KVH * 16, SPAN), 1) < len_ref[row]
        scores = jnp.where(in_range, scores * SCALE, -1e30)
        top = jnp.max(scores, axis=1, keepdims=True)
        weights = jnp.where(in_range, jnp.exp(scores - top), 0.0)
        total = jnp.sum(weights, axis=1, keepdims=True)
        scale = 1.0 / total
        lse = top + jnp.log(total)
        weights = weights.astype(BF16)
        for h in range(KVH):
            cut = slice(h * 16, (h + 1) * 16)
            values = kv[row, :, KVW + h * HD : KVW + (h + 1) * HD]
            out_ref[row, h] = dot(weights[cut], values) * scale[cut]
            lse_ref[row, h] = jnp.broadcast_to(lse[cut], (16, HD))
        return carry

    lax.fori_loop(0, ROWS, one, 0)


def suffix(page_table, suffix_len, queries, suffix_pool):
    q = queries.reshape(ROWS, KVH, GROUP, HD)
    q = jnp.pad(q, ((0, 0), (0, 0), (0, 16 - GROUP), (0, 0)))
    smem = pl.BlockSpec(memory_space=pltpu.SMEM)
    vmem = pl.BlockSpec(memory_space=pltpu.VMEM)
    shape = jax.ShapeDtypeStruct((ROWS, KVH, 16, HD), F32)
    out, lse = pl.pallas_call(
        suffix_kernel,
        out_shape=[shape, shape],
        in_specs=[smem, smem, vmem, pl.BlockSpec(memory_space=pl.ANY)],
        out_specs=[vmem, vmem],
        scratch_shapes=[
            pltpu.VMEM((ROWS, SPAN, 2 * KVW), BF16),
            pltpu.SemaphoreType.DMA((ROWS,)),
        ],
        compiler_params=pltpu.CompilerParams(vmem_limit_bytes=56 * MB),
        cost_estimate=pl.CostEstimate(
            flops=10**9, bytes_accessed=9 * MB, transcendentals=0
        ),
        name="suffix",
    )(page_table, suffix_len, q, suffix_pool)
    return (
        out[:, :, :GROUP].reshape(ROWS, KVH * WIDE),
        lse[:, :, :GROUP].reshape(ROWS, KVH * WIDE),
    )


def line_turn(line):
    return line // CAP % 2


def line_half(line):
    return line // SLOTS % HALVES


def gather_kernel(x_ref, q_ref, place_ref):
    pick = (iota((8, HD), 1) == 0).astype(BF16)
    held = dot_t(pick, x_ref[:, :HD]) < EMPTY / 2
    a, b = iota((ARR, ARR), 0), iota((ARR, ARR), 1)
    before = (a <= b) & (((a ^ b) & (LINES - CAP)) == 0)
    place = dot(held.astype(BF16), before.astype(BF16)).astype(jnp.int32) - 1
    place = jnp.where(held, place, -1)
    place_ref[...] = place
    line = iota((1, ARR), 1)
    for turn in range(2):
        for half in range(HALVES):
            mine = (line_turn(line) == turn) & (line_half(line) == half)
            row = jnp.where(mine, place[0:1], -1)
            gather = (row == iota((HALF, ARR), 0)).astype(BF16)
            for p in range(PAIRS):
                two = dot(gather, x_ref[:, p * 2 * HD : (p + 1) * 2 * HD]).astype(BF16)
                q_ref[turn, half * PER_HALF + 2 * p] = two[:, :HD]
                q_ref[turn, half * PER_HALF + 2 * p + 1] = two[:, HD:]


def gather_rows(arrived):
    return pl.pallas_call(
        gather_kernel,
        out_shape=[
            jax.ShapeDtypeStruct((2, GROUP, HALF, HD), BF16),
            jax.ShapeDtypeStruct((8, ARR), jnp.int32),
        ],
        compiler_params=pltpu.CompilerParams(vmem_limit_bytes=16 * MB),
        name="gather_rows",
    )(arrived)


def row_counts(place_ref):
    line = iota((1, ARR), 1)
    return [
        jnp.max(jnp.where(line_turn(line) == turn, place_ref[0:1], -1)) + 1
        for turn in range(2)
    ]


def widen(pair, column):
    lane = iota((TILE, HD), 1)
    wide = jnp.zeros((TILE, HD), F32)
    for i in range(2):
        mine = (lane % GROUP == 2 * pair + i) & (lane < 3 * GROUP)
        wide = wide + jnp.where(mine, column[i * TILE : (i + 1) * TILE], 0.0)
    return wide


def pair_rows(q_ref, turn, pair, at):
    return q_ref[turn, pl.ds(2 * pair, 2), pl.ds(at, TILE), :].reshape(2 * TILE, HD)


def plain_part(q, keys, values):
    weights = jnp.exp2(dot_t(q, keys) * FACTOR)
    cuts = [weights[:, c : c + HD] for c in range(0, weights.shape[1], HD)]
    total = jnp.sum(functools.reduce(jnp.add, cuts), axis=1, keepdims=True)
    return dot(weights.astype(BF16), values), total


def load_blocks(kv_refs, ks, vs, sems):
    copies = []
    for n, ref in enumerate(kv_refs):
        rows = pl.ds(n // 2 * BLOCK, BLOCK)
        copies.append(pltpu.make_async_copy(ref.at[0], ks.at[n % 2, rows], sems.at[n, 0]))
        copies.append(pltpu.make_async_copy(ref.at[1], vs.at[n % 2, rows], sems.at[n, 1]))
    for copy in copies:
        copy.start()
    return copies


def over_tiles(place_ref, step):
    first, second = [(count + TILE - 1) // TILE for count in row_counts(place_ref)]

    def tile(t, carry):
        turn = (t >= first).astype(jnp.int32)
        step(turn, pl.multiple_of((t - turn * first) * TILE, TILE))
        return carry

    lax.fori_loop(0, first + second, tile, 0)


def sums_kernel(blocks, first, q_ref, place_ref, *refs):
    kv_refs, refs = refs[: 2 * blocks], refs[2 * blocks :]
    out_ref, total_ref, ks, vs, sems = refs[-5:]
    for copy in load_blocks(kv_refs, ks, vs, sems):
        copy.wait()

    def step(turn, at):
        def one(pair, wide):
            q = pair_rows(q_ref, turn, pair, at)
            out, total = plain_part(q, ks[turn], vs[turn])
            out = out.reshape(2, TILE, HD)
            place = (turn, pl.ds(2 * pair, 2), pl.ds(at, TILE))
            if not first:
                out = out + refs[0][place]
            out_ref[place] = out
            return wide + widen(pair, total)

        if first:
            wide = jnp.zeros((TILE, HD), F32)
        else:
            wide = refs[1][turn, pl.ds(at, TILE), :]
        total_ref[turn, pl.ds(at, TILE), :] = lax.fori_loop(
            0, GROUP // 2, one, wide, unroll=UNROLL
        )

    over_tiles(place_ref, step)


def block_scratch(blocks):
    return [
        pltpu.VMEM((2, blocks * BLOCK, HD), BF16),
        pltpu.VMEM((2, blocks * BLOCK, HD), BF16),
        pltpu.SemaphoreType.DMA((2 * blocks, 2)),
    ]


def add_sums(rows, place, kv, state):
    blocks = len(kv) // 2
    vmem = pl.BlockSpec(memory_space=pltpu.VMEM)
    return pl.pallas_call(
        functools.partial(sums_kernel, blocks, not state),
        out_shape=[
            jax.ShapeDtypeStruct((2, GROUP, HALF, HD), F32),
            jax.ShapeDtypeStruct((2, HALF, HD), F32),
        ],
        in_specs=[vmem] * 2 + [pl.BlockSpec(memory_space=pl.ANY)] * len(kv) + [vmem] * len(state),
        out_specs=[vmem, vmem],
        scratch_shapes=block_scratch(blocks),
        compiler_params=pltpu.CompilerParams(vmem_limit_bytes=24 * MB),
        cost_estimate=pl.CostEstimate(
            flops=blocks * 4 * 10**9, bytes_accessed=8 * MB, transcendentals=0
        ),
        name="sums_%d" % blocks,
    )(rows, place, *kv, *state)


def last_kernel(q_ref, place_ref, sum_ref, total_ref, *refs):
    kv_refs, all_refs, (out_ref, os, ls, ks, vs, sems, held, held_sem) = (
        refs[:2],
        refs[2:10],
        refs[10:],
    )
    copies = load_blocks(kv_refs, ks, vs, sems)
    os[...] = jnp.zeros((2, GROUP // 2, HALF, 2 * HD), BF16)
    ls[...] = jnp.zeros((2, HALF, HD), BF16)
    for copy in copies:
        copy.wait()
    lane = iota((TILE, HD), 1)

    def keep(turn, pair, at, out, totals):
        for i in range(2):
            os[turn, pair, pl.ds(at, TILE), i * HD : (i + 1) * HD] = (
                out[i * TILE : (i + 1) * TILE] / totals[i]
            ).astype(BF16)

    def keep_lse(turn, at, total, shift):
        lse = jnp.where(lane < 3 * GROUP, shift + jnp.log(total), 0.0)
        one = lse.astype(BF16).astype(F32)
        two = (lse - one).astype(BF16).astype(F32)
        three = lse - one - two
        split = jnp.where(lane < GROUP, one, jnp.where(lane < 2 * GROUP, two, three))
        ls[turn, pl.ds(at, TILE), :] = split.astype(BF16)

    def fetch(k, turn):
        for n, ref in enumerate(all_refs):

            @pl.when(2 * k + turn == n)
            def _(ref=ref):
                copy = pltpu.make_async_copy(ref, held, held_sem.at[0])
                copy.start()
                copy.wait()

    def step(turn, at):
        before = total_ref[turn, pl.ds(at, TILE), :]

        def one(pair, wide):
            q = pair_rows(q_ref, turn, pair, at)
            out, total = plain_part(q, ks[turn], vs[turn])
            out = out + sum_ref[turn, pl.ds(2 * pair, 2), pl.ds(at, TILE), :].reshape(
                2 * TILE, HD
            )
            totals = [
                total[i * TILE : (i + 1) * TILE]
                + jnp.sum(
                    jnp.where(lane == 2 * pair + i, before, 0.0), axis=1, keepdims=True
                )
                for i in range(2)
            ]
            keep(turn, pair, at, out, totals)
            return wide + widen(pair, total)

        total = lax.fori_loop(0, GROUP // 2, one, before, unroll=UNROLL)
        keep_lse(turn, at, total, 0.0)
        known = jnp.where(lane < 3 * GROUP, total, 1.0)
        plain = (jnp.min(known) > LEAST) & (jnp.max(known) < MOST)

        @pl.when(jnp.logical_not(plain))
        def _():
            def again(pair, carry):
                q = pair_rows(q_ref, turn, pair, at)

                def block(k, state):
                    top, amount, acc = state
                    fetch(k, turn)
                    score = dot_t(q, held[0])
                    high = jnp.maximum(top, jnp.max(score, axis=1, keepdims=True))
                    weights = jnp.exp2(score * FACTOR - high * FACTOR)
                    fade = jnp.exp2((top - high) * FACTOR)
                    amount = amount * fade + jnp.sum(weights, axis=1, keepdims=True)
                    return high, amount, acc * fade + dot(weights.astype(BF16), held[1])

                top, amount, acc = lax.fori_loop(
                    0,
                    4,
                    block,
                    (
                        jnp.full((2 * TILE, 1), -1e30, F32),
                        jnp.zeros((2 * TILE, 1), F32),
                        jnp.zeros((2 * TILE, HD), F32),
                    ),
                )
                keep(turn, pair, at, acc, [amount[:TILE], amount[TILE:]])
                return carry[0] + widen(pair, amount), carry[1] + widen(pair, top * SCALE)

            empty = jnp.zeros((TILE, HD), F32)
            amount, shift = lax.fori_loop(0, GROUP // 2, again, (empty, empty))
            keep_lse(turn, at, amount, shift)

    over_tiles(place_ref, step)

    place_col = jnp.transpose(place_ref[...].astype(F32))[:, 0:1].astype(jnp.int32)
    line = iota((ARR, 1), 0)
    scatter = jnp.concatenate(
        [
            (
                jnp.where((line_turn(line) == turn) & (line_half(line) == half), place_col, -1)
                == iota((ARR, HALF), 1)
            ).astype(BF16)
            for turn in range(2)
            for half in range(HALVES)
        ],
        axis=1,
    )
    for p in range(PAIRS):
        source = jnp.concatenate(
            [os[turn, half * PAIRS + p] for turn in range(2) for half in range(HALVES)], axis=0
        )
        out_ref[:, p * 2 * HD : (p + 1) * 2 * HD] = dot(scatter, source).astype(BF16)
    source = jnp.concatenate([ls[0], ls[0], ls[1], ls[1]], axis=0)
    out_ref[:, PART:] = dot(scatter, source).astype(BF16)


def finish_prefix(rows, place, state, last, everything):
    vmem = pl.BlockSpec(memory_space=pltpu.VMEM)
    return pl.pallas_call(
        last_kernel,
        out_shape=jax.ShapeDtypeStruct((ARR, PART + HD), BF16),
        in_specs=[vmem] * 4 + [pl.BlockSpec(memory_space=pl.ANY)] * 10,
        scratch_shapes=[
            pltpu.VMEM((2, GROUP // 2, HALF, 2 * HD), BF16),
            pltpu.VMEM((2, HALF, HD), BF16),
            *block_scratch(1),
            pltpu.VMEM((2, BLOCK, HD), BF16),
            pltpu.SemaphoreType.DMA((1,)),
        ],
        compiler_params=pltpu.CompilerParams(vmem_limit_bytes=32 * MB),
        cost_estimate=pl.CostEstimate(
            flops=6 * 10**9, bytes_accessed=8 * MB, transcendentals=0
        ),
        name="finish_prefix",
    )(rows, place, *state, *last, *everything)


def merge_kernel(at_ref, back_ref, so_ref, sl_ref, out_ref):
    picked = KVH * 4 * ROWS
    line = iota((picked, ARR), 1)
    first = dot((at_ref[...] == line).astype(BF16), back_ref[...])
    second = dot((at_ref[...] + SLOTS == line).astype(BF16), back_ref[:, :PART])
    spread = (
        (iota((HD, WIDE), 0) % GROUP == iota((HD, WIDE), 1) // HD)
        & (iota((HD, WIDE), 0) < 3 * GROUP)
    ).astype(BF16)
    lse = dot(first[:, PART:].astype(BF16), spread)
    for h in range(KVH):
        cut = slice(h * WIDE, (h + 1) * WIDE)
        rows = [slice((h * 4 + j) * ROWS, (h * 4 + j + 1) * ROWS) for j in range(4)]
        parts = [
            (lse[r], jnp.concatenate([first[r, :PART], second[r]], axis=1)) for r in rows
        ]
        parts.append((sl_ref[:, cut], so_ref[:, cut]))
        top = functools.reduce(jnp.maximum, [p[0] for p in parts])
        weights = [jnp.exp(p[0] - top) for p in parts]
        total = functools.reduce(jnp.add, weights)
        acc = functools.reduce(jnp.add, [w * p[1] for w, p in zip(weights, parts)])
        out_ref[:, cut] = (acc / total).astype(BF16)


def merge(prompt_ids, back, so, sl):
    prompt = prompt_ids[:, 0]
    earlier = jnp.arange(ROWS)[None, :] < jnp.arange(ROWS)[:, None]
    rank = jnp.sum(((prompt[:, None] == prompt[None, :]) & earlier).astype(jnp.int32), axis=1)
    h = jnp.arange(KVH)[:, None, None]
    j = jnp.arange(4)[None, :, None]
    c = h // 4
    z = jnp.where(c == 0, h, j)
    y = jnp.where(c == 0, j, h - 4)
    place = (prompt % 2 != c).astype(jnp.int32) * CAP + rank
    at = device_number(prompt // 2, c, z, y) * LINES + place
    return pl.pallas_call(
        merge_kernel,
        out_shape=jax.ShapeDtypeStruct((ROWS, KVH * WIDE), BF16),
        compiler_params=pltpu.CompilerParams(vmem_limit_bytes=16 * MB),
        name="merge",
    )(at.reshape(-1, 1), back, so, sl)


def exchange(array):
    width = array.shape[1]
    moved = lax.all_to_all(
        array.reshape(DEVS, LINES, width), AXES, split_axis=0, concat_axis=0, tiled=True
    )
    return moved.reshape(ARR, width)


def body(queries, prompt_ids, suffix_len, page_table, suffix_pool, prefix_kv):
    c = lax.axis_index("pre") % NC
    z = lax.axis_index("row") // NY
    y = lax.axis_index("row") % NY
    heads = jnp.stack(
        [
            jnp.where(c ^ cross == 0, (z + k) % NZ, NZ + (y + k) % NY)
            for k in range(4)
            for cross in range(2)
        ]
    ).astype(jnp.int32)
    sends = fill_sends(prompt_ids, queries)
    sends, heads = lax.optimization_barrier((sends, heads))
    arrived = exchange(sends)
    pieces = split_heads(heads, prefix_kv)

    def move(n, piece):
        return lax.ppermute(piece, AXES, routes(n // 2, n % 2))

    kv = list(pieces)
    for n in (1, 2, 3, 6, 7):
        kv[n] = move(n, pieces[n])
    kv[1], later = lax.optimization_barrier((kv[1], pieces[4]))
    kv[4] = move(4, later)
    arrived, kv[1] = lax.optimization_barrier((arrived, kv[1]))
    rows, place = gather_rows(arrived)
    state = add_sums(rows, place, kv[0:2], ())
    state, kv[2], kv[3], kv[6], kv[7], later = lax.optimization_barrier(
        (state, kv[2], kv[3], kv[6], kv[7], pieces[5])
    )
    kv[5] = move(5, later)
    state = add_sums(rows, place, kv[2:4] + kv[6:8], state)
    parts = finish_prefix(rows, place, state, kv[4:6], kv)
    parts, queries = lax.optimization_barrier((parts, queries))
    so, sl = suffix(page_table, suffix_len, queries, suffix_pool)
    return merge(prompt_ids, exchange(parts), so, sl)


def solution(mesh):
    return jax.shard_map(
        body,
        mesh=mesh,
        in_specs=(
            P(("pre", "row"), None),
            P(("pre", "row"), None),
            P(("pre", "row")),
            P(("pre", "row"), None),
            P(("pre", "row"), None, None),
            P("pre", "row", None),
        ),
        out_specs=P(("pre", "row"), None),
        check_vma=False,
    )
```

```python
import functools
import math

import jax
import jax.numpy as jnp
from jax import lax
from jax.experimental import pallas as pl
from jax.experimental.pallas import tpu as pltpu
from jax.sharding import PartitionSpec as P

KVH = 8
HD = 128
CAP = 2
GROUP = 12
ROWS = 8
WIDE = GROUP * HD
KVW = KVH * HD
NX, NC, NZ, NY = 4, 2, 4, 4
DEVS = NX * NC * NZ * NY
BLOCK = 1024
PAGE = 16
MAXP = 16
SPAN = PAGE * MAXP
SLOTS = 2 * CAP
HALVES = 2
PER_HALF = GROUP // HALVES
PAIRS = PER_HALF // 2
PART = PER_HALF * HD
LINES = HALVES * SLOTS
ARR = DEVS * LINES
HALF = DEVS * CAP
TILE = 128
UNROLL = 3
EMPTY = 256.0
SCALE = 1.0 / math.sqrt(HD)
FACTOR = SCALE / math.log(2.0)
LEAST = 1e-26
MOST = 1e30
AXES = ("pre", "row")
MB = 1 << 20
F32 = jnp.float32
BF16 = jnp.bfloat16


def dot(a, b):
    return jnp.dot(a, b, preferred_element_type=F32)


def dot_t(a, b):
    return lax.dot_general(a, b, (((1,), (1,)), ((), ())), preferred_element_type=F32)


def iota(shape, dim):
    return lax.broadcasted_iota(jnp.int32, shape, dim)


def device_number(x, c, z, y):
    return ((x * NC + c) * NZ + z) * NY + y


def routes(k, cross):
    pairs = []
    for x in range(NX):
        for c in range(NC):
            for z in range(NZ):
                for y in range(NY):
                    if (c ^ cross) == 0:
                        to = device_number(x, 0, (z + k) % NZ, y)
                    else:
                        to = device_number(x, 1, z, (y + k) % NY)
                    pairs.append((device_number(x, c, z, y), to))
    return pairs


def split_heads_kernel(head_ref, kv_ref, *refs):
    outs, (held, sems) = refs[:-2], refs[-2:]
    inward, outward = [], []
    for i, out in enumerate(outs):
        for part in range(2):
            start = pl.multiple_of(part * KVW + head_ref[i] * HD, HD)
            inward.append(
                pltpu.make_async_copy(
                    kv_ref.at[0, :, pl.ds(start, HD)], held.at[i, part], sems.at[0, i, part]
                )
            )
            outward.append(
                pltpu.make_async_copy(held.at[i, part], out.at[part], sems.at[1, i, part])
            )
    for copy in inward:
        copy.start()
    for copy, onward in zip(inward, outward):
        copy.wait()
        onward.start()
    for copy in outward:
        copy.wait()


def split_heads(heads, prefix_kv):
    n = heads.shape[0]
    return pl.pallas_call(
        split_heads_kernel,
        out_shape=[jax.ShapeDtypeStruct((2, BLOCK, HD), BF16)] * n,
        in_specs=[pl.BlockSpec(memory_space=pltpu.SMEM), pl.BlockSpec(memory_space=pltpu.HBM)],
        out_specs=[pl.BlockSpec(memory_space=pltpu.HBM)] * n,
        scratch_shapes=[
            pltpu.VMEM((n, 2, BLOCK, HD), BF16),
            pltpu.SemaphoreType.DMA((2, n, 2)),
        ],
        compiler_params=pltpu.CompilerParams(vmem_limit_bytes=8 * MB),
        name="split_heads",
    )(heads, prefix_kv)


def send_kernel(prompt_ref, q_ref, out_ref):
    wide = HALVES * NY * ROWS
    lane = iota((1, wide), 1) % ROWS
    slot = jnp.zeros((1, wide), jnp.int32)
    for i in range(ROWS):
        rank = sum((prompt_ref[j] == prompt_ref[i]).astype(jnp.int32) for j in range(i))
        slot = jnp.where(lane == i, prompt_ref[i] * CAP + rank, slot)
    unit = NY * LINES
    rows = NX * unit
    r = iota((rows, wide), 0)
    lane = iota((rows, wide), 1)
    base = r // unit * SLOTS
    half_fits = r // SLOTS % HALVES == lane // ROWS % HALVES
    first = (base + r % SLOTS == slot) & half_fits & (lane < HALVES * ROWS)
    second = (
        (base + (r + CAP) % SLOTS == slot)
        & half_fits
        & (r // LINES % NY == lane // (HALVES * ROWS))
    )
    first = first.astype(F32)
    second = second.astype(F32)
    empty_first = (1.0 - jnp.sum(first, axis=1, keepdims=True)) * EMPTY
    empty_second = (1.0 - jnp.sum(second, axis=1, keepdims=True)) * EMPTY
    first = first[:, : HALVES * ROWS].astype(BF16)
    second = second.astype(BF16)

    def stacked(heads):
        return jnp.concatenate(
            [
                q_ref[:, h * WIDE + half * PART : h * WIDE + (half + 1) * PART].astype(F32)
                for h in heads
                for half in range(HALVES)
            ],
            axis=0,
        ).astype(BF16)

    for z in range(NZ):
        piece = (dot(first, stacked([z])) + empty_first).astype(BF16)
        for x in range(NX):
            at = device_number(x, 0, z, 0) * LINES
            out_ref[at : at + unit, :] = piece[x * unit : (x + 1) * unit]
    piece = dot(second, stacked([NZ + y for y in range(NY)])) + empty_second
    piece = piece.astype(BF16)
    for x in range(NX):
        for z in range(NZ):
            at = device_number(x, 1, z, 0) * LINES
            out_ref[at : at + unit, :] = piece[x * unit : (x + 1) * unit]


def fill_sends(prompt_ids, queries):
    return pl.pallas_call(
        send_kernel,
        out_shape=jax.ShapeDtypeStruct((ARR, PART), BF16),
        in_specs=[
            pl.BlockSpec(memory_space=pltpu.SMEM),
            pl.BlockSpec(memory_space=pltpu.VMEM),
        ],
        compiler_params=pltpu.CompilerParams(vmem_limit_bytes=60 * MB),
        name="fill_sends",
    )(prompt_ids[:, 0], queries)


def suffix_kernel(table_ref, len_ref, q_ref, pool_ref, out_ref, lse_ref, kv, sems):
    for row in range(ROWS):
        for p in range(MAXP):
            pltpu.make_async_copy(
                pool_ref.at[table_ref[row, p]],
                kv.at[row, pl.ds(p * PAGE, PAGE), :],
                sems.at[row],
            ).start()

    def one(row, carry):
        pltpu.make_async_copy(kv.at[row], kv.at[row], sems.at[row]).wait()
        scores = jnp.concatenate(
            [
                dot_t(q_ref[row, h], kv[row, :, h * HD : (h + 1) * HD])
                for h in range(KVH)
            ],
            axis=0,
        )
        in_range = iota((KVH * 16, SPAN), 1) < len_ref[row]
        scores = jnp.where(in_range, scores * SCALE, -1e30)
        top = jnp.max(scores, axis=1, keepdims=True)
        weights = jnp.where(in_range, jnp.exp(scores - top), 0.0)
        total = jnp.sum(weights, axis=1, keepdims=True)
        scale = 1.0 / total
        lse = top + jnp.log(total)
        weights = weights.astype(BF16)
        for h in range(KVH):
            cut = slice(h * 16, (h + 1) * 16)
            values = kv[row, :, KVW + h * HD : KVW + (h + 1) * HD]
            out_ref[row, h] = dot(weights[cut], values) * scale[cut]
            lse_ref[row, h] = jnp.broadcast_to(lse[cut], (16, HD))
        return carry

    lax.fori_loop(0, ROWS, one, 0)


def suffix(page_table, suffix_len, queries, suffix_pool):
    q = queries.reshape(ROWS, KVH, GROUP, HD)
    q = jnp.pad(q, ((0, 0), (0, 0), (0, 16 - GROUP), (0, 0)))
    smem = pl.BlockSpec(memory_space=pltpu.SMEM)
    vmem = pl.BlockSpec(memory_space=pltpu.VMEM)
    shape = jax.ShapeDtypeStruct((ROWS, KVH, 16, HD), F32)
    out, lse = pl.pallas_call(
        suffix_kernel,
        out_shape=[shape, shape],
        in_specs=[smem, smem, vmem, pl.BlockSpec(memory_space=pl.ANY)],
        out_specs=[vmem, vmem],
        scratch_shapes=[
            pltpu.VMEM((ROWS, SPAN, 2 * KVW), BF16),
            pltpu.SemaphoreType.DMA((ROWS,)),
        ],
        compiler_params=pltpu.CompilerParams(vmem_limit_bytes=56 * MB),
        cost_estimate=pl.CostEstimate(
            flops=10**9, bytes_accessed=9 * MB, transcendentals=0
        ),
        name="suffix",
    )(page_table, suffix_len, q, suffix_pool)
    return (
        out[:, :, :GROUP].reshape(ROWS, KVH * WIDE),
        lse[:, :, :GROUP].reshape(ROWS, KVH * WIDE),
    )


def line_turn(line):
    return line // CAP % 2


def line_half(line):
    return line // SLOTS % HALVES


def gather_kernel(x_ref, q_ref, place_ref):
    pick = (iota((8, HD), 1) == 0).astype(BF16)
    held = dot_t(pick, x_ref[:, :HD]) < EMPTY / 2
    a, b = iota((ARR, ARR), 0), iota((ARR, ARR), 1)
    before = (a <= b) & (((a ^ b) & (LINES - CAP)) == 0)
    place = dot(held.astype(BF16), before.astype(BF16)).astype(jnp.int32) - 1
    place = jnp.where(held, place, -1)
    place_ref[...] = place
    line = iota((1, ARR), 1)
    for turn in range(2):
        for half in range(HALVES):
            mine = (line_turn(line) == turn) & (line_half(line) == half)
            row = jnp.where(mine, place[0:1], -1)
            gather = (row == iota((HALF, ARR), 0)).astype(BF16)
            for p in range(PAIRS):
                two = dot(gather, x_ref[:, p * 2 * HD : (p + 1) * 2 * HD]).astype(BF16)
                q_ref[turn, half * PER_HALF + 2 * p] = two[:, :HD]
                q_ref[turn, half * PER_HALF + 2 * p + 1] = two[:, HD:]


def gather_rows(arrived):
    return pl.pallas_call(
        gather_kernel,
        out_shape=[
            jax.ShapeDtypeStruct((2, GROUP, HALF, HD), BF16),
            jax.ShapeDtypeStruct((8, ARR), jnp.int32),
        ],
        compiler_params=pltpu.CompilerParams(vmem_limit_bytes=16 * MB),
        name="gather_rows",
    )(arrived)


def row_counts(place_ref):
    line = iota((1, ARR), 1)
    return [
        jnp.max(jnp.where(line_turn(line) == turn, place_ref[0:1], -1)) + 1
        for turn in range(2)
    ]


def widen(pair, column):
    lane = iota((TILE, HD), 1)
    wide = jnp.zeros((TILE, HD), F32)
    for i in range(2):
        mine = (lane % GROUP == 2 * pair + i) & (lane < 3 * GROUP)
        wide = wide + jnp.where(mine, column[i * TILE : (i + 1) * TILE], 0.0)
    return wide


def pair_rows(q_ref, turn, pair, at):
    return q_ref[turn, pl.ds(2 * pair, 2), pl.ds(at, TILE), :].reshape(2 * TILE, HD)


def plain_part(q, keys, values):
    weights = jnp.exp2(dot_t(q, keys) * FACTOR)
    cuts = [weights[:, c : c + HD] for c in range(0, weights.shape[1], HD)]
    total = jnp.sum(functools.reduce(jnp.add, cuts), axis=1, keepdims=True)
    return dot(weights.astype(BF16), values), total


def load_blocks(kv_refs, ks, vs, sems):
    copies = []
    for n, ref in enumerate(kv_refs):
        rows = pl.ds(n // 2 * BLOCK, BLOCK)
        copies.append(pltpu.make_async_copy(ref.at[0], ks.at[n % 2, rows], sems.at[n, 0]))
        copies.append(pltpu.make_async_copy(ref.at[1], vs.at[n % 2, rows], sems.at[n, 1]))
    for copy in copies:
        copy.start()
    return copies


def over_tiles(place_ref, step):
    first, second = [(count + TILE - 1) // TILE for count in row_counts(place_ref)]

    def tile(t, carry):
        turn = (t >= first).astype(jnp.int32)
        step(turn, pl.multiple_of((t - turn * first) * TILE, TILE))
        return carry

    lax.fori_loop(0, first + second, tile, 0)


def sums_kernel(blocks, first, q_ref, place_ref, *refs):
    kv_refs, refs = refs[: 2 * blocks], refs[2 * blocks :]
    out_ref, total_ref, ks, vs, sems = refs[-5:]
    for copy in load_blocks(kv_refs, ks, vs, sems):
        copy.wait()

    def step(turn, at):
        def one(pair, wide):
            q = pair_rows(q_ref, turn, pair, at)
            out, total = plain_part(q, ks[turn], vs[turn])
            out = out.reshape(2, TILE, HD)
            place = (turn, pl.ds(2 * pair, 2), pl.ds(at, TILE))
            if not first:
                out = out + refs[0][place]
            out_ref[place] = out
            return wide + widen(pair, total)

        if first:
            wide = jnp.zeros((TILE, HD), F32)
        else:
            wide = refs[1][turn, pl.ds(at, TILE), :]
        total_ref[turn, pl.ds(at, TILE), :] = lax.fori_loop(
            0, GROUP // 2, one, wide, unroll=UNROLL
        )

    over_tiles(place_ref, step)


def block_scratch(blocks):
    return [
        pltpu.VMEM((2, blocks * BLOCK, HD), BF16),
        pltpu.VMEM((2, blocks * BLOCK, HD), BF16),
        pltpu.SemaphoreType.DMA((2 * blocks, 2)),
    ]


def add_sums(rows, place, kv, state):
    blocks = len(kv) // 2
    vmem = pl.BlockSpec(memory_space=pltpu.VMEM)
    return pl.pallas_call(
        functools.partial(sums_kernel, blocks, not state),
        out_shape=[
            jax.ShapeDtypeStruct((2, GROUP, HALF, HD), F32),
            jax.ShapeDtypeStruct((2, HALF, HD), F32),
        ],
        in_specs=[vmem] * 2 + [pl.BlockSpec(memory_space=pl.ANY)] * len(kv) + [vmem] * len(state),
        out_specs=[vmem, vmem],
        scratch_shapes=block_scratch(blocks),
        compiler_params=pltpu.CompilerParams(vmem_limit_bytes=24 * MB),
        cost_estimate=pl.CostEstimate(
            flops=blocks * 4 * 10**9, bytes_accessed=8 * MB, transcendentals=0
        ),
        name="sums_%d" % blocks,
    )(rows, place, *kv, *state)


def last_kernel(q_ref, place_ref, sum_ref, total_ref, *refs):
    kv_refs, all_refs, (out_ref, os, ls, ks, vs, sems, held, held_sem) = (
        refs[:2],
        refs[2:10],
        refs[10:],
    )
    copies = load_blocks(kv_refs, ks, vs, sems)
    os[...] = jnp.zeros((2, GROUP // 2, HALF, 2 * HD), BF16)
    ls[...] = jnp.zeros((2, HALF, HD), BF16)
    for copy in copies:
        copy.wait()
    lane = iota((TILE, HD), 1)

    def keep(turn, pair, at, out, totals):
        for i in range(2):
            os[turn, pair, pl.ds(at, TILE), i * HD : (i + 1) * HD] = (
                out[i * TILE : (i + 1) * TILE] / totals[i]
            ).astype(BF16)

    def keep_lse(turn, at, total, shift):
        lse = jnp.where(lane < 3 * GROUP, shift + jnp.log(total), 0.0)
        one = lse.astype(BF16).astype(F32)
        two = (lse - one).astype(BF16).astype(F32)
        three = lse - one - two
        split = jnp.where(lane < GROUP, one, jnp.where(lane < 2 * GROUP, two, three))
        ls[turn, pl.ds(at, TILE), :] = split.astype(BF16)

    def fetch(k, turn):
        for n, ref in enumerate(all_refs):

            @pl.when(2 * k + turn == n)
            def _(ref=ref):
                copy = pltpu.make_async_copy(ref, held, held_sem.at[0])
                copy.start()
                copy.wait()

    def step(turn, at):
        before = total_ref[turn, pl.ds(at, TILE), :]

        def one(pair, wide):
            q = pair_rows(q_ref, turn, pair, at)
            out, total = plain_part(q, ks[turn], vs[turn])
            out = out + sum_ref[turn, pl.ds(2 * pair, 2), pl.ds(at, TILE), :].reshape(
                2 * TILE, HD
            )
            totals = [
                total[i * TILE : (i + 1) * TILE]
                + jnp.sum(
                    jnp.where(lane == 2 * pair + i, before, 0.0), axis=1, keepdims=True
                )
                for i in range(2)
            ]
            keep(turn, pair, at, out, totals)
            return wide + widen(pair, total)

        total = lax.fori_loop(0, GROUP // 2, one, before, unroll=UNROLL)
        keep_lse(turn, at, total, 0.0)
        known = jnp.where(lane < 3 * GROUP, total, 1.0)
        plain = (jnp.min(known) > LEAST) & (jnp.max(known) < MOST)

        @pl.when(jnp.logical_not(plain))
        def _():
            def again(pair, carry):
                q = pair_rows(q_ref, turn, pair, at)

                def block(k, state):
                    top, amount, acc = state
                    fetch(k, turn)
                    score = dot_t(q, held[0])
                    high = jnp.maximum(top, jnp.max(score, axis=1, keepdims=True))
                    weights = jnp.exp2(score * FACTOR - high * FACTOR)
                    fade = jnp.exp2((top - high) * FACTOR)
                    amount = amount * fade + jnp.sum(weights, axis=1, keepdims=True)
                    return high, amount, acc * fade + dot(weights.astype(BF16), held[1])

                top, amount, acc = lax.fori_loop(
                    0,
                    4,
                    block,
                    (
                        jnp.full((2 * TILE, 1), -1e30, F32),
                        jnp.zeros((2 * TILE, 1), F32),
                        jnp.zeros((2 * TILE, HD), F32),
                    ),
                )
                keep(turn, pair, at, acc, [amount[:TILE], amount[TILE:]])
                return carry[0] + widen(pair, amount), carry[1] + widen(pair, top * SCALE)

            empty = jnp.zeros((TILE, HD), F32)
            amount, shift = lax.fori_loop(0, GROUP // 2, again, (empty, empty))
            keep_lse(turn, at, amount, shift)

    over_tiles(place_ref, step)

    place_col = jnp.transpose(place_ref[...].astype(F32))[:, 0:1].astype(jnp.int32)
    line = iota((ARR, 1), 0)
    scatter = jnp.concatenate(
        [
            (
                jnp.where((line_turn(line) == turn) & (line_half(line) == half), place_col, -1)
                == iota((ARR, HALF), 1)
            ).astype(BF16)
            for turn in range(2)
            for half in range(HALVES)
        ],
        axis=1,
    )
    for p in range(PAIRS):
        source = jnp.concatenate(
            [os[turn, half * PAIRS + p] for turn in range(2) for half in range(HALVES)], axis=0
        )
        out_ref[:, p * 2 * HD : (p + 1) * 2 * HD] = dot(scatter, source).astype(BF16)
    source = jnp.concatenate([ls[0], ls[0], ls[1], ls[1]], axis=0)
    out_ref[:, PART:] = dot(scatter, source).astype(BF16)


def finish_prefix(rows, place, state, last, everything):
    vmem = pl.BlockSpec(memory_space=pltpu.VMEM)
    return pl.pallas_call(
        last_kernel,
        out_shape=jax.ShapeDtypeStruct((ARR, PART + HD), BF16),
        in_specs=[vmem] * 4 + [pl.BlockSpec(memory_space=pl.ANY)] * 10,
        scratch_shapes=[
            pltpu.VMEM((2, GROUP // 2, HALF, 2 * HD), BF16),
            pltpu.VMEM((2, HALF, HD), BF16),
            *block_scratch(1),
            pltpu.VMEM((2, BLOCK, HD), BF16),
            pltpu.SemaphoreType.DMA((1,)),
        ],
        compiler_params=pltpu.CompilerParams(vmem_limit_bytes=32 * MB),
        cost_estimate=pl.CostEstimate(
            flops=6 * 10**9, bytes_accessed=8 * MB, transcendentals=0
        ),
        name="finish_prefix",
    )(rows, place, *state, *last, *everything)


def merge_kernel(at_ref, back_ref, so_ref, sl_ref, out_ref):
    picked = KVH * 4 * ROWS
    line = iota((picked, ARR), 1)
    first = dot((at_ref[...] == line).astype(BF16), back_ref[...])
    second = dot((at_ref[...] + SLOTS == line).astype(BF16), back_ref[:, :PART])
    spread = (
        (iota((HD, WIDE), 0) % GROUP == iota((HD, WIDE), 1) // HD)
        & (iota((HD, WIDE), 0) < 3 * GROUP)
    ).astype(BF16)
    lse = dot(first[:, PART:].astype(BF16), spread)
    for h in range(KVH):
        cut = slice(h * WIDE, (h + 1) * WIDE)
        rows = [slice((h * 4 + j) * ROWS, (h * 4 + j + 1) * ROWS) for j in range(4)]
        parts = [
            (lse[r], jnp.concatenate([first[r, :PART], second[r]], axis=1)) for r in rows
        ]
        parts.append((sl_ref[:, cut], so_ref[:, cut]))
        top = functools.reduce(jnp.maximum, [p[0] for p in parts])
        weights = [jnp.exp(p[0] - top) for p in parts]
        total = functools.reduce(jnp.add, weights)
        acc = functools.reduce(jnp.add, [w * p[1] for w, p in zip(weights, parts)])
        out_ref[:, cut] = (acc / total).astype(BF16)


def merge(prompt_ids, back, so, sl):
    prompt = prompt_ids[:, 0]
    earlier = jnp.arange(ROWS)[None, :] < jnp.arange(ROWS)[:, None]
    rank = jnp.sum(((prompt[:, None] == prompt[None, :]) & earlier).astype(jnp.int32), axis=1)
    h = jnp.arange(KVH)[:, None, None]
    j = jnp.arange(4)[None, :, None]
    c = h // 4
    z = jnp.where(c == 0, h, j)
    y = jnp.where(c == 0, j, h - 4)
    place = (prompt % 2 != c).astype(jnp.int32) * CAP + rank
    at = device_number(prompt // 2, c, z, y) * LINES + place
    return pl.pallas_call(
        merge_kernel,
        out_shape=jax.ShapeDtypeStruct((ROWS, KVH * WIDE), BF16),
        compiler_params=pltpu.CompilerParams(vmem_limit_bytes=16 * MB),
        name="merge",
    )(at.reshape(-1, 1), back, so, sl)


def exchange(array):
    width = array.shape[1]
    moved = lax.all_to_all(
        array.reshape(DEVS, LINES, width), AXES, split_axis=0, concat_axis=0, tiled=True
    )
    return moved.reshape(ARR, width)


def body(queries, prompt_ids, suffix_len, page_table, suffix_pool, prefix_kv):
    c = lax.axis_index("pre") % NC
    z = lax.axis_index("row") // NY
    y = lax.axis_index("row") % NY
    heads = jnp.stack(
        [
            jnp.where(c ^ cross == 0, (z + k) % NZ, NZ + (y + k) % NY)
            for k in range(4)
            for cross in range(2)
        ]
    ).astype(jnp.int32)
    sends = fill_sends(prompt_ids, queries)
    sends, heads = lax.optimization_barrier((sends, heads))
    arrived = exchange(sends)
    pieces = split_heads(heads, prefix_kv)

    def move(n, piece):
        return lax.ppermute(piece, AXES, routes(n // 2, n % 2))

    kv = list(pieces)
    for n in (1, 2, 3, 6, 7):
        kv[n] = move(n, pieces[n])
    arrived, kv[1] = lax.optimization_barrier((arrived, kv[1]))
    rows, place = gather_rows(arrived)
    place, later = lax.optimization_barrier((place, pieces[4]))
    kv[4] = move(4, later)
    state = add_sums(rows, place, kv[0:2], ())
    state, kv[2], kv[3], kv[6], kv[7], later = lax.optimization_barrier(
        (state, kv[2], kv[3], kv[6], kv[7], pieces[5])
    )
    kv[5] = move(5, later)
    state = add_sums(rows, place, kv[2:4] + kv[6:8], state)
    parts = finish_prefix(rows, place, state, kv[4:6], kv)
    parts, queries = lax.optimization_barrier((parts, queries))
    so, sl = suffix(page_table, suffix_len, queries, suffix_pool)
    return merge(prompt_ids, exchange(parts), so, sl)


def solution(mesh):
    return jax.shard_map(
        body,
        mesh=mesh,
        in_specs=(
            P(("pre", "row"), None),
            P(("pre", "row"), None),
            P(("pre", "row")),
            P(("pre", "row"), None),
            P(("pre", "row"), None, None),
            P("pre", "row", None),
        ),
        out_specs=P(("pre", "row"), None),
        check_vma=False,
    )
```

```python
import functools
import math

import jax
import jax.numpy as jnp
from jax import lax
from jax.experimental import pallas as pl
from jax.experimental.pallas import tpu as pltpu
from jax.sharding import PartitionSpec as P

KVH = 8
HD = 128
CAP = 2
GROUP = 12
ROWS = 8
WIDE = GROUP * HD
KVW = KVH * HD
NX, NC, NZ, NY = 4, 2, 4, 4
DEVS = NX * NC * NZ * NY
BLOCK = 1024
PAGE = 16
MAXP = 16
SPAN = PAGE * MAXP
SLOTS = 2 * CAP
HALVES = 2
PER_HALF = GROUP // HALVES
PAIRS = PER_HALF // 2
PART = PER_HALF * HD
THIRD = PAIRS * HD
LINES = HALVES * SLOTS
ARR = DEVS * LINES
HALF = DEVS * CAP
TILE = 128
UNROLL = 3
EMPTY = 256.0
SCALE = 1.0 / math.sqrt(HD)
FACTOR = SCALE / math.log(2.0)
LEAST = 1e-26
MOST = 1e30
AXES = ("pre", "row")
MB = 1 << 20
F32 = jnp.float32
BF16 = jnp.bfloat16


def dot(a, b):
    return jnp.dot(a, b, preferred_element_type=F32)


def dot_t(a, b):
    return lax.dot_general(a, b, (((1,), (1,)), ((), ())), preferred_element_type=F32)


def iota(shape, dim):
    return lax.broadcasted_iota(jnp.int32, shape, dim)


def device_number(x, c, z, y):
    return ((x * NC + c) * NZ + z) * NY + y


def routes(k, cross):
    pairs = []
    for x in range(NX):
        for c in range(NC):
            for z in range(NZ):
                for y in range(NY):
                    if (c ^ cross) == 0:
                        to = device_number(x, 0, (z + k) % NZ, y)
                    else:
                        to = device_number(x, 1, z, (y + k) % NY)
                    pairs.append((device_number(x, c, z, y), to))
    return pairs


def split_heads_kernel(head_ref, kv_ref, *refs):
    outs, (held, sems) = refs[:-2], refs[-2:]
    inward, outward = [], []
    for i, out in enumerate(outs):
        for part in range(2):
            start = pl.multiple_of(part * KVW + head_ref[i] * HD, HD)
            inward.append(
                pltpu.make_async_copy(
                    kv_ref.at[0, :, pl.ds(start, HD)], held.at[i, part], sems.at[0, i, part]
                )
            )
            outward.append(
                pltpu.make_async_copy(held.at[i, part], out.at[part], sems.at[1, i, part])
            )
    for copy in inward:
        copy.start()
    for copy, onward in zip(inward, outward):
        copy.wait()
        onward.start()
    for copy in outward:
        copy.wait()


def split_heads(heads, prefix_kv):
    n = heads.shape[0]
    return pl.pallas_call(
        split_heads_kernel,
        out_shape=[jax.ShapeDtypeStruct((2, BLOCK, HD), BF16)] * n,
        in_specs=[pl.BlockSpec(memory_space=pltpu.SMEM), pl.BlockSpec(memory_space=pltpu.HBM)],
        out_specs=[pl.BlockSpec(memory_space=pltpu.HBM)] * n,
        scratch_shapes=[
            pltpu.VMEM((n, 2, BLOCK, HD), BF16),
            pltpu.SemaphoreType.DMA((2, n, 2)),
        ],
        compiler_params=pltpu.CompilerParams(vmem_limit_bytes=8 * MB),
        name="split_heads",
    )(heads, prefix_kv)


def send_kernel(prompt_ref, q_ref, out_ref):
    wide = HALVES * NY * ROWS
    lane = iota((1, wide), 1) % ROWS
    slot = jnp.zeros((1, wide), jnp.int32)
    for i in range(ROWS):
        rank = sum((prompt_ref[j] == prompt_ref[i]).astype(jnp.int32) for j in range(i))
        slot = jnp.where(lane == i, prompt_ref[i] * CAP + rank, slot)
    unit = NY * LINES
    rows = NX * unit
    r = iota((rows, wide), 0)
    lane = iota((rows, wide), 1)
    base = r // unit * SLOTS
    half_fits = r // SLOTS % HALVES == lane // ROWS % HALVES
    first = (base + r % SLOTS == slot) & half_fits & (lane < HALVES * ROWS)
    second = (
        (base + (r + CAP) % SLOTS == slot)
        & half_fits
        & (r // LINES % NY == lane // (HALVES * ROWS))
    )
    first = first.astype(F32)
    second = second.astype(F32)
    empty_first = (1.0 - jnp.sum(first, axis=1, keepdims=True)) * EMPTY
    empty_second = (1.0 - jnp.sum(second, axis=1, keepdims=True)) * EMPTY
    first = first[:, : HALVES * ROWS].astype(BF16)
    second = second.astype(BF16)

    def stacked(heads):
        return jnp.concatenate(
            [
                q_ref[:, h * WIDE + half * PART : h * WIDE + (half + 1) * PART].astype(F32)
                for h in heads
                for half in range(HALVES)
            ],
            axis=0,
        ).astype(BF16)

    for z in range(NZ):
        piece = (dot(first, stacked([z])) + empty_first).astype(BF16)
        for x in range(NX):
            at = device_number(x, 0, z, 0) * LINES
            out_ref[at : at + unit, :] = piece[x * unit : (x + 1) * unit]
    piece = dot(second, stacked([NZ + y for y in range(NY)])) + empty_second
    piece = piece.astype(BF16)
    for x in range(NX):
        for z in range(NZ):
            at = device_number(x, 1, z, 0) * LINES
            out_ref[at : at + unit, :] = piece[x * unit : (x + 1) * unit]


def fill_sends(prompt_ids, queries):
    return pl.pallas_call(
        send_kernel,
        out_shape=jax.ShapeDtypeStruct((ARR, PART), BF16),
        in_specs=[
            pl.BlockSpec(memory_space=pltpu.SMEM),
            pl.BlockSpec(memory_space=pltpu.VMEM),
        ],
        compiler_params=pltpu.CompilerParams(vmem_limit_bytes=60 * MB),
        name="fill_sends",
    )(prompt_ids[:, 0], queries)


def suffix_kernel(table_ref, len_ref, q_ref, pool_ref, out_ref, lse_ref, kv, sems):
    for row in range(ROWS):
        for p in range(MAXP):
            pltpu.make_async_copy(
                pool_ref.at[table_ref[row, p]],
                kv.at[row, pl.ds(p * PAGE, PAGE), :],
                sems.at[row],
            ).start()

    def one(row, carry):
        pltpu.make_async_copy(kv.at[row], kv.at[row], sems.at[row]).wait()
        scores = jnp.concatenate(
            [
                dot_t(q_ref[row, h], kv[row, :, h * HD : (h + 1) * HD])
                for h in range(KVH)
            ],
            axis=0,
        )
        in_range = iota((KVH * 16, SPAN), 1) < len_ref[row]
        scores = jnp.where(in_range, scores * SCALE, -1e30)
        top = jnp.max(scores, axis=1, keepdims=True)
        weights = jnp.where(in_range, jnp.exp(scores - top), 0.0)
        total = jnp.sum(weights, axis=1, keepdims=True)
        scale = 1.0 / total
        lse = top + jnp.log(total)
        weights = weights.astype(BF16)
        for h in range(KVH):
            cut = slice(h * 16, (h + 1) * 16)
            values = kv[row, :, KVW + h * HD : KVW + (h + 1) * HD]
            out_ref[row, h] = dot(weights[cut], values) * scale[cut]
            lse_ref[row, h] = jnp.broadcast_to(lse[cut], (16, HD))
        return carry

    lax.fori_loop(0, ROWS, one, 0)


def suffix(page_table, suffix_len, queries, suffix_pool):
    q = queries.reshape(ROWS, KVH, GROUP, HD)
    q = jnp.pad(q, ((0, 0), (0, 0), (0, 16 - GROUP), (0, 0)))
    smem = pl.BlockSpec(memory_space=pltpu.SMEM)
    vmem = pl.BlockSpec(memory_space=pltpu.VMEM)
    shape = jax.ShapeDtypeStruct((ROWS, KVH, 16, HD), F32)
    out, lse = pl.pallas_call(
        suffix_kernel,
        out_shape=[shape, shape],
        in_specs=[smem, smem, vmem, pl.BlockSpec(memory_space=pl.ANY)],
        out_specs=[vmem, vmem],
        scratch_shapes=[
            pltpu.VMEM((ROWS, SPAN, 2 * KVW), BF16),
            pltpu.SemaphoreType.DMA((ROWS,)),
        ],
        compiler_params=pltpu.CompilerParams(vmem_limit_bytes=48 * MB),
        cost_estimate=pl.CostEstimate(
            flops=10**9, bytes_accessed=9 * MB, transcendentals=0
        ),
        name="suffix",
    )(page_table, suffix_len, q, suffix_pool)
    return (
        out[:, :, :GROUP].reshape(ROWS, KVH * WIDE),
        lse[:, :, :GROUP].reshape(ROWS, KVH * WIDE),
    )


def line_turn(line):
    return line // CAP % 2


def line_half(line):
    return line // SLOTS % HALVES


def gather_kernel(x_ref, q_ref, place_ref):
    pick = (iota((8, HD), 1) == 0).astype(BF16)
    held = dot_t(pick, x_ref[:, :HD]) < EMPTY / 2
    a, b = iota((ARR, ARR), 0), iota((ARR, ARR), 1)
    before = (a <= b) & (((a ^ b) & (LINES - CAP)) == 0)
    place = dot(held.astype(BF16), before.astype(BF16)).astype(jnp.int32) - 1
    place = jnp.where(held, place, -1)
    place_ref[...] = place
    line = iota((1, ARR), 1)
    for turn in range(2):
        for half in range(HALVES):
            mine = (line_turn(line) == turn) & (line_half(line) == half)
            row = jnp.where(mine, place[0:1], -1)
            gather = (row == iota((HALF, ARR), 0)).astype(BF16)
            for p in range(PAIRS):
                two = dot(gather, x_ref[:, p * 2 * HD : (p + 1) * 2 * HD]).astype(BF16)
                q_ref[turn, half * PER_HALF + 2 * p] = two[:, :HD]
                q_ref[turn, half * PER_HALF + 2 * p + 1] = two[:, HD:]


def gather_rows(arrived):
    return pl.pallas_call(
        gather_kernel,
        out_shape=[
            jax.ShapeDtypeStruct((2, GROUP, HALF, HD), BF16),
            jax.ShapeDtypeStruct((8, ARR), jnp.int32),
        ],
        compiler_params=pltpu.CompilerParams(vmem_limit_bytes=16 * MB),
        name="gather_rows",
    )(arrived)


def row_counts(place_ref):
    line = iota((1, ARR), 1)
    return [
        jnp.max(jnp.where(line_turn(line) == turn, place_ref[0:1], -1)) + 1
        for turn in range(2)
    ]


def widen(pair, column):
    lane = iota((TILE, HD), 1)
    wide = jnp.zeros((TILE, HD), F32)
    for i in range(2):
        mine = (lane % GROUP == 2 * pair + i) & (lane < 3 * GROUP)
        wide = wide + jnp.where(mine, column[i * TILE : (i + 1) * TILE], 0.0)
    return wide


def pair_rows(q_ref, turn, pair, at):
    return q_ref[turn, pl.ds(2 * pair, 2), pl.ds(at, TILE), :].reshape(2 * TILE, HD)


def plain_part(q, keys, values):
    weights = jnp.exp2(dot_t(q, keys) * FACTOR)
    cuts = [weights[:, c : c + HD] for c in range(0, weights.shape[1], HD)]
    total = jnp.sum(functools.reduce(jnp.add, cuts), axis=1, keepdims=True)
    return dot(weights.astype(BF16), values), total


def load_blocks(kv_refs, ks, vs, sems):
    copies = []
    for n, ref in enumerate(kv_refs):
        rows = pl.ds(n // 2 * BLOCK, BLOCK)
        copies.append(pltpu.make_async_copy(ref.at[0], ks.at[n % 2, rows], sems.at[n, 0]))
        copies.append(pltpu.make_async_copy(ref.at[1], vs.at[n % 2, rows], sems.at[n, 1]))
    for copy in copies:
        copy.start()
    return copies


def over_tiles(place_ref, step):
    first, second = [(count + TILE - 1) // TILE for count in row_counts(place_ref)]

    def tile(t, carry):
        turn = (t >= first).astype(jnp.int32)
        step(turn, pl.multiple_of((t - turn * first) * TILE, TILE))
        return carry

    lax.fori_loop(0, first + second, tile, 0)


def sums_kernel(blocks, first, q_ref, place_ref, *refs):
    kv_refs, refs = refs[: 2 * blocks], refs[2 * blocks :]
    out_ref, total_ref, ks, vs, sems = refs[-5:]
    for copy in load_blocks(kv_refs, ks, vs, sems):
        copy.wait()

    def step(turn, at):
        def one(pair, wide):
            q = pair_rows(q_ref, turn, pair, at)
            out, total = plain_part(q, ks[turn], vs[turn])
            out = out.reshape(2, TILE, HD)
            place = (turn, pl.ds(2 * pair, 2), pl.ds(at, TILE))
            if not first:
                out = out + refs[0][place]
            out_ref[place] = out
            return wide + widen(pair, total)

        if first:
            wide = jnp.zeros((TILE, HD), F32)
        else:
            wide = refs[1][turn, pl.ds(at, TILE), :]
        total_ref[turn, pl.ds(at, TILE), :] = lax.fori_loop(
            0, GROUP // 2, one, wide, unroll=UNROLL
        )

    over_tiles(place_ref, step)


def block_scratch(blocks):
    return [
        pltpu.VMEM((2, blocks * BLOCK, HD), BF16),
        pltpu.VMEM((2, blocks * BLOCK, HD), BF16),
        pltpu.SemaphoreType.DMA((2 * blocks, 2)),
    ]


def add_sums(rows, place, kv, state):
    blocks = len(kv) // 2
    vmem = pl.BlockSpec(memory_space=pltpu.VMEM)
    return pl.pallas_call(
        functools.partial(sums_kernel, blocks, not state),
        out_shape=[
            jax.ShapeDtypeStruct((2, GROUP, HALF, HD), F32),
            jax.ShapeDtypeStruct((2, HALF, HD), F32),
        ],
        in_specs=[vmem] * 2 + [pl.BlockSpec(memory_space=pl.ANY)] * len(kv) + [vmem] * len(state),
        out_specs=[vmem, vmem],
        scratch_shapes=block_scratch(blocks),
        compiler_params=pltpu.CompilerParams(vmem_limit_bytes=24 * MB),
        cost_estimate=pl.CostEstimate(
            flops=blocks * 4 * 10**9, bytes_accessed=8 * MB, transcendentals=0
        ),
        name="sums_%d" % blocks,
    )(rows, place, *kv, *state)


def last_kernel(half, q_ref, place_ref, sum_ref, total_ref, *refs):
    if half == 0:
        kv_refs, all_refs, (out_ref, ls, os, ks, vs, sems, held, held_sem) = (
            refs[:2],
            refs[2:10],
            refs[10:],
        )
    else:
        earlier_ls, kv_refs, all_refs, (out_ref, os, ks, vs, sems, held, held_sem, ls) = (
            refs[0],
            refs[1:3],
            refs[3:11],
            refs[11:],
        )
    copies = load_blocks(kv_refs, ks, vs, sems)
    os[...] = jnp.zeros((2, HALVES, HALF, THIRD), BF16)
    ls[...] = jnp.zeros((2, HALF, HD), BF16)
    for copy in copies:
        copy.wait()
    lane = iota((TILE, HD), 1)
    pairs = range(half * PAIRS, (half + 1) * PAIRS)
    mine = (lane < 3 * GROUP) & (lane % GROUP // PER_HALF == half)

    def keep(turn, pair, at, out, totals):
        for i in range(2):
            line, column = divmod(2 * pair + i - half * PER_HALF, PAIRS)
            os[turn, line, pl.ds(at, TILE), column * HD : (column + 1) * HD] = (
                out[i * TILE : (i + 1) * TILE] / totals[i]
            ).astype(BF16)

    def keep_lse(turn, at, total, shift):
        lse = jnp.where(mine, shift + jnp.log(total), 0.0)
        one = lse.astype(BF16).astype(F32)
        two = (lse - one).astype(BF16).astype(F32)
        three = lse - one - two
        split = jnp.where(lane < GROUP, one, jnp.where(lane < 2 * GROUP, two, three))
        ls[turn, pl.ds(at, TILE), :] = split.astype(BF16)

    def fetch(k, turn):
        for n, ref in enumerate(all_refs):

            @pl.when(2 * k + turn == n)
            def _(ref=ref):
                copy = pltpu.make_async_copy(ref, held, held_sem.at[0])
                copy.start()
                copy.wait()

    def step(turn, at):
        before = total_ref[turn, pl.ds(at, TILE), :]
        wide = before
        for pair in pairs:
            q = pair_rows(q_ref, turn, pair, at)
            out, total = plain_part(q, ks[turn], vs[turn])
            out = out + sum_ref[turn, pl.ds(2 * pair, 2), pl.ds(at, TILE), :].reshape(
                2 * TILE, HD
            )
            totals = [
                total[i * TILE : (i + 1) * TILE] + before[:, 2 * pair + i : 2 * pair + i + 1]
                for i in range(2)
            ]
            keep(turn, pair, at, out, totals)
            wide = wide + widen(pair, total)
        keep_lse(turn, at, wide, 0.0)
        known = jnp.where(mine, wide, 1.0)
        plain = (jnp.min(known) > LEAST) & (jnp.max(known) < MOST)

        @pl.when(jnp.logical_not(plain))
        def _():
            amounts = shifts = jnp.zeros((TILE, HD), F32)
            for pair in pairs:
                q = pair_rows(q_ref, turn, pair, at)

                def block(k, state, q=q):
                    top, amount, acc = state
                    fetch(k, turn)
                    score = dot_t(q, held[0])
                    high = jnp.maximum(top, jnp.max(score, axis=1, keepdims=True))
                    weights = jnp.exp2(score * FACTOR - high * FACTOR)
                    fade = jnp.exp2((top - high) * FACTOR)
                    amount = amount * fade + jnp.sum(weights, axis=1, keepdims=True)
                    return high, amount, acc * fade + dot(weights.astype(BF16), held[1])

                top, amount, acc = lax.fori_loop(
                    0,
                    4,
                    block,
                    (
                        jnp.full((2 * TILE, 1), -1e30, F32),
                        jnp.zeros((2 * TILE, 1), F32),
                        jnp.zeros((2 * TILE, HD), F32),
                    ),
                )
                keep(turn, pair, at, acc, [amount[:TILE], amount[TILE:]])
                amounts = amounts + widen(pair, amount)
                shifts = shifts + widen(pair, top * SCALE)
            keep_lse(turn, at, amounts, shifts)

    over_tiles(place_ref, step)

    place_col = jnp.transpose(place_ref[...].astype(F32))[:, 0:1].astype(jnp.int32)
    line = iota((ARR, 1), 0)
    scatter = jnp.concatenate(
        [
            (
                jnp.where((line_turn(line) == turn) & (line_half(line) == part), place_col, -1)
                == iota((ARR, HALF), 1)
            ).astype(BF16)
            for turn in range(2)
            for part in range(HALVES)
        ],
        axis=1,
    )
    source = jnp.concatenate(
        [os[turn, part] for turn in range(2) for part in range(HALVES)], axis=0
    )
    out_ref[:, :THIRD] = dot(scatter, source).astype(BF16)
    if half == 1:
        both = [ls[turn] + earlier_ls[turn] for turn in range(2)]
        source = jnp.concatenate([both[0], both[0], both[1], both[1]], axis=0)
        out_ref[:, THIRD:] = dot(scatter, source).astype(BF16)


def finish_prefix(half, rows, place, state, last, everything, earlier=()):
    vmem = pl.BlockSpec(memory_space=pltpu.VMEM)
    logs = (2, HALF, HD)
    out_shape = [jax.ShapeDtypeStruct((ARR, THIRD + half * HD), BF16)]
    scratch = [
        pltpu.VMEM((2, HALVES, HALF, THIRD), BF16),
        *block_scratch(1),
        pltpu.VMEM((2, BLOCK, HD), BF16),
        pltpu.SemaphoreType.DMA((1,)),
    ]
    if half == 0:
        out_shape.append(jax.ShapeDtypeStruct(logs, BF16))
    else:
        scratch.append(pltpu.VMEM(logs, BF16))
    return pl.pallas_call(
        functools.partial(last_kernel, half),
        out_shape=out_shape,
        in_specs=[vmem] * (4 + len(earlier)) + [pl.BlockSpec(memory_space=pl.ANY)] * 10,
        scratch_shapes=scratch,
        compiler_params=pltpu.CompilerParams(vmem_limit_bytes=28 * MB),
        cost_estimate=pl.CostEstimate(
            flops=6 * 10**9, bytes_accessed=8 * MB, transcendentals=0
        ),
        name="finish_%d" % half,
    )(rows, place, *state, *earlier, *last, *everything)


def merge_kernel(at_ref, back0_ref, back1_ref, so_ref, sl_ref, out_ref):
    picked = KVH * 4 * ROWS
    line = iota((picked, ARR), 1)
    first = (at_ref[...] == line).astype(BF16)
    second = (at_ref[...] + SLOTS == line).astype(BF16)
    pieces = [dot(first, back0_ref[...]), dot(second, back0_ref[...])]
    ends = dot(first, back1_ref[...])
    pieces += [ends[:, :THIRD], dot(second, back1_ref[:, :THIRD])]
    spread = (
        (iota((HD, WIDE), 0) % GROUP == iota((HD, WIDE), 1) // HD)
        & (iota((HD, WIDE), 0) < 3 * GROUP)
    ).astype(BF16)
    lse = dot(ends[:, THIRD:].astype(BF16), spread)
    for h in range(KVH):
        cut = slice(h * WIDE, (h + 1) * WIDE)
        rows = [slice((h * 4 + j) * ROWS, (h * 4 + j + 1) * ROWS) for j in range(4)]
        parts = [
            (lse[r], jnp.concatenate([piece[r] for piece in pieces], axis=1)) for r in rows
        ]
        parts.append((sl_ref[:, cut], so_ref[:, cut]))
        top = functools.reduce(jnp.maximum, [p[0] for p in parts])
        weights = [jnp.exp(p[0] - top) for p in parts]
        total = functools.reduce(jnp.add, weights)
        acc = functools.reduce(jnp.add, [w * p[1] for w, p in zip(weights, parts)])
        out_ref[:, cut] = (acc / total).astype(BF16)


def merge(prompt_ids, back0, back1, so, sl):
    prompt = prompt_ids[:, 0]
    earlier = jnp.arange(ROWS)[None, :] < jnp.arange(ROWS)[:, None]
    rank = jnp.sum(((prompt[:, None] == prompt[None, :]) & earlier).astype(jnp.int32), axis=1)
    h = jnp.arange(KVH)[:, None, None]
    j = jnp.arange(4)[None, :, None]
    c = h // 4
    z = jnp.where(c == 0, h, j)
    y = jnp.where(c == 0, j, h - 4)
    place = (prompt % 2 != c).astype(jnp.int32) * CAP + rank
    at = device_number(prompt // 2, c, z, y) * LINES + place
    return pl.pallas_call(
        merge_kernel,
        out_shape=jax.ShapeDtypeStruct((ROWS, KVH * WIDE), BF16),
        compiler_params=pltpu.CompilerParams(vmem_limit_bytes=16 * MB),
        name="merge",
    )(at.reshape(-1, 1), back0, back1, so, sl)


def exchange(array):
    width = array.shape[1]
    moved = lax.all_to_all(
        array.reshape(DEVS, LINES, width), AXES, split_axis=0, concat_axis=0, tiled=True
    )
    return moved.reshape(ARR, width)


def body(queries, prompt_ids, suffix_len, page_table, suffix_pool, prefix_kv):
    c = lax.axis_index("pre") % NC
    z = lax.axis_index("row") // NY
    y = lax.axis_index("row") % NY
    heads = jnp.stack(
        [
            jnp.where(c ^ cross == 0, (z + k) % NZ, NZ + (y + k) % NY)
            for k in range(4)
            for cross in range(2)
        ]
    ).astype(jnp.int32)
    sends = fill_sends(prompt_ids, queries)
    sends, heads = lax.optimization_barrier((sends, heads))
    arrived = exchange(sends)
    pieces = split_heads(heads, prefix_kv)

    def move(n, piece):
        return lax.ppermute(piece, AXES, routes(n // 2, n % 2))

    kv = list(pieces)
    for n in (1, 2, 3, 6, 7):
        kv[n] = move(n, pieces[n])
    so, sl = suffix(page_table, suffix_len, queries, suffix_pool)
    arrived, kv[1], so, sl = lax.optimization_barrier((arrived, kv[1], so, sl))
    rows, place = gather_rows(arrived)
    place, later = lax.optimization_barrier((place, pieces[4]))
    kv[4] = move(4, later)
    state = add_sums(rows, place, kv[0:2], ())
    state, kv[2], kv[3], kv[6], kv[7], later = lax.optimization_barrier(
        (state, kv[2], kv[3], kv[6], kv[7], pieces[5])
    )
    kv[5] = move(5, later)
    state = add_sums(rows, place, kv[2:4] + kv[6:8], state)
    part, logs = finish_prefix(0, rows, place, state, kv[4:6], kv)
    back0 = exchange(part)
    (part,) = finish_prefix(1, rows, place, state, kv[4:6], kv, (logs,))
    back1 = exchange(part)
    return merge(prompt_ids, back0, back1, so, sl)


def solution(mesh):
    return jax.shard_map(
        body,
        mesh=mesh,
        in_specs=(
            P(("pre", "row"), None),
            P(("pre", "row"), None),
            P(("pre", "row")),
            P(("pre", "row"), None),
            P(("pre", "row"), None, None),
            P("pre", "row", None),
        ),
        out_specs=P(("pre", "row"), None),
        check_vma=False,
    )
```

```python
import functools
import math

import jax
import jax.numpy as jnp
from jax import lax
from jax.experimental import pallas as pl
from jax.experimental.pallas import tpu as pltpu
from jax.sharding import PartitionSpec as P

KVH = 8
HD = 128
CAP = 2
GROUP = 12
ROWS = 8
WIDE = GROUP * HD
KVW = KVH * HD
NX, NC, NZ, NY = 4, 2, 4, 4
DEVS = NX * NC * NZ * NY
BLOCK = 1024
PAGE = 16
MAXP = 16
SPAN = PAGE * MAXP
SLOTS = 2 * CAP
HALVES = 2
PER_HALF = GROUP // HALVES
PAIRS = PER_HALF // 2
PART = PER_HALF * HD
LINES = HALVES * SLOTS
ARR = DEVS * LINES
HALF = DEVS * CAP
TILE = 128
UNROLL = 3
EMPTY = 256.0
SCALE = 1.0 / math.sqrt(HD)
FACTOR = SCALE / math.log(2.0)
LEAST = 1e-26
MOST = 1e30
AXES = ("pre", "row")
MB = 1 << 20
F32 = jnp.float32
BF16 = jnp.bfloat16


def dot(a, b):
    return jnp.dot(a, b, preferred_element_type=F32)


def dot_t(a, b):
    return lax.dot_general(a, b, (((1,), (1,)), ((), ())), preferred_element_type=F32)


def iota(shape, dim):
    return lax.broadcasted_iota(jnp.int32, shape, dim)


def device_number(x, c, z, y):
    return ((x * NC + c) * NZ + z) * NY + y


def routes(k, cross):
    pairs = []
    for x in range(NX):
        for c in range(NC):
            for z in range(NZ):
                for y in range(NY):
                    if (c ^ cross) == 0:
                        to = device_number(x, 0, (z + k) % NZ, y)
                    else:
                        to = device_number(x, 1, z, (y + k) % NY)
                    pairs.append((device_number(x, c, z, y), to))
    return pairs


def split_heads_kernel(head_ref, kv_ref, *refs):
    outs, (held, sems) = refs[:-2], refs[-2:]
    inward, outward = [], []
    for i, out in enumerate(outs):
        for part in range(2):
            start = pl.multiple_of(part * KVW + head_ref[i] * HD, HD)
            inward.append(
                pltpu.make_async_copy(
                    kv_ref.at[0, :, pl.ds(start, HD)], held.at[i, part], sems.at[0, i, part]
                )
            )
            outward.append(
                pltpu.make_async_copy(held.at[i, part], out.at[part], sems.at[1, i, part])
            )
    for copy in inward:
        copy.start()
    for copy, onward in zip(inward, outward):
        copy.wait()
        onward.start()
    for copy in outward:
        copy.wait()


def split_heads(heads, prefix_kv):
    n = heads.shape[0]
    return pl.pallas_call(
        split_heads_kernel,
        out_shape=[jax.ShapeDtypeStruct((2, BLOCK, HD), BF16)] * n,
        in_specs=[pl.BlockSpec(memory_space=pltpu.SMEM), pl.BlockSpec(memory_space=pltpu.HBM)],
        out_specs=[pl.BlockSpec(memory_space=pltpu.HBM)] * n,
        scratch_shapes=[
            pltpu.VMEM((n, 2, BLOCK, HD), BF16),
            pltpu.SemaphoreType.DMA((2, n, 2)),
        ],
        compiler_params=pltpu.CompilerParams(vmem_limit_bytes=8 * MB),
        name="split_heads",
    )(heads, prefix_kv)


def send_kernel(prompt_ref, q_ref, out_ref):
    wide = HALVES * NY * ROWS
    lane = iota((1, wide), 1) % ROWS
    slot = jnp.zeros((1, wide), jnp.int32)
    for i in range(ROWS):
        rank = sum((prompt_ref[j] == prompt_ref[i]).astype(jnp.int32) for j in range(i))
        slot = jnp.where(lane == i, prompt_ref[i] * CAP + rank, slot)
    unit = NY * LINES
    rows = NX * unit
    r = iota((rows, wide), 0)
    lane = iota((rows, wide), 1)
    base = r // unit * SLOTS
    half_fits = r // SLOTS % HALVES == lane // ROWS % HALVES
    first = (base + r % SLOTS == slot) & half_fits & (lane < HALVES * ROWS)
    second = (
        (base + (r + CAP) % SLOTS == slot)
        & half_fits
        & (r // LINES % NY == lane // (HALVES * ROWS))
    )
    first = first.astype(F32)
    second = second.astype(F32)
    empty_first = (1.0 - jnp.sum(first, axis=1, keepdims=True)) * EMPTY
    empty_second = (1.0 - jnp.sum(second, axis=1, keepdims=True)) * EMPTY
    first = first[:, : HALVES * ROWS].astype(BF16)
    second = second.astype(BF16)

    def stacked(heads):
        return jnp.concatenate(
            [
                q_ref[:, h * WIDE + half * PART : h * WIDE + (half + 1) * PART].astype(F32)
                for h in heads
                for half in range(HALVES)
            ],
            axis=0,
        ).astype(BF16)

    for z in range(NZ):
        piece = (dot(first, stacked([z])) + empty_first).astype(BF16)
        for x in range(NX):
            at = device_number(x, 0, z, 0) * LINES
            out_ref[at : at + unit, :] = piece[x * unit : (x + 1) * unit]
    piece = dot(second, stacked([NZ + y for y in range(NY)])) + empty_second
    piece = piece.astype(BF16)
    for x in range(NX):
        for z in range(NZ):
            at = device_number(x, 1, z, 0) * LINES
            out_ref[at : at + unit, :] = piece[x * unit : (x + 1) * unit]


def fill_sends(prompt_ids, queries):
    return pl.pallas_call(
        send_kernel,
        out_shape=jax.ShapeDtypeStruct((ARR, PART), BF16),
        in_specs=[
            pl.BlockSpec(memory_space=pltpu.SMEM),
            pl.BlockSpec(memory_space=pltpu.VMEM),
        ],
        compiler_params=pltpu.CompilerParams(vmem_limit_bytes=60 * MB),
        name="fill_sends",
    )(prompt_ids[:, 0], queries)


def suffix_kernel(table_ref, len_ref, q_ref, pool_ref, out_ref, lse_ref, kv, sems):
    for row in range(ROWS):
        for p in range(MAXP):
            pltpu.make_async_copy(
                pool_ref.at[table_ref[row, p]],
                kv.at[row, pl.ds(p * PAGE, PAGE), :],
                sems.at[row],
            ).start()

    def one(row, carry):
        pltpu.make_async_copy(kv.at[row], kv.at[row], sems.at[row]).wait()
        scores = jnp.concatenate(
            [
                dot_t(q_ref[row, h], kv[row, :, h * HD : (h + 1) * HD])
                for h in range(KVH)
            ],
            axis=0,
        )
        in_range = iota((KVH * 16, SPAN), 1) < len_ref[row]
        scores = jnp.where(in_range, scores * SCALE, -1e30)
        top = jnp.max(scores, axis=1, keepdims=True)
        weights = jnp.where(in_range, jnp.exp(scores - top), 0.0)
        total = jnp.sum(weights, axis=1, keepdims=True)
        scale = 1.0 / total
        lse = top + jnp.log(total)
        weights = weights.astype(BF16)
        for h in range(KVH):
            cut = slice(h * 16, (h + 1) * 16)
            values = kv[row, :, KVW + h * HD : KVW + (h + 1) * HD]
            out_ref[row, h] = dot(weights[cut], values) * scale[cut]
            lse_ref[row, h] = jnp.broadcast_to(lse[cut], (16, HD))
        return carry

    lax.fori_loop(0, ROWS, one, 0)


def suffix(page_table, suffix_len, queries, suffix_pool):
    q = queries.reshape(ROWS, KVH, GROUP, HD)
    q = jnp.pad(q, ((0, 0), (0, 0), (0, 16 - GROUP), (0, 0)))
    smem = pl.BlockSpec(memory_space=pltpu.SMEM)
    vmem = pl.BlockSpec(memory_space=pltpu.VMEM)
    shape = jax.ShapeDtypeStruct((ROWS, KVH, 16, HD), F32)
    out, lse = pl.pallas_call(
        suffix_kernel,
        out_shape=[shape, shape],
        in_specs=[smem, smem, vmem, pl.BlockSpec(memory_space=pl.ANY)],
        out_specs=[vmem, vmem],
        scratch_shapes=[
            pltpu.VMEM((ROWS, SPAN, 2 * KVW), BF16),
            pltpu.SemaphoreType.DMA((ROWS,)),
        ],
        compiler_params=pltpu.CompilerParams(vmem_limit_bytes=56 * MB),
        cost_estimate=pl.CostEstimate(
            flops=10**9, bytes_accessed=9 * MB, transcendentals=0
        ),
        name="suffix",
    )(page_table, suffix_len, q, suffix_pool)
    return (
        out[:, :, :GROUP].reshape(ROWS, KVH * WIDE),
        lse[:, :, :GROUP].reshape(ROWS, KVH * WIDE),
    )


def line_turn(line):
    return line // CAP % 2


def line_half(line):
    return line // SLOTS % HALVES


def gather_kernel(x_ref, q_ref, place_ref):
    pick = (iota((8, HD), 1) == 0).astype(BF16)
    held = dot_t(pick, x_ref[:, :HD]) < EMPTY / 2
    own = iota((8, ARR), 1) % LINES // CAP == iota((8, ARR), 0)
    mine = (held & own).astype(F32)
    upto = (iota((HALF, HALF), 0) <= iota((HALF, HALF), 1)).astype(BF16)
    seen = jnp.zeros((8, 1), F32)
    counts = []
    for start in range(0, ARR, HALF):
        block = mine[:, start : start + HALF]
        counts.append(dot(block.astype(BF16), upto) + seen)
        seen = seen + jnp.sum(block, axis=1, keepdims=True)
    counts = jnp.where(own, jnp.concatenate(counts, axis=1), 0.0)
    place = jnp.sum(counts, axis=0, keepdims=True).astype(jnp.int32) - 1
    place = jnp.where(held, place, -1)
    place_ref[...] = place
    line = iota((1, ARR), 1)
    for turn in range(2):
        for half in range(HALVES):
            mine = (line_turn(line) == turn) & (line_half(line) == half)
            row = jnp.where(mine, place[0:1], -1)
            gather = (row == iota((HALF, ARR), 0)).astype(BF16)
            for p in range(PAIRS):
                two = dot(gather, x_ref[:, p * 2 * HD : (p + 1) * 2 * HD]).astype(BF16)
                q_ref[turn, half * PER_HALF + 2 * p] = two[:, :HD]
                q_ref[turn, half * PER_HALF + 2 * p + 1] = two[:, HD:]


def gather_rows(arrived):
    return pl.pallas_call(
        gather_kernel,
        out_shape=[
            jax.ShapeDtypeStruct((2, GROUP, HALF, HD), BF16),
            jax.ShapeDtypeStruct((8, ARR), jnp.int32),
        ],
        compiler_params=pltpu.CompilerParams(vmem_limit_bytes=16 * MB),
        name="gather_rows",
    )(arrived)


def row_counts(place_ref):
    line = iota((1, ARR), 1)
    return [
        jnp.max(jnp.where(line_turn(line) == turn, place_ref[0:1], -1)) + 1
        for turn in range(2)
    ]


def widen(pair, column):
    lane = iota((TILE, HD), 1)
    wide = jnp.zeros((TILE, HD), F32)
    for i in range(2):
        mine = (lane % GROUP == 2 * pair + i) & (lane < 3 * GROUP)
        wide = wide + jnp.where(mine, column[i * TILE : (i + 1) * TILE], 0.0)
    return wide


def pair_rows(q_ref, turn, pair, at):
    return q_ref[turn, pl.ds(2 * pair, 2), pl.ds(at, TILE), :].reshape(2 * TILE, HD)


def plain_part(q, keys, values):
    weights = jnp.exp2(dot_t(q, keys) * FACTOR)
    cuts = [weights[:, c : c + HD] for c in range(0, weights.shape[1], HD)]
    total = jnp.sum(functools.reduce(jnp.add, cuts), axis=1, keepdims=True)
    return dot(weights.astype(BF16), values), total


def load_blocks(kv_refs, ks, vs, sems):
    copies = [[], []]
    for turn in range(2):
        for n in range(turn, len(kv_refs), 2):
            ref, rows = kv_refs[n], pl.ds(n // 2 * BLOCK, BLOCK)
            for part, to in enumerate((ks, vs)):
                copies[turn].append(
                    pltpu.make_async_copy(ref.at[part], to.at[turn, rows], sems.at[n, part])
                )
        for copy in copies[turn]:
            copy.start()
    return copies


def over_tiles(place_ref, copies, step):
    first, second = [(count + TILE - 1) // TILE for count in row_counts(place_ref)]

    def arrive(turn):
        for copy in copies[turn]:
            copy.wait()

    arrive(0)
    pl.when(second == 0)(lambda: arrive(1))

    def tile(t, carry):
        pl.when((t == first) & (second > 0))(lambda: arrive(1))
        turn = (t >= first).astype(jnp.int32)
        step(turn, pl.multiple_of((t - turn * first) * TILE, TILE))
        return carry

    lax.fori_loop(0, first + second, tile, 0)


def sums_kernel(blocks, first, q_ref, place_ref, *refs):
    kv_refs, refs = refs[: 2 * blocks], refs[2 * blocks :]
    out_ref, total_ref, ks, vs, sems = refs[-5:]
    copies = load_blocks(kv_refs, ks, vs, sems)

    def step(turn, at):
        def one(pair, wide):
            q = pair_rows(q_ref, turn, pair, at)
            out, total = plain_part(q, ks[turn], vs[turn])
            out = out.reshape(2, TILE, HD)
            place = (turn, pl.ds(2 * pair, 2), pl.ds(at, TILE))
            if not first:
                out = out + refs[0][place]
            out_ref[place] = out
            return wide + widen(pair, total)

        if first:
            wide = jnp.zeros((TILE, HD), F32)
        else:
            wide = refs[1][turn, pl.ds(at, TILE), :]
        total_ref[turn, pl.ds(at, TILE), :] = lax.fori_loop(
            0, GROUP // 2, one, wide, unroll=UNROLL
        )

    over_tiles(place_ref, copies, step)


def block_scratch(blocks):
    return [
        pltpu.VMEM((2, blocks * BLOCK, HD), BF16),
        pltpu.VMEM((2, blocks * BLOCK, HD), BF16),
        pltpu.SemaphoreType.DMA((2 * blocks, 2)),
    ]


def add_sums(rows, place, kv, state):
    blocks = len(kv) // 2
    vmem = pl.BlockSpec(memory_space=pltpu.VMEM)
    return pl.pallas_call(
        functools.partial(sums_kernel, blocks, not state),
        out_shape=[
            jax.ShapeDtypeStruct((2, GROUP, HALF, HD), F32),
            jax.ShapeDtypeStruct((2, HALF, HD), F32),
        ],
        in_specs=[vmem] * 2 + [pl.BlockSpec(memory_space=pl.ANY)] * len(kv) + [vmem] * len(state),
        out_specs=[vmem, vmem],
        scratch_shapes=block_scratch(blocks),
        compiler_params=pltpu.CompilerParams(vmem_limit_bytes=24 * MB),
        cost_estimate=pl.CostEstimate(
            flops=blocks * 4 * 10**9, bytes_accessed=8 * MB, transcendentals=0
        ),
        name="sums_%d" % blocks,
    )(rows, place, *kv, *state)


def last_kernel(q_ref, place_ref, sum_ref, total_ref, *refs):
    kv_refs, all_refs, (out_ref, os, ls, ks, vs, sems, held, held_sem) = (
        refs[:2],
        refs[2:10],
        refs[10:],
    )
    copies = load_blocks(kv_refs, ks, vs, sems)
    os[...] = jnp.zeros((2, GROUP // 2, HALF, 2 * HD), BF16)
    ls[...] = jnp.zeros((2, HALF, HD), BF16)
    lane = iota((TILE, HD), 1)

    def keep(turn, pair, at, out, totals):
        for i in range(2):
            os[turn, pair, pl.ds(at, TILE), i * HD : (i + 1) * HD] = (
                out[i * TILE : (i + 1) * TILE] / totals[i]
            ).astype(BF16)

    def keep_lse(turn, at, total, shift):
        lse = jnp.where(lane < 3 * GROUP, shift + jnp.log(total), 0.0)
        one = lse.astype(BF16).astype(F32)
        two = (lse - one).astype(BF16).astype(F32)
        three = lse - one - two
        split = jnp.where(lane < GROUP, one, jnp.where(lane < 2 * GROUP, two, three))
        ls[turn, pl.ds(at, TILE), :] = split.astype(BF16)

    def fetch(k, turn):
        for n, ref in enumerate(all_refs):

            @pl.when(2 * k + turn == n)
            def _(ref=ref):
                copy = pltpu.make_async_copy(ref, held, held_sem.at[0])
                copy.start()
                copy.wait()

    def step(turn, at):
        before = total_ref[turn, pl.ds(at, TILE), :]

        def one(pair, wide):
            q = pair_rows(q_ref, turn, pair, at)
            out, total = plain_part(q, ks[turn], vs[turn])
            out = out + sum_ref[turn, pl.ds(2 * pair, 2), pl.ds(at, TILE), :].reshape(
                2 * TILE, HD
            )
            totals = [
                total[i * TILE : (i + 1) * TILE]
                + jnp.sum(
                    jnp.where(lane == 2 * pair + i, before, 0.0), axis=1, keepdims=True
                )
                for i in range(2)
            ]
            keep(turn, pair, at, out, totals)
            return wide + widen(pair, total)

        total = lax.fori_loop(0, GROUP // 2, one, before, unroll=UNROLL)
        keep_lse(turn, at, total, 0.0)
        known = jnp.where(lane < 3 * GROUP, total, 1.0)
        plain = (jnp.min(known) > LEAST) & (jnp.max(known) < MOST)

        @pl.when(jnp.logical_not(plain))
        def _():
            def again(pair, carry):
                q = pair_rows(q_ref, turn, pair, at)

                def block(k, state):
                    top, amount, acc = state
                    fetch(k, turn)
                    score = dot_t(q, held[0])
                    high = jnp.maximum(top, jnp.max(score, axis=1, keepdims=True))
                    weights = jnp.exp2(score * FACTOR - high * FACTOR)
                    fade = jnp.exp2((top - high) * FACTOR)
                    amount = amount * fade + jnp.sum(weights, axis=1, keepdims=True)
                    return high, amount, acc * fade + dot(weights.astype(BF16), held[1])

                top, amount, acc = lax.fori_loop(
                    0,
                    4,
                    block,
                    (
                        jnp.full((2 * TILE, 1), -1e30, F32),
                        jnp.zeros((2 * TILE, 1), F32),
                        jnp.zeros((2 * TILE, HD), F32),
                    ),
                )
                keep(turn, pair, at, acc, [amount[:TILE], amount[TILE:]])
                return carry[0] + widen(pair, amount), carry[1] + widen(pair, top * SCALE)

            empty = jnp.zeros((TILE, HD), F32)
            amount, shift = lax.fori_loop(0, GROUP // 2, again, (empty, empty))
            keep_lse(turn, at, amount, shift)

    over_tiles(place_ref, copies, step)

    place_col = jnp.transpose(place_ref[...].astype(F32))[:, 0:1].astype(jnp.int32)
    line = iota((ARR, 1), 0)
    scatter = jnp.concatenate(
        [
            (
                jnp.where((line_turn(line) == turn) & (line_half(line) == half), place_col, -1)
                == iota((ARR, HALF), 1)
            ).astype(BF16)
            for turn in range(2)
            for half in range(HALVES)
        ],
        axis=1,
    )
    for p in range(PAIRS):
        source = jnp.concatenate(
            [os[turn, half * PAIRS + p] for turn in range(2) for half in range(HALVES)], axis=0
        )
        out_ref[:, p * 2 * HD : (p + 1) * 2 * HD] = dot(scatter, source).astype(BF16)
    source = jnp.concatenate([ls[0], ls[0], ls[1], ls[1]], axis=0)
    out_ref[:, PART:] = dot(scatter, source).astype(BF16)


def finish_prefix(rows, place, state, last, everything):
    vmem = pl.BlockSpec(memory_space=pltpu.VMEM)
    return pl.pallas_call(
        last_kernel,
        out_shape=jax.ShapeDtypeStruct((ARR, PART + HD), BF16),
        in_specs=[vmem] * 4 + [pl.BlockSpec(memory_space=pl.ANY)] * 10,
        scratch_shapes=[
            pltpu.VMEM((2, GROUP // 2, HALF, 2 * HD), BF16),
            pltpu.VMEM((2, HALF, HD), BF16),
            *block_scratch(1),
            pltpu.VMEM((2, BLOCK, HD), BF16),
            pltpu.SemaphoreType.DMA((1,)),
        ],
        compiler_params=pltpu.CompilerParams(vmem_limit_bytes=32 * MB),
        cost_estimate=pl.CostEstimate(
            flops=6 * 10**9, bytes_accessed=8 * MB, transcendentals=0
        ),
        name="finish_prefix",
    )(rows, place, *state, *last, *everything)


def merge_kernel(at_ref, back_ref, so_ref, sl_ref, out_ref):
    picked = KVH * 4 * ROWS
    line = iota((picked, ARR), 1)
    first = dot((at_ref[...] == line).astype(BF16), back_ref[...])
    second = dot((at_ref[...] + SLOTS == line).astype(BF16), back_ref[:, :PART])
    spread = (
        (iota((HD, WIDE), 0) % GROUP == iota((HD, WIDE), 1) // HD)
        & (iota((HD, WIDE), 0) < 3 * GROUP)
    ).astype(BF16)
    lse = dot(first[:, PART:].astype(BF16), spread)
    for h in range(KVH):
        cut = slice(h * WIDE, (h + 1) * WIDE)
        rows = [slice((h * 4 + j) * ROWS, (h * 4 + j + 1) * ROWS) for j in range(4)]
        parts = [
            (lse[r], jnp.concatenate([first[r, :PART], second[r]], axis=1)) for r in rows
        ]
        parts.append((sl_ref[:, cut], so_ref[:, cut]))
        top = functools.reduce(jnp.maximum, [p[0] for p in parts])
        weights = [jnp.exp(p[0] - top) for p in parts]
        total = functools.reduce(jnp.add, weights)
        acc = functools.reduce(jnp.add, [w * p[1] for w, p in zip(weights, parts)])
        out_ref[:, cut] = (acc / total).astype(BF16)


def merge(prompt_ids, back, so, sl):
    prompt = prompt_ids[:, 0]
    earlier = jnp.arange(ROWS)[None, :] < jnp.arange(ROWS)[:, None]
    rank = jnp.sum(((prompt[:, None] == prompt[None, :]) & earlier).astype(jnp.int32), axis=1)
    h = jnp.arange(KVH)[:, None, None]
    j = jnp.arange(4)[None, :, None]
    c = h // 4
    z = jnp.where(c == 0, h, j)
    y = jnp.where(c == 0, j, h - 4)
    place = (prompt % 2 != c).astype(jnp.int32) * CAP + rank
    at = device_number(prompt // 2, c, z, y) * LINES + place
    return pl.pallas_call(
        merge_kernel,
        out_shape=jax.ShapeDtypeStruct((ROWS, KVH * WIDE), BF16),
        compiler_params=pltpu.CompilerParams(vmem_limit_bytes=16 * MB),
        name="merge",
    )(at.reshape(-1, 1), back, so, sl)


def exchange(array):
    width = array.shape[1]
    moved = lax.all_to_all(
        array.reshape(DEVS, LINES, width), AXES, split_axis=0, concat_axis=0, tiled=True
    )
    return moved.reshape(ARR, width)


def body(queries, prompt_ids, suffix_len, page_table, suffix_pool, prefix_kv):
    c = lax.axis_index("pre") % NC
    z = lax.axis_index("row") // NY
    y = lax.axis_index("row") % NY
    heads = jnp.stack(
        [
            jnp.where(c ^ cross == 0, (z + k) % NZ, NZ + (y + k) % NY)
            for k in range(4)
            for cross in range(2)
        ]
    ).astype(jnp.int32)
    sends = fill_sends(prompt_ids, queries)
    sends, heads = lax.optimization_barrier((sends, heads))
    arrived = exchange(sends)
    pieces = split_heads(heads, prefix_kv)

    def move(n, piece):
        return lax.ppermute(piece, AXES, routes(n // 2, n % 2))

    kv = list(pieces)
    for n in (1, 2, 3, 6, 7):
        kv[n] = move(n, pieces[n])
    arrived, kv[1] = lax.optimization_barrier((arrived, kv[1]))
    rows, place = gather_rows(arrived)
    place, later = lax.optimization_barrier((place, pieces[4]))
    kv[4] = move(4, later)
    state = add_sums(rows, place, kv[0:2], ())
    state, kv[2], kv[3], kv[6], kv[7], later = lax.optimization_barrier(
        (state, kv[2], kv[3], kv[6], kv[7], pieces[5])
    )
    kv[5] = move(5, later)
    state = add_sums(rows, place, kv[2:4] + kv[6:8], state)
    parts = finish_prefix(rows, place, state, kv[4:6], kv)
    parts, queries = lax.optimization_barrier((parts, queries))
    so, sl = suffix(page_table, suffix_len, queries, suffix_pool)
    return merge(prompt_ids, exchange(parts), so, sl)


def solution(mesh):
    return jax.shard_map(
        body,
        mesh=mesh,
        in_specs=(
            P(("pre", "row"), None),
            P(("pre", "row"), None),
            P(("pre", "row")),
            P(("pre", "row"), None),
            P(("pre", "row"), None, None),
            P("pre", "row", None),
        ),
        out_specs=P(("pre", "row"), None),
        check_vma=False,
    )
```

```python
import functools
import math

import jax
import jax.numpy as jnp
from jax import lax
from jax.experimental import pallas as pl
from jax.experimental.pallas import tpu as pltpu
from jax.sharding import PartitionSpec as P

KVH = 8
HD = 128
CAP = 2
GROUP = 12
ROWS = 8
WIDE = GROUP * HD
KVW = KVH * HD
NX, NC, NZ, NY = 4, 2, 4, 4
DEVS = NX * NC * NZ * NY
BLOCK = 1024
PAGE = 16
MAXP = 16
SPAN = PAGE * MAXP
SLOTS = 2 * CAP
HALVES = 2
PER_HALF = GROUP // HALVES
PAIRS = PER_HALF // 2
PART = PER_HALF * HD
LINES = HALVES * SLOTS
ARR = DEVS * LINES
HALF = DEVS * CAP
TILE = 128
UNROLL = 3
EMPTY = 256.0
SCALE = 1.0 / math.sqrt(HD)
FACTOR = SCALE / math.log(2.0)
LEAST = 1e-26
MOST = 1e30
AXES = ("pre", "row")
MB = 1 << 20
F32 = jnp.float32
BF16 = jnp.bfloat16


def dot(a, b):
    return jnp.dot(a, b, preferred_element_type=F32)


def dot_t(a, b):
    return lax.dot_general(a, b, (((1,), (1,)), ((), ())), preferred_element_type=F32)


def iota(shape, dim):
    return lax.broadcasted_iota(jnp.int32, shape, dim)


def device_number(x, c, z, y):
    return ((x * NC + c) * NZ + z) * NY + y


def routes(k, cross):
    pairs = []
    for x in range(NX):
        for c in range(NC):
            for z in range(NZ):
                for y in range(NY):
                    if (c ^ cross) == 0:
                        to = device_number(x, 0, (z + k) % NZ, y)
                    else:
                        to = device_number(x, 1, z, (y + k) % NY)
                    pairs.append((device_number(x, c, z, y), to))
    return pairs


def split_heads_kernel(head_ref, kv_ref, *refs):
    outs, (held, sems) = refs[:-2], refs[-2:]
    inward, outward = [], []
    for i, out in enumerate(outs):
        for part in range(2):
            start = pl.multiple_of(part * KVW + head_ref[i] * HD, HD)
            inward.append(
                pltpu.make_async_copy(
                    kv_ref.at[0, :, pl.ds(start, HD)], held.at[i, part], sems.at[0, i, part]
                )
            )
            outward.append(
                pltpu.make_async_copy(held.at[i, part], out.at[part], sems.at[1, i, part])
            )
    for copy in inward:
        copy.start()
    for copy, onward in zip(inward, outward):
        copy.wait()
        onward.start()
    for copy in outward:
        copy.wait()


def split_heads(heads, prefix_kv):
    n = heads.shape[0]
    return pl.pallas_call(
        split_heads_kernel,
        out_shape=[jax.ShapeDtypeStruct((2, BLOCK, HD), BF16)] * n,
        in_specs=[pl.BlockSpec(memory_space=pltpu.SMEM), pl.BlockSpec(memory_space=pltpu.HBM)],
        out_specs=[pl.BlockSpec(memory_space=pltpu.HBM)] * n,
        scratch_shapes=[
            pltpu.VMEM((n, 2, BLOCK, HD), BF16),
            pltpu.SemaphoreType.DMA((2, n, 2)),
        ],
        compiler_params=pltpu.CompilerParams(vmem_limit_bytes=60 * MB),
        name="split_heads",
    )(heads, prefix_kv)


def send_kernel(prompt_ref, q_ref, out_ref):
    wide = HALVES * NY * ROWS
    lane = iota((1, wide), 1) % ROWS
    slot = jnp.zeros((1, wide), jnp.int32)
    for i in range(ROWS):
        rank = sum((prompt_ref[j] == prompt_ref[i]).astype(jnp.int32) for j in range(i))
        slot = jnp.where(lane == i, prompt_ref[i] * CAP + rank, slot)
    unit = NY * LINES
    rows = NX * unit
    r = iota((rows, wide), 0)
    lane = iota((rows, wide), 1)
    base = r // unit * SLOTS
    half_fits = r // SLOTS % HALVES == lane // ROWS % HALVES
    first = (base + r % SLOTS == slot) & half_fits & (lane < HALVES * ROWS)
    second = (
        (base + (r + CAP) % SLOTS == slot)
        & half_fits
        & (r // LINES % NY == lane // (HALVES * ROWS))
    )
    first = first.astype(F32)
    second = second.astype(F32)
    empty_first = (1.0 - jnp.sum(first, axis=1, keepdims=True)) * EMPTY
    empty_second = (1.0 - jnp.sum(second, axis=1, keepdims=True)) * EMPTY
    first = first[:, : HALVES * ROWS].astype(BF16)
    second = second.astype(BF16)

    def stacked(heads):
        return jnp.concatenate(
            [
                q_ref[:, h * WIDE + half * PART : h * WIDE + (half + 1) * PART].astype(F32)
                for h in heads
                for half in range(HALVES)
            ],
            axis=0,
        ).astype(BF16)

    for z in range(NZ):
        piece = (dot(first, stacked([z])) + empty_first).astype(BF16)
        for x in range(NX):
            at = device_number(x, 0, z, 0) * LINES
            out_ref[at : at + unit, :] = piece[x * unit : (x + 1) * unit]
    piece = dot(second, stacked([NZ + y for y in range(NY)])) + empty_second
    piece = piece.astype(BF16)
    for x in range(NX):
        for z in range(NZ):
            at = device_number(x, 1, z, 0) * LINES
            out_ref[at : at + unit, :] = piece[x * unit : (x + 1) * unit]


def fill_sends(prompt_ids, queries):
    return pl.pallas_call(
        send_kernel,
        out_shape=jax.ShapeDtypeStruct((ARR, PART), BF16),
        in_specs=[
            pl.BlockSpec(memory_space=pltpu.SMEM),
            pl.BlockSpec(memory_space=pltpu.VMEM),
        ],
        compiler_params=pltpu.CompilerParams(vmem_limit_bytes=60 * MB),
        name="fill_sends",
    )(prompt_ids[:, 0], queries)


def suffix_kernel(table_ref, len_ref, q_ref, pool_ref, out_ref, lse_ref, kv, sems):
    for row in range(ROWS):
        for p in range(MAXP):
            pltpu.make_async_copy(
                pool_ref.at[table_ref[row, p]],
                kv.at[row, pl.ds(p * PAGE, PAGE), :],
                sems.at[row],
            ).start()

    def one(row, carry):
        pltpu.make_async_copy(kv.at[row], kv.at[row], sems.at[row]).wait()
        scores = jnp.concatenate(
            [
                dot_t(q_ref[row, h], kv[row, :, h * HD : (h + 1) * HD])
                for h in range(KVH)
            ],
            axis=0,
        )
        in_range = iota((KVH * 16, SPAN), 1) < len_ref[row]
        scores = jnp.where(in_range, scores * SCALE, -1e30)
        top = jnp.max(scores, axis=1, keepdims=True)
        weights = jnp.where(in_range, jnp.exp(scores - top), 0.0)
        total = jnp.sum(weights, axis=1, keepdims=True)
        scale = 1.0 / total
        lse = top + jnp.log(total)
        weights = weights.astype(BF16)
        for h in range(KVH):
            cut = slice(h * 16, (h + 1) * 16)
            values = kv[row, :, KVW + h * HD : KVW + (h + 1) * HD]
            out_ref[row, h] = dot(weights[cut], values) * scale[cut]
            lse_ref[row, h] = jnp.broadcast_to(lse[cut], (16, HD))
        return carry

    lax.fori_loop(0, ROWS, one, 0)


def suffix(page_table, suffix_len, queries, suffix_pool):
    q = queries.reshape(ROWS, KVH, GROUP, HD)
    q = jnp.pad(q, ((0, 0), (0, 0), (0, 16 - GROUP), (0, 0)))
    smem = pl.BlockSpec(memory_space=pltpu.SMEM)
    vmem = pl.BlockSpec(memory_space=pltpu.VMEM)
    shape = jax.ShapeDtypeStruct((ROWS, KVH, 16, HD), F32)
    out, lse = pl.pallas_call(
        suffix_kernel,
        out_shape=[shape, shape],
        in_specs=[smem, smem, vmem, pl.BlockSpec(memory_space=pl.ANY)],
        out_specs=[vmem, vmem],
        scratch_shapes=[
            pltpu.VMEM((ROWS, SPAN, 2 * KVW), BF16),
            pltpu.SemaphoreType.DMA((ROWS,)),
        ],
        compiler_params=pltpu.CompilerParams(vmem_limit_bytes=56 * MB),
        cost_estimate=pl.CostEstimate(
            flops=10**9, bytes_accessed=9 * MB, transcendentals=0
        ),
        name="suffix",
    )(page_table, suffix_len, q, suffix_pool)
    return (
        out[:, :, :GROUP].reshape(ROWS, KVH * WIDE),
        lse[:, :, :GROUP].reshape(ROWS, KVH * WIDE),
    )


def line_turn(line):
    return line // CAP % 2


def line_half(line):
    return line // SLOTS % HALVES


def gather_kernel(x_ref, q_ref, place_ref):
    pick = (iota((8, HD), 1) == 0).astype(BF16)
    held = dot_t(pick, x_ref[:, :HD]) < EMPTY / 2
    own = iota((8, ARR), 1) % LINES // CAP == iota((8, ARR), 0)
    mine = (held & own).astype(F32)
    upto = (iota((HALF, HALF), 0) <= iota((HALF, HALF), 1)).astype(BF16)
    seen = jnp.zeros((8, 1), F32)
    counts = []
    for start in range(0, ARR, HALF):
        block = mine[:, start : start + HALF]
        counts.append(dot(block.astype(BF16), upto) + seen)
        seen = seen + jnp.sum(block, axis=1, keepdims=True)
    counts = jnp.where(own, jnp.concatenate(counts, axis=1), 0.0)
    place = jnp.sum(counts, axis=0, keepdims=True).astype(jnp.int32) - 1
    place = jnp.where(held, place, -1)
    place_ref[...] = place
    line = iota((1, ARR), 1)
    for turn in range(2):
        for half in range(HALVES):
            mine = (line_turn(line) == turn) & (line_half(line) == half)
            row = jnp.where(mine, place[0:1], -1)
            gather = (row == iota((HALF, ARR), 0)).astype(BF16)
            for p in range(PAIRS):
                two = dot(gather, x_ref[:, p * 2 * HD : (p + 1) * 2 * HD]).astype(BF16)
                q_ref[turn, half * PER_HALF + 2 * p] = two[:, :HD]
                q_ref[turn, half * PER_HALF + 2 * p + 1] = two[:, HD:]


def gather_rows(arrived):
    return pl.pallas_call(
        gather_kernel,
        out_shape=[
            jax.ShapeDtypeStruct((2, GROUP, HALF, HD), BF16),
            jax.ShapeDtypeStruct((8, ARR), jnp.int32),
        ],
        compiler_params=pltpu.CompilerParams(vmem_limit_bytes=16 * MB),
        name="gather_rows",
    )(arrived)


def row_counts(place_ref):
    line = iota((1, ARR), 1)
    return [
        jnp.max(jnp.where(line_turn(line) == turn, place_ref[0:1], -1)) + 1
        for turn in range(2)
    ]


def widen(pair, column):
    lane = iota((TILE, HD), 1)
    wide = jnp.zeros((TILE, HD), F32)
    for i in range(2):
        mine = (lane % GROUP == 2 * pair + i) & (lane < 3 * GROUP)
        wide = wide + jnp.where(mine, column[i * TILE : (i + 1) * TILE], 0.0)
    return wide


def pair_rows(q_ref, turn, pair, at):
    return q_ref[turn, pl.ds(2 * pair, 2), pl.ds(at, TILE), :].reshape(2 * TILE, HD)


def plain_part(q, keys, values):
    weights = jnp.exp2(dot_t(q, keys) * FACTOR)
    cuts = [weights[:, c : c + HD] for c in range(0, weights.shape[1], HD)]
    total = jnp.sum(functools.reduce(jnp.add, cuts), axis=1, keepdims=True)
    return dot(weights.astype(BF16), values), total


def load_blocks(kv_refs, ks, vs, sems):
    copies = [[], []]
    for turn in range(2):
        for n in range(turn, len(kv_refs), 2):
            ref, rows = kv_refs[n], pl.ds(n // 2 * BLOCK, BLOCK)
            for part, to in enumerate((ks, vs)):
                copies[turn].append(
                    pltpu.make_async_copy(ref.at[part], to.at[turn, rows], sems.at[n, part])
                )
        for copy in copies[turn]:
            copy.start()
    return copies


def over_tiles(place_ref, copies, step):
    first, second = [(count + TILE - 1) // TILE for count in row_counts(place_ref)]

    def arrive(turn):
        for copy in copies[turn]:
            copy.wait()

    arrive(0)
    pl.when(second == 0)(lambda: arrive(1))

    def tile(t, carry):
        pl.when((t == first) & (second > 0))(lambda: arrive(1))
        turn = (t >= first).astype(jnp.int32)
        step(turn, pl.multiple_of((t - turn * first) * TILE, TILE))
        return carry

    lax.fori_loop(0, first + second, tile, 0)


def sums_kernel(blocks, first, q_ref, place_ref, *refs):
    kv_refs, refs = refs[: 2 * blocks], refs[2 * blocks :]
    out_ref, total_ref, ks, vs, sems = refs[-5:]
    copies = load_blocks(kv_refs, ks, vs, sems)

    def step(turn, at):
        def one(pair, wide):
            q = pair_rows(q_ref, turn, pair, at)
            out, total = plain_part(q, ks[turn], vs[turn])
            out = out.reshape(2, TILE, HD)
            place = (turn, pl.ds(2 * pair, 2), pl.ds(at, TILE))
            if not first:
                out = out + refs[0][place]
            out_ref[place] = out
            return wide + widen(pair, total)

        if first:
            wide = jnp.zeros((TILE, HD), F32)
        else:
            wide = refs[1][turn, pl.ds(at, TILE), :]
        total_ref[turn, pl.ds(at, TILE), :] = lax.fori_loop(
            0, GROUP // 2, one, wide, unroll=UNROLL
        )

    over_tiles(place_ref, copies, step)


def block_scratch(blocks):
    return [
        pltpu.VMEM((2, blocks * BLOCK, HD), BF16),
        pltpu.VMEM((2, blocks * BLOCK, HD), BF16),
        pltpu.SemaphoreType.DMA((2 * blocks, 2)),
    ]


def add_sums(rows, place, kv, state):
    blocks = len(kv) // 2
    vmem = pl.BlockSpec(memory_space=pltpu.VMEM)
    return pl.pallas_call(
        functools.partial(sums_kernel, blocks, not state),
        out_shape=[
            jax.ShapeDtypeStruct((2, GROUP, HALF, HD), F32),
            jax.ShapeDtypeStruct((2, HALF, HD), F32),
        ],
        in_specs=[vmem] * 2 + [pl.BlockSpec(memory_space=pl.ANY)] * len(kv) + [vmem] * len(state),
        out_specs=[vmem, vmem],
        scratch_shapes=block_scratch(blocks),
        compiler_params=pltpu.CompilerParams(vmem_limit_bytes=24 * MB),
        cost_estimate=pl.CostEstimate(
            flops=blocks * 4 * 10**9, bytes_accessed=8 * MB, transcendentals=0
        ),
        name="sums_%d" % blocks,
    )(rows, place, *kv, *state)


def last_kernel(q_ref, place_ref, sum_ref, total_ref, *refs):
    kv_refs, all_refs, (out_ref, os, ls, ks, vs, sems, held, held_sem) = (
        refs[:2],
        refs[2:10],
        refs[10:],
    )
    copies = load_blocks(kv_refs, ks, vs, sems)
    os[...] = jnp.zeros((2, GROUP // 2, HALF, 2 * HD), BF16)
    ls[...] = jnp.zeros((2, HALF, HD), BF16)
    lane = iota((TILE, HD), 1)

    def keep(turn, pair, at, out, totals):
        for i in range(2):
            os[turn, pair, pl.ds(at, TILE), i * HD : (i + 1) * HD] = (
                out[i * TILE : (i + 1) * TILE] / totals[i]
            ).astype(BF16)

    def keep_lse(turn, at, total, shift):
        lse = jnp.where(lane < 3 * GROUP, shift + jnp.log(total), 0.0)
        one = lse.astype(BF16).astype(F32)
        two = (lse - one).astype(BF16).astype(F32)
        three = lse - one - two
        split = jnp.where(lane < GROUP, one, jnp.where(lane < 2 * GROUP, two, three))
        ls[turn, pl.ds(at, TILE), :] = split.astype(BF16)

    def fetch(k, turn):
        for n, ref in enumerate(all_refs):

            @pl.when(2 * k + turn == n)
            def _(ref=ref):
                copy = pltpu.make_async_copy(ref, held, held_sem.at[0])
                copy.start()
                copy.wait()

    def step(turn, at):
        before = total_ref[turn, pl.ds(at, TILE), :]

        def one(pair, wide):
            q = pair_rows(q_ref, turn, pair, at)
            out, total = plain_part(q, ks[turn], vs[turn])
            out = out + sum_ref[turn, pl.ds(2 * pair, 2), pl.ds(at, TILE), :].reshape(
                2 * TILE, HD
            )
            totals = [
                total[i * TILE : (i + 1) * TILE]
                + jnp.sum(
                    jnp.where(lane == 2 * pair + i, before, 0.0), axis=1, keepdims=True
                )
                for i in range(2)
            ]
            keep(turn, pair, at, out, totals)
            return wide + widen(pair, total)

        total = lax.fori_loop(0, GROUP // 2, one, before, unroll=UNROLL)
        keep_lse(turn, at, total, 0.0)
        known = jnp.where(lane < 3 * GROUP, total, 1.0)
        plain = (jnp.min(known) > LEAST) & (jnp.max(known) < MOST)

        @pl.when(jnp.logical_not(plain))
        def _():
            def again(pair, carry):
                q = pair_rows(q_ref, turn, pair, at)

                def block(k, state):
                    top, amount, acc = state
                    fetch(k, turn)
                    score = dot_t(q, held[0])
                    high = jnp.maximum(top, jnp.max(score, axis=1, keepdims=True))
                    weights = jnp.exp2(score * FACTOR - high * FACTOR)
                    fade = jnp.exp2((top - high) * FACTOR)
                    amount = amount * fade + jnp.sum(weights, axis=1, keepdims=True)
                    return high, amount, acc * fade + dot(weights.astype(BF16), held[1])

                top, amount, acc = lax.fori_loop(
                    0,
                    4,
                    block,
                    (
                        jnp.full((2 * TILE, 1), -1e30, F32),
                        jnp.zeros((2 * TILE, 1), F32),
                        jnp.zeros((2 * TILE, HD), F32),
                    ),
                )
                keep(turn, pair, at, acc, [amount[:TILE], amount[TILE:]])
                return carry[0] + widen(pair, amount), carry[1] + widen(pair, top * SCALE)

            empty = jnp.zeros((TILE, HD), F32)
            amount, shift = lax.fori_loop(0, GROUP // 2, again, (empty, empty))
            keep_lse(turn, at, amount, shift)

    over_tiles(place_ref, copies, step)

    place_col = jnp.transpose(place_ref[...].astype(F32))[:, 0:1].astype(jnp.int32)
    line = iota((ARR, 1), 0)
    scatter = jnp.concatenate(
        [
            (
                jnp.where((line_turn(line) == turn) & (line_half(line) == half), place_col, -1)
                == iota((ARR, HALF), 1)
            ).astype(BF16)
            for turn in range(2)
            for half in range(HALVES)
        ],
        axis=1,
    )
    for p in range(PAIRS):
        source = jnp.concatenate(
            [os[turn, half * PAIRS + p] for turn in range(2) for half in range(HALVES)], axis=0
        )
        out_ref[:, p * 2 * HD : (p + 1) * 2 * HD] = dot(scatter, source).astype(BF16)
    source = jnp.concatenate([ls[0], ls[0], ls[1], ls[1]], axis=0)
    out_ref[:, PART:] = dot(scatter, source).astype(BF16)


def finish_prefix(rows, place, state, last, everything):
    vmem = pl.BlockSpec(memory_space=pltpu.VMEM)
    return pl.pallas_call(
        last_kernel,
        out_shape=jax.ShapeDtypeStruct((ARR, PART + HD), BF16),
        in_specs=[vmem] * 4 + [pl.BlockSpec(memory_space=pl.ANY)] * 10,
        scratch_shapes=[
            pltpu.VMEM((2, GROUP // 2, HALF, 2 * HD), BF16),
            pltpu.VMEM((2, HALF, HD), BF16),
            *block_scratch(1),
            pltpu.VMEM((2, BLOCK, HD), BF16),
            pltpu.SemaphoreType.DMA((1,)),
        ],
        compiler_params=pltpu.CompilerParams(vmem_limit_bytes=32 * MB),
        cost_estimate=pl.CostEstimate(
            flops=6 * 10**9, bytes_accessed=8 * MB, transcendentals=0
        ),
        name="finish_prefix",
    )(rows, place, *state, *last, *everything)


def merge_kernel(at_ref, back_ref, so_ref, sl_ref, out_ref):
    picked = KVH * 4 * ROWS
    line = iota((picked, ARR), 1)
    first = dot((at_ref[...] == line).astype(BF16), back_ref[...])
    second = dot((at_ref[...] + SLOTS == line).astype(BF16), back_ref[:, :PART])
    spread = (
        (iota((HD, WIDE), 0) % GROUP == iota((HD, WIDE), 1) // HD)
        & (iota((HD, WIDE), 0) < 3 * GROUP)
    ).astype(BF16)
    lse = dot(first[:, PART:].astype(BF16), spread)
    for h in range(KVH):
        cut = slice(h * WIDE, (h + 1) * WIDE)
        rows = [slice((h * 4 + j) * ROWS, (h * 4 + j + 1) * ROWS) for j in range(4)]
        parts = [
            (lse[r], jnp.concatenate([first[r, :PART], second[r]], axis=1)) for r in rows
        ]
        parts.append((sl_ref[:, cut], so_ref[:, cut]))
        top = functools.reduce(jnp.maximum, [p[0] for p in parts])
        weights = [jnp.exp(p[0] - top) for p in parts]
        total = functools.reduce(jnp.add, weights)
        acc = functools.reduce(jnp.add, [w * p[1] for w, p in zip(weights, parts)])
        out_ref[:, cut] = (acc / total).astype(BF16)


def merge(prompt_ids, back, so, sl):
    prompt = prompt_ids[:, 0]
    earlier = jnp.arange(ROWS)[None, :] < jnp.arange(ROWS)[:, None]
    rank = jnp.sum(((prompt[:, None] == prompt[None, :]) & earlier).astype(jnp.int32), axis=1)
    h = jnp.arange(KVH)[:, None, None]
    j = jnp.arange(4)[None, :, None]
    c = h // 4
    z = jnp.where(c == 0, h, j)
    y = jnp.where(c == 0, j, h - 4)
    place = (prompt % 2 != c).astype(jnp.int32) * CAP + rank
    at = device_number(prompt // 2, c, z, y) * LINES + place
    return pl.pallas_call(
        merge_kernel,
        out_shape=jax.ShapeDtypeStruct((ROWS, KVH * WIDE), BF16),
        compiler_params=pltpu.CompilerParams(vmem_limit_bytes=16 * MB),
        name="merge",
    )(at.reshape(-1, 1), back, so, sl)


def exchange(array):
    width = array.shape[1]
    moved = lax.all_to_all(
        array.reshape(DEVS, LINES, width), AXES, split_axis=0, concat_axis=0, tiled=True
    )
    return moved.reshape(ARR, width)


def body(queries, prompt_ids, suffix_len, page_table, suffix_pool, prefix_kv):
    c = lax.axis_index("pre") % NC
    z = lax.axis_index("row") // NY
    y = lax.axis_index("row") % NY
    heads = jnp.stack(
        [
            jnp.where(c ^ cross == 0, (z + k) % NZ, NZ + (y + k) % NY)
            for k in range(4)
            for cross in range(2)
        ]
    ).astype(jnp.int32)
    sends = fill_sends(prompt_ids, queries)
    sends, heads = lax.optimization_barrier((sends, heads))
    arrived = exchange(sends)
    pieces = split_heads(heads, prefix_kv)

    def move(n, piece):
        return lax.ppermute(piece, AXES, routes(n // 2, n % 2))

    kv = list(pieces)
    for n in (1, 2, 3, 6, 7):
        kv[n] = move(n, pieces[n])
    arrived, kv[1] = lax.optimization_barrier((arrived, kv[1]))
    rows, place = gather_rows(arrived)
    place, later = lax.optimization_barrier((place, pieces[4]))
    kv[4] = move(4, later)
    state = add_sums(rows, place, kv[0:2], ())
    state, kv[2], kv[3], kv[6], kv[7], later = lax.optimization_barrier(
        (state, kv[2], kv[3], kv[6], kv[7], pieces[5])
    )
    kv[5] = move(5, later)
    state = add_sums(rows, place, kv[2:4] + kv[6:8], state)
    parts = finish_prefix(rows, place, state, kv[4:6], kv)
    parts, queries = lax.optimization_barrier((parts, queries))
    so, sl = suffix(page_table, suffix_len, queries, suffix_pool)
    return merge(prompt_ids, exchange(parts), so, sl)


def solution(mesh):
    return jax.shard_map(
        body,
        mesh=mesh,
        in_specs=(
            P(("pre", "row"), None),
            P(("pre", "row"), None),
            P(("pre", "row")),
            P(("pre", "row"), None),
            P(("pre", "row"), None, None),
            P("pre", "row", None),
        ),
        out_specs=P(("pre", "row"), None),
        check_vma=False,
    )
```
